32 devices in a mesh: pb: 8 (over y, x, core), ha: 4 (over z).
Axes of the slice: x: 2, y: 2, z: 4, core: 2. Of those that a mesh axis runs over, the one named last changes fastest.
Arguments:
- main_query: bfloat16 [1024, 128, 576], P('pb', 'ha'), may hold values from -1.8 to 1.8
- latent: bfloat16 [1024, 576], P('pb'), may hold values from -6 to 6
- log_sums: float32 [1024, 128], P('pb', 'ha'), may hold values from 0 to 4
- window_start: int32 [1024], P('pb'), may hold values from 0 to 1022, as said below
- index_query: bfloat16 [1024, 64, 128], P('pb', 'ha'), may hold values from -0.6 to 0.6
- index_key: bfloat16 [1024, 128], P('pb'), may hold values from -4 to 4
- index_weight: float32 [1024, 64], P('pb', 'ha'), may hold values from -4 to 4
Outputs:
- index_query_grad: bfloat16 [1024, 64, 128], P('pb', 'ha')
- index_key_grad: bfloat16 [1024, 128], P('pb')
- index_weight_grad: float32 [1024, 64], P('pb', 'ha')
The draws below stay inside these ranges and needn't reach their ends.
Inputs may be any that keep to these rules, and one draw needn't show every extreme that they name: window_start[0] is 0, window_start[t] is at most t - 1 for t >= 1, and window_start[1023] is 1022, so every query sees itself and, past the first, at least one earlier key.
All inputs are finite; a program needn't handle non-finite values.
Results may differ from the reference program's by a relative error of at most 0.0049.
Values may be sent and summed in bfloat16 or wider, within the bound.
No kernel may reach another device: no remote copies, remote signals or barrier semaphores. Data moves between devices by JAX's collectives and lax.ppermute only.
A program may use at most 64 MiB of HBM per device.

```python
import jax
import jax.numpy as jnp
from jax import lax

HEADS = 128
LAT = 576
IHEADS = 64
IDIM = 128
TOK_DEV = 128
TOKENS = 1024


def draw_window_start(key, part):
    positions = jnp.arange(TOKENS, dtype=jnp.int32)
    upper = jnp.maximum(positions, 1)
    starts = jax.random.randint(jax.random.fold_in(key, 7), (TOKENS,), 0, upper, dtype=jnp.int32)
    return jnp.where(positions == TOKENS - 1, jnp.int32(TOKENS - 2), starts).astype(jnp.int32)


def draw_main_query(key, part):
    base_key = jax.random.fold_in(key, 31)
    values = jnp.clip(0.3 * jax.random.normal(base_key, (TOKENS, HEADS, LAT), jnp.float32), -1.8, 1.8)
    return values.astype(jnp.bfloat16)


def draw_latent(key, part):
    base_key = jax.random.fold_in(key, 41)
    values = jnp.clip(jax.random.normal(base_key, (TOKENS, LAT), jnp.float32), -6.0, 6.0)
    return values.astype(jnp.bfloat16)


def index_tables(key):
    weight_key = jax.random.fold_in(key, 21)
    keys_key = jax.random.fold_in(key, 22)
    query_key = jax.random.fold_in(key, 23)
    scale_key = jax.random.fold_in(key, 24)
    weights = jnp.clip(jax.random.normal(weight_key, (TOKENS, IHEADS), jnp.float32), -4.0, 4.0)
    keys = jnp.clip(jax.random.normal(keys_key, (TOKENS, IDIM), jnp.float32), -4.0, 4.0)
    queries = 0.044 * jnp.clip(jax.random.normal(query_key, (TOKENS, IHEADS, IDIM), jnp.float32), -4.0, 4.0)
    scales = jnp.exp(jax.random.uniform(scale_key, (TOKENS, 1, 1), jnp.float32, jnp.log(0.5), jnp.log(2.0)))
    queries = queries * scales
    return (weights, keys, queries)


def draw_index_query(key, part):
    return index_tables(key)[2].astype(jnp.bfloat16)


def draw_index_key(key, part):
    return index_tables(key)[1].astype(jnp.bfloat16)


def draw_index_weight(key, part):
    return index_tables(key)[0]


def steps_of(rng, dims, shards, smallest, largest):
    def one(dim, blocks):
        steps = jax.random.uniform(jax.random.fold_in(jax.random.fold_in(rng, 6), dim), (blocks,), jnp.float32, smallest / len(shards), largest / len(shards))
        return jnp.repeat(jnp.exp(steps), dims[dim] // blocks).reshape((-1,) + (1,) * (len(dims) - dim - 1))

    gain = one(*shards[0])
    for cut in shards[1:]:
        gain = gain * one(*cut)
    return gain


def setup_inputs(seed: int = 0) -> dict:
    key_of = jax.random.split(jax.random.key(seed), 8)
    return {
        "main_query": draw_main_query(jax.random.fold_in(key_of[7], 71), 0),
        "latent": draw_latent(jax.random.fold_in(key_of[7], 71), 0),
        "log_sums": jnp.clip(4.0 * jax.random.uniform(key_of[2], (TOKENS, HEADS), jnp.float32) ** steps_of(key_of[2], (TOKENS, HEADS), ((0, 8), (1, 4)), -0.2, 0.2), 0.0, 4.0),
        "window_start": draw_window_start(jax.random.fold_in(key_of[7], 71), 0),
        "index_query": draw_index_query(jax.random.fold_in(key_of[7], 71), 0),
        "index_key": draw_index_key(jax.random.fold_in(key_of[7], 71), 0),
        "index_weight": draw_index_weight(jax.random.fold_in(key_of[7], 71), 0),
    }


main_scale = 192.0 ** -0.5
very_low = -1e30


def reference(main_query, latent, log_sums, window_start, index_query, index_key, index_weight):
    tokens = latent.shape[0]
    blocks = tokens // TOK_DEV
    columns = jnp.arange(tokens, dtype=jnp.int32)
    latent_wide = latent.astype(jnp.float32)
    keys_wide = index_key.astype(jnp.float32)
    first_rows = jnp.arange(blocks, dtype=jnp.int32) * TOK_DEV

    def one_block(key_grad, inputs):
        query_block, sums_block, start_block, index_block, weight_block, first_row = inputs
        positions = first_row + jnp.arange(TOK_DEV, dtype=jnp.int32)
        visible_mask = (columns[None, :] >= start_block[:, None]) & (columns[None, :] <= positions[:, None])
        scores = jnp.dot(query_block.reshape(TOK_DEV * HEADS, LAT).astype(jnp.float32), latent_wide.T, preferred_element_type=jnp.float32)
        scores = scores.reshape(TOK_DEV, HEADS, tokens) * main_scale
        head_probs = jnp.where(visible_mask, jnp.sum(jnp.exp(scores - sums_block[:, :, None]), axis=1), 0.0)
        target = head_probs / jnp.sum(head_probs, axis=1, keepdims=True)
        flat_index = index_block.reshape(TOK_DEV * IHEADS, IDIM)
        act = jnp.dot(flat_index.astype(jnp.float32), keys_wide.T, preferred_element_type=jnp.float32)
        act = act.reshape(TOK_DEV, IHEADS, tokens)
        relu_act = jnp.maximum(act, 0.0)
        logits = jnp.sum(weight_block[:, :, None] * relu_act, axis=1)
        masked = jnp.where(visible_mask, logits, very_low)
        row_top = jnp.max(masked, axis=1, keepdims=True)
        expo = jnp.where(visible_mask, jnp.exp(masked - row_top), 0.0)
        logit_grad = jnp.where(visible_mask, expo / jnp.sum(expo, axis=1, keepdims=True) - target, 0.0)
        weight_grad = jnp.sum(logit_grad[:, None, :] * relu_act, axis=2)
        coeffs = jnp.where(act > 0.0, logit_grad[:, None, :] * weight_block[:, :, None], 0.0).astype(jnp.bfloat16)
        coeffs = coeffs.reshape(TOK_DEV * IHEADS, tokens).astype(jnp.float32)
        query_grad = jnp.dot(coeffs, keys_wide, preferred_element_type=jnp.float32).astype(jnp.bfloat16)
        key_grad = key_grad + jnp.dot(coeffs.T, flat_index.astype(jnp.float32), preferred_element_type=jnp.float32)
        return key_grad, (query_grad.reshape(TOK_DEV, IHEADS, IDIM), weight_grad)

    inputs = (main_query.reshape(blocks, TOK_DEV, HEADS, LAT), log_sums.reshape(blocks, TOK_DEV, HEADS),
              window_start.reshape(blocks, TOK_DEV), index_query.reshape(blocks, TOK_DEV, IHEADS, IDIM),
              index_weight.reshape(blocks, TOK_DEV, IHEADS), first_rows)
    key_grad, outputs = lax.scan(one_block, jnp.zeros((tokens, IDIM), jnp.float32), inputs)
    query_grads, weight_grads = outputs
    return (query_grads.reshape(tokens, IHEADS, IDIM), key_grad.astype(jnp.bfloat16), weight_grads.reshape(tokens, IHEADS))
```

```python
import functools

import jax
import jax.numpy as jnp
from jax import lax
from jax.experimental import pallas as pl
from jax.experimental.pallas import tpu as pltpu
from jax.sharding import PartitionSpec as P

main_scale = 192.0 ** (-0.5)
log2e = 1.4426950408889634
very_low = -1e30
group = 4
VMEM = pl.BlockSpec(memory_space=pltpu.VMEM)


def params(**kwargs):
    return pltpu.CompilerParams(vmem_limit_bytes=48 * 1024 * 1024, **kwargs)


def visible_block(rel, rows, start_row):
    me = lax.axis_index("pb")
    keys = (me ^ rel) * rows + lax.broadcasted_iota(jnp.int32, (rows, rows), 0)
    queries = me * rows + lax.broadcasted_iota(jnp.int32, (rows, rows), 1)
    return (keys >= start_row) & (keys <= queries)


def pack_kernel(latent_ref, key_ref, out_ref):
    width = key_ref.shape[1]
    out_ref[:, :width] = key_ref[...]
    out_ref[:, width:] = latent_ref[...].T


def put_slices(outs, turned):
    me = lax.axis_index("ha")
    rows = outs[0].shape[0]
    for r, out in enumerate(outs):
        first = pl.multiple_of((me ^ r) * rows, rows)
        out[...] = turned[pl.ds(first, rows), :].astype(out.dtype)


def index_kernel(count, *refs):
    blocks = refs[:count]
    query_ref, weight_ref = refs[count : count + 2]
    outs = refs[count + 2 : -3]
    keys, total, turned = refs[-3:]
    rows = query_ref.shape[1]
    for k in range(count):
        keys[k * rows : (k + 1) * rows, :] = blocks[k][...]
    total[...] = jnp.zeros_like(total)

    def body(pair, carry):
        two = query_ref[pl.ds(2 * pair, 2)].reshape(2 * rows, -1)
        act = lax.dot_general(
            keys[...], two, (((1,), (1,)), ((), ())), preferred_element_type=jnp.float32
        )
        act = jnp.maximum(act, 0.0)
        total[...] += (
            act[:, :rows] * weight_ref[pl.ds(2 * pair, 1), :]
            + act[:, rows:] * weight_ref[pl.ds(2 * pair + 1, 1), :]
        )
        return carry

    lax.fori_loop(0, query_ref.shape[0] // 2, body, 0)
    for k in range(count):
        turned[:, k * rows : (k + 1) * rows] = total[k * rows : (k + 1) * rows, :].T
    put_slices(outs, turned)


def main_kernel(rels, *refs):
    count = len(rels)
    blocks = refs[:count]
    query_ref, sums_ref, start_ref = refs[count : count + 3]
    outs = refs[count + 3 : -3]
    keys, total, turned = refs[-3:]
    heads, width, rows = query_ref.shape
    step = pl.program_id(0)

    @pl.when(step == 0)
    def _():
        for k in range(count):
            block = blocks[k][...]
            keys[k * rows : (k + 1) * rows, :] = block[:, block.shape[1] - width :]
        total[...] = jnp.zeros_like(total)

    def body(pair, carry):
        two = jnp.concatenate([query_ref[2 * pair], query_ref[2 * pair + 1]], axis=1)
        scores = jnp.dot(keys[...], two, preferred_element_type=jnp.float32)
        first = jnp.exp2(
            scores[:, :rows] * (main_scale * log2e) - sums_ref[pl.ds(2 * pair, 1), :] * log2e
        )
        second = jnp.exp2(
            scores[:, rows:] * (main_scale * log2e) - sums_ref[pl.ds(2 * pair + 1, 1), :] * log2e
        )
        total[...] += first + second
        return carry

    lax.fori_loop(0, heads // 2, body, 0)

    @pl.when(step == pl.num_programs(0) - 1)
    def _():
        for k in range(count):
            seen = visible_block(rels[k], rows, start_ref[...])
            piece = jnp.where(seen, total[k * rows : (k + 1) * rows, :], 0.0)
            turned[:, k * rows : (k + 1) * rows] = piece.T
        put_slices(outs, turned)


def tree(values):
    while len(values) > 1:
        values = [values[i] + values[i + 1] for i in range(0, len(values), 2)]
    return values[0]


def grad_kernel(parts, chunks, *refs):
    logit_refs = refs[: parts * chunks]
    prob_refs = refs[parts * chunks : 2 * parts * chunks]
    start_ref, out_ref = refs[2 * parts * chunks :]
    rows = out_ref.shape[0]
    me = lax.axis_index("pb")
    first = lax.axis_index("ha") * rows
    starts = start_ref[pl.ds(pl.multiple_of(first, rows), rows), :]
    block = rows * parts

    def gather(some):
        return jnp.concatenate(
            [
                tree([some[c * parts + r][...].astype(jnp.float32) for r in range(parts)])
                for c in range(chunks)
            ],
            axis=1,
        )

    logits = gather(logit_refs)
    probs = gather(prob_refs)
    lanes = lax.broadcasted_iota(jnp.int32, logits.shape, 1)
    keys = ((lanes // block) ^ me) * block + lanes % block
    queries = me * block + first + lax.broadcasted_iota(jnp.int32, logits.shape, 0)
    seen = (keys >= starts) & (keys <= queries)
    target = probs / jnp.sum(probs, axis=1, keepdims=True)
    masked = jnp.where(seen, logits, very_low)
    expo = jnp.where(seen, jnp.exp(masked - jnp.max(masked, axis=1, keepdims=True)), 0.0)
    result = expo / jnp.sum(expo, axis=1, keepdims=True) - target
    out_ref[...] = jnp.where(seen, result, 0.0).astype(out_ref.dtype)


def back_kernel(parts, count, *refs):
    grad_refs = refs[:parts]
    blocks = refs[parts : parts + count]
    query_ref, weight_ref = refs[parts + count : parts + count + 2]
    query_out, weight_out = refs[parts + count + 2 : parts + count + 4]
    key_outs = refs[parts + count + 4 : parts + 2 * count + 4]
    keys, turned_keys, grad, grad_turned, key_total, query_total = refs[parts + 2 * count + 4 :]
    heads, rows, width = query_ref.shape
    me = lax.axis_index("ha")
    for r in range(parts):
        size = grad_refs[r].shape[0]
        grad[pl.ds(pl.multiple_of((me ^ r) * size, size), size), :] = grad_refs[r][...].astype(
            jnp.float32
        )
    for k in range(count):
        at = slice(k * rows, (k + 1) * rows)
        keys[at, :] = blocks[k][...]
        turned_keys[:, at] = blocks[k][...].T
        grad_turned[at, :] = grad[:, at].T
    key_total[...] = jnp.zeros_like(key_total)

    def body(pair, carry):
        two = query_ref[pl.ds(2 * pair, 2)].reshape(2 * rows, width)
        act = lax.dot_general(
            keys[...], two, (((1,), (1,)), ((), ())), preferred_element_type=jnp.float32
        )
        coeffs = []
        for half in range(2):
            head = 2 * pair + half
            mine = act[:, half * rows : (half + 1) * rows]
            g = grad_turned[...]
            weight_out[pl.ds(head, 1), :] = jnp.sum(
                g * jnp.maximum(mine, 0.0), axis=0, keepdims=True
            )
            coeffs.append(
                jnp.where(mine > 0.0, g * weight_ref[pl.ds(head, 1), :], 0.0).astype(jnp.bfloat16)
            )
        coeffs = jnp.concatenate(coeffs, axis=1)
        key_total[...] += jnp.dot(coeffs, two, preferred_element_type=jnp.float32)
        found = jnp.dot(turned_keys[...], coeffs, preferred_element_type=jnp.float32)
        for half in range(2):
            query_total[pl.ds(2 * pair + half, rows, stride=heads), :] = found[
                :, half * rows : (half + 1) * rows
            ].T
        return carry

    lax.fori_loop(0, heads // 2, body, 0)
    query_out[...] = query_total[...].astype(query_out.dtype)
    for k in range(count):
        key_outs[k][...] = key_total[k * rows : (k + 1) * rows, :].astype(key_outs[k].dtype)


def sum_kernel(*refs):
    out_ref = refs[-1]
    out_ref[...] = tree([ref[...].astype(jnp.float32) for ref in refs[:-1]]).astype(out_ref.dtype)


def on_device(main_query, latent, log_sums, window_start, index_query, index_key, index_weight):
    rows, head_count, width = main_query.shape
    index_heads, index_width = index_query.shape[1:]
    blocks = lax.axis_size("pb")
    parts = lax.axis_size("ha")
    share = rows // parts
    chunks = blocks // group
    span = group * rows

    def swap(value, axis, rel):
        size = lax.axis_size(axis)
        return lax.ppermute(value, axis, [(i, i ^ rel) for i in range(size)])

    packed = pl.pallas_call(
        pack_kernel,
        out_shape=jax.ShapeDtypeStruct((rows, index_width + width), jnp.bfloat16),
        in_specs=[VMEM, VMEM],
        out_specs=VMEM,
        compiler_params=params(),
    )(latent.T, index_key)
    held = [None] * blocks
    held[0] = packed
    held[1] = swap(packed, "pb", 1)
    for k in range(2, blocks, 2):
        held[k] = swap(packed, "pb", k)
        held[k + 1] = swap(held[k], "pb", 1)

    query_by_head = jnp.transpose(index_query, (1, 0, 2))
    weights = index_weight.T
    sums = log_sums.T
    start_row = window_start.reshape(1, rows)
    start_column = window_start.reshape(rows, 1)
    key_only = pl.BlockSpec((rows, index_width), lambda *_: (0, 0))

    logit_parts, prob_parts = [], []
    for c in range(chunks):
        rels = list(range(c * group, (c + 1) * group))
        mine = pl.pallas_call(
            functools.partial(index_kernel, group),
            grid=(1,),
            out_shape=[jax.ShapeDtypeStruct((share, span), jnp.float32)] * parts,
            in_specs=[key_only] * group + [VMEM, VMEM],
            out_specs=[VMEM] * parts,
            scratch_shapes=[
                pltpu.VMEM((span, index_width), jnp.bfloat16),
                pltpu.VMEM((span, rows), jnp.float32),
                pltpu.VMEM((rows, span), jnp.float32),
            ],
            compiler_params=params(),
            cost_estimate=pl.CostEstimate(
                flops=2 * span * rows * index_heads * index_width,
                bytes_accessed=2 * rows * index_heads * index_width,
                transcendentals=0,
            ),
        )(*[held[k] for k in rels], query_by_head, weights)
        logit_parts += [mine[0]] + [swap(mine[r], "ha", r) for r in range(1, parts)]
    per_step = min(8, head_count)
    for c in range(chunks):
        rels = list(range(c * group, (c + 1) * group))
        mine = pl.pallas_call(
            functools.partial(main_kernel, rels),
            grid=(head_count // per_step,),
            out_shape=[jax.ShapeDtypeStruct((share, span), jnp.bfloat16)] * parts,
            in_specs=[VMEM] * group
            + [
                pl.BlockSpec((per_step, width, rows), lambda i: (i, 0, 0)),
                pl.BlockSpec((per_step, rows), lambda i: (i, 0)),
                VMEM,
            ],
            out_specs=[VMEM] * parts,
            scratch_shapes=[
                pltpu.VMEM((span, width), jnp.bfloat16),
                pltpu.VMEM((span, rows), jnp.float32),
                pltpu.VMEM((rows, span), jnp.float32),
            ],
            compiler_params=params(),
            cost_estimate=pl.CostEstimate(
                flops=2 * span * rows * head_count * width,
                bytes_accessed=2 * rows * head_count * width,
                transcendentals=span * rows * head_count,
            ),
        )(*[held[k] for k in rels], jnp.transpose(main_query, (1, 2, 0)), sums, start_row)
        prob_parts += [mine[0]] + [swap(mine[r], "ha", r) for r in range(1, parts)]

    grad = pl.pallas_call(
        functools.partial(grad_kernel, parts, chunks),
        out_shape=jax.ShapeDtypeStruct((share, chunks * span), jnp.bfloat16),
        in_specs=[VMEM] * (2 * parts * chunks + 1),
        out_specs=VMEM,
        compiler_params=params(),
    )(*logit_parts, *prob_parts, start_column)
    grads = [grad] + [swap(grad, "ha", r) for r in range(1, parts)]

    tokens = blocks * rows
    found = pl.pallas_call(
        functools.partial(back_kernel, parts, blocks),
        grid=(1,),
        out_shape=[
            jax.ShapeDtypeStruct((rows * index_heads, index_width), jnp.bfloat16),
            jax.ShapeDtypeStruct((index_heads, rows), jnp.float32),
        ]
        + [jax.ShapeDtypeStruct((rows, index_width), jnp.bfloat16)] * blocks,
        in_specs=[VMEM] * parts + [key_only] * blocks + [VMEM, VMEM],
        out_specs=[VMEM] * (2 + blocks),
        scratch_shapes=[
            pltpu.VMEM((tokens, index_width), jnp.bfloat16),
            pltpu.VMEM((index_width, tokens), jnp.bfloat16),
            pltpu.VMEM((rows, tokens), jnp.float32),
            pltpu.VMEM((tokens, rows), jnp.float32),
            pltpu.VMEM((tokens, index_width), jnp.float32),
            pltpu.VMEM((rows * index_heads, index_width), jnp.float32),
        ],
        compiler_params=params(),
    )(*grads, *held, query_by_head, weights)
    query_grad, weight_grad = found[:2]
    terms = [found[2]] + [swap(found[2 + k], "pb", k) for k in range(1, blocks)]

    def add_up(values):
        return pl.pallas_call(
            sum_kernel,
            out_shape=jax.ShapeDtypeStruct(values[0].shape, jnp.bfloat16),
            in_specs=[VMEM] * len(values),
            out_specs=VMEM,
            compiler_params=params(),
        )(*values)

    mine = add_up(terms)
    key_grad = add_up([mine] + [swap(mine, "ha", r) for r in range(1, parts)])
    return (query_grad.reshape(index_query.shape), key_grad, weight_grad.T)


def solution(mesh):
    return jax.shard_map(
        on_device,
        mesh=mesh,
        in_specs=(
            P("pb", "ha", None),
            P("pb", None),
            P("pb", "ha"),
            P("pb"),
            P("pb", "ha", None),
            P("pb", None),
            P("pb", "ha"),
        ),
        out_specs=(P("pb", "ha", None), P("pb", None), P("pb", "ha")),
        check_vma=False,
    )
```

```python
import functools

import jax
import jax.numpy as jnp
from jax import lax
from jax.experimental import pallas as pl
from jax.experimental.pallas import tpu as pltpu
from jax.sharding import PartitionSpec as P

main_scale = 192.0 ** (-0.5)
log2e = 1.4426950408889634
very_low = -1e30
group = 4
VMEM = pl.BlockSpec(memory_space=pltpu.VMEM)


def params(**kwargs):
    return pltpu.CompilerParams(vmem_limit_bytes=48 * 1024 * 1024, **kwargs)


def visible_block(rel, rows, start_row):
    me = lax.axis_index("pb")
    keys = (me ^ rel) * rows + lax.broadcasted_iota(jnp.int32, (rows, rows), 0)
    queries = me * rows + lax.broadcasted_iota(jnp.int32, (rows, rows), 1)
    return (keys >= start_row) & (keys <= queries)


def pack_kernel(latent_ref, key_ref, out_ref):
    width = key_ref.shape[1]
    out_ref[:, :width] = key_ref[...]
    out_ref[:, width:] = latent_ref[...].T


def index_kernel(count, *refs):
    blocks = refs[:count]
    query_ref, weight_ref = refs[count : count + 2]
    out_ref, keys, total = refs[count + 2 :]
    rows = query_ref.shape[1]
    for k in range(count):
        keys[k * rows : (k + 1) * rows, :] = blocks[k][...]
    total[...] = jnp.zeros_like(total)

    def body(pair, carry):
        two = query_ref[pl.ds(2 * pair, 2)].reshape(2 * rows, -1)
        act = lax.dot_general(
            keys[...], two, (((1,), (1,)), ((), ())), preferred_element_type=jnp.float32
        )
        act = jnp.maximum(act, 0.0)
        total[...] += (
            act[:, :rows] * weight_ref[pl.ds(2 * pair, 1), :]
            + act[:, rows:] * weight_ref[pl.ds(2 * pair + 1, 1), :]
        )
        return carry

    lax.fori_loop(0, query_ref.shape[0] // 2, body, 0)
    for k in range(count):
        out_ref[:, k * rows : (k + 1) * rows] = total[k * rows : (k + 1) * rows, :].T


def main_kernel(rels, *refs):
    count = len(rels)
    blocks = refs[:count]
    query_ref, sums_ref, start_ref = refs[count : count + 3]
    out_ref, keys, total = refs[count + 3 :]
    heads, width, rows = query_ref.shape
    step = pl.program_id(0)

    @pl.when(step == 0)
    def _():
        for k in range(count):
            block = blocks[k][...]
            keys[k * rows : (k + 1) * rows, :] = block[:, block.shape[1] - width :]
        total[...] = jnp.zeros_like(total)

    def body(pair, carry):
        two = jnp.concatenate([query_ref[2 * pair], query_ref[2 * pair + 1]], axis=1)
        scores = jnp.dot(keys[...], two, preferred_element_type=jnp.float32)
        first = jnp.exp2(
            scores[:, :rows] * (main_scale * log2e) - sums_ref[pl.ds(2 * pair, 1), :] * log2e
        )
        second = jnp.exp2(
            scores[:, rows:] * (main_scale * log2e) - sums_ref[pl.ds(2 * pair + 1, 1), :] * log2e
        )
        total[...] += first + second
        return carry

    lax.fori_loop(0, heads // 2, body, 0)

    @pl.when(step == pl.num_programs(0) - 1)
    def _():
        for k in range(count):
            seen = visible_block(rels[k], rows, start_ref[...])
            piece = jnp.where(seen, total[k * rows : (k + 1) * rows, :], 0.0)
            out_ref[:, k * rows : (k + 1) * rows] = piece.T.astype(out_ref.dtype)


def tree(values):
    while len(values) > 1:
        values = [values[i] + values[i + 1] for i in range(0, len(values), 2)]
    return values[0]


def grad_kernel(chunks, *refs):
    logit_refs = refs[:chunks]
    prob_refs = refs[chunks : 2 * chunks]
    start_ref, out_ref = refs[2 * chunks :]
    copies, rows = out_ref.shape[:2]
    me = lax.axis_index("pb")
    first = lax.axis_index("ha") * rows
    starts = start_ref[pl.ds(pl.multiple_of(first, rows), rows), :]
    block = rows * copies

    def gather(some):
        return jnp.concatenate(
            [
                tree([part[r].astype(jnp.float32) for r in range(copies)])
                for part in some
            ],
            axis=1,
        )

    logits = gather(logit_refs)
    probs = gather(prob_refs)
    lanes = lax.broadcasted_iota(jnp.int32, logits.shape, 1)
    keys = ((lanes // block) ^ me) * block + lanes % block
    queries = me * block + first + lax.broadcasted_iota(jnp.int32, logits.shape, 0)
    seen = (keys >= starts) & (keys <= queries)
    target = probs / jnp.sum(probs, axis=1, keepdims=True)
    masked = jnp.where(seen, logits, very_low)
    expo = jnp.where(seen, jnp.exp(masked - jnp.max(masked, axis=1, keepdims=True)), 0.0)
    result = expo / jnp.sum(expo, axis=1, keepdims=True) - target
    result = jnp.where(seen, result, 0.0).astype(out_ref.dtype)
    for r in range(copies):
        out_ref[r] = result


def back_kernel(count, *refs):
    grad_ref = refs[0]
    blocks = refs[1 : 1 + count]
    query_ref, weight_ref, query_out, weight_out, key_out = refs[1 + count : 6 + count]
    keys, turned_keys, grad_turned, key_total, query_total = refs[6 + count :]
    heads, rows, width = query_ref.shape
    me = lax.axis_index("pb")
    for k in range(count):
        at = slice(k * rows, (k + 1) * rows)
        keys[at, :] = blocks[k][...]
        turned_keys[:, at] = blocks[k][...].T
        grad_turned[at, :] = grad_ref[:, at].astype(jnp.float32).T
    key_total[...] = jnp.zeros_like(key_total)

    def body(pair, carry):
        two = query_ref[pl.ds(2 * pair, 2)].reshape(2 * rows, width)
        act = lax.dot_general(
            keys[...], two, (((1,), (1,)), ((), ())), preferred_element_type=jnp.float32
        )
        coeffs = []
        for half in range(2):
            head = 2 * pair + half
            mine = act[:, half * rows : (half + 1) * rows]
            g = grad_turned[...]
            weight_out[pl.ds(head, 1), :] = jnp.sum(
                g * jnp.maximum(mine, 0.0), axis=0, keepdims=True
            )
            coeffs.append(
                jnp.where(mine > 0.0, g * weight_ref[pl.ds(head, 1), :], 0.0).astype(jnp.bfloat16)
            )
        coeffs = jnp.concatenate(coeffs, axis=1)
        key_total[...] += jnp.dot(coeffs, two, preferred_element_type=jnp.float32)
        found = jnp.dot(turned_keys[...], coeffs, preferred_element_type=jnp.float32)
        for half in range(2):
            query_total[pl.ds(2 * pair + half, rows, stride=heads), :] = found[
                :, half * rows : (half + 1) * rows
            ].T
        return carry

    lax.fori_loop(0, heads // 2, body, 0)
    query_out[...] = query_total[...].astype(query_out.dtype)
    for k in range(count):
        at = pl.ds(pl.multiple_of((me ^ k) * rows, rows), rows)
        key_out[at, :] = key_total[k * rows : (k + 1) * rows, :].astype(key_out.dtype)


def sum_kernel(in_ref, out_ref):
    total = tree([in_ref[i].astype(jnp.float32) for i in range(in_ref.shape[0])])
    total = total.astype(out_ref.dtype)
    if len(out_ref.shape) == 2:
        out_ref[...] = total
    else:
        for r in range(out_ref.shape[0]):
            out_ref[r] = total


def on_device(main_query, latent, log_sums, window_start, index_query, index_key, index_weight):
    rows, head_count, width = main_query.shape
    index_heads, index_width = index_query.shape[1:]
    blocks = lax.axis_size("pb")
    parts = lax.axis_size("ha")
    share = rows // parts
    chunks = blocks // group
    span = group * rows

    def swap(value, axis, rel):
        size = lax.axis_size(axis)
        return lax.ppermute(value, axis, [(i, i ^ rel) for i in range(size)])

    def deal(value, axis):
        return lax.all_to_all(value, axis, 0, 0)

    packed = pl.pallas_call(
        pack_kernel,
        out_shape=jax.ShapeDtypeStruct((rows, index_width + width), jnp.bfloat16),
        in_specs=[VMEM, VMEM],
        out_specs=VMEM,
        compiler_params=params(),
    )(latent.T, index_key)
    held = [None] * blocks
    held[0] = packed
    held[1] = swap(packed, "pb", 1)
    for k in range(2, blocks, 2):
        held[k] = swap(packed, "pb", k)
        held[k + 1] = swap(held[k], "pb", 1)

    query_by_head = jnp.transpose(index_query, (1, 0, 2))
    weights = index_weight.T
    sums = log_sums.T
    start_row = window_start.reshape(1, rows)
    start_column = window_start.reshape(rows, 1)
    key_only = pl.BlockSpec((rows, index_width), lambda *_: (0, 0))

    logit_parts, prob_parts = [], []
    for c in range(chunks):
        rels = list(range(c * group, (c + 1) * group))
        mine = pl.pallas_call(
            functools.partial(index_kernel, group),
            grid=(1,),
            out_shape=jax.ShapeDtypeStruct((rows, span), jnp.float32),
            in_specs=[key_only] * group + [VMEM, VMEM],
            out_specs=VMEM,
            scratch_shapes=[
                pltpu.VMEM((span, index_width), jnp.bfloat16),
                pltpu.VMEM((span, rows), jnp.float32),
            ],
            compiler_params=params(),
            cost_estimate=pl.CostEstimate(
                flops=2 * span * rows * index_heads * index_width,
                bytes_accessed=2 * rows * index_heads * index_width,
                transcendentals=0,
            ),
        )(*[held[k] for k in rels], query_by_head, weights)
        logit_parts.append(deal(mine.reshape(parts, share, span), "ha"))
    per_step = min(8, head_count)
    for c in range(chunks):
        rels = list(range(c * group, (c + 1) * group))
        mine = pl.pallas_call(
            functools.partial(main_kernel, rels),
            grid=(head_count // per_step,),
            out_shape=jax.ShapeDtypeStruct((rows, span), jnp.bfloat16),
            in_specs=[VMEM] * group
            + [
                pl.BlockSpec((per_step, width, rows), lambda i: (i, 0, 0)),
                pl.BlockSpec((per_step, rows), lambda i: (i, 0)),
                VMEM,
            ],
            out_specs=VMEM,
            scratch_shapes=[
                pltpu.VMEM((span, width), jnp.bfloat16),
                pltpu.VMEM((span, rows), jnp.float32),
            ],
            compiler_params=params(),
            cost_estimate=pl.CostEstimate(
                flops=2 * span * rows * head_count * width,
                bytes_accessed=2 * rows * head_count * width,
                transcendentals=span * rows * head_count,
            ),
        )(*[held[k] for k in rels], jnp.transpose(main_query, (1, 2, 0)), sums, start_row)
        prob_parts.append(deal(mine.reshape(parts, share, span), "ha"))

    tokens = blocks * rows
    grad = pl.pallas_call(
        functools.partial(grad_kernel, chunks),
        out_shape=jax.ShapeDtypeStruct((parts, share, tokens), jnp.bfloat16),
        in_specs=[VMEM] * (2 * chunks + 1),
        out_specs=VMEM,
        compiler_params=params(),
    )(*logit_parts, *prob_parts, start_column)
    grad = deal(grad, "ha").reshape(rows, tokens)

    query_grad, weight_grad, terms = pl.pallas_call(
        functools.partial(back_kernel, blocks),
        grid=(1,),
        out_shape=[
            jax.ShapeDtypeStruct((rows * index_heads, index_width), jnp.bfloat16),
            jax.ShapeDtypeStruct((index_heads, rows), jnp.float32),
            jax.ShapeDtypeStruct((tokens, index_width), jnp.bfloat16),
        ],
        in_specs=[VMEM] + [key_only] * blocks + [VMEM, VMEM],
        out_specs=[VMEM] * 3,
        scratch_shapes=[
            pltpu.VMEM((tokens, index_width), jnp.bfloat16),
            pltpu.VMEM((index_width, tokens), jnp.bfloat16),
            pltpu.VMEM((tokens, rows), jnp.float32),
            pltpu.VMEM((tokens, index_width), jnp.float32),
            pltpu.VMEM((rows * index_heads, index_width), jnp.float32),
        ],
        compiler_params=params(),
    )(grad, *held, query_by_head, weights)

    def add_up(values, shape):
        return pl.pallas_call(
            sum_kernel,
            out_shape=jax.ShapeDtypeStruct(shape, jnp.bfloat16),
            in_specs=[VMEM],
            out_specs=VMEM,
            compiler_params=params(),
        )(values)

    terms = deal(terms.reshape(blocks, rows, index_width), "pb")
    mine = deal(add_up(terms, (parts, rows, index_width)), "ha")
    key_grad = add_up(mine, (rows, index_width))
    return (query_grad.reshape(index_query.shape), key_grad, weight_grad.T)


def solution(mesh):
    return jax.shard_map(
        on_device,
        mesh=mesh,
        in_specs=(
            P("pb", "ha", None),
            P("pb", None),
            P("pb", "ha"),
            P("pb"),
            P("pb", "ha", None),
            P("pb", None),
            P("pb", "ha"),
        ),
        out_specs=(P("pb", "ha", None), P("pb", None), P("pb", "ha")),
        check_vma=False,
    )
```

```python
import functools

import jax
import jax.numpy as jnp
from jax import lax
from jax.experimental import pallas as pl
from jax.experimental.pallas import tpu as pltpu
from jax.sharding import PartitionSpec as P

main_scale = 192.0 ** (-0.5)
log2e = 1.4426950408889634
very_low = -1e30
LANES = 128
TAIL = 16
f32, bf16 = jnp.float32, jnp.bfloat16


def params():
    return pltpu.CompilerParams(vmem_limit_bytes=48 * 1024 * 1024)


def whole(value):
    zeros = (0,) * len(value.shape)
    return pl.BlockSpec(value.shape, lambda *_: zeros)


def call(kernel, outs, values, scratch=(), specs=None, cost=None):
    many = isinstance(outs, list)
    found = pl.pallas_call(
        kernel,
        grid=(1,),
        out_shape=outs,
        in_specs=specs or [whole(v) for v in values],
        out_specs=[whole(o) for o in outs] if many else whole(outs),
        scratch_shapes=list(scratch),
        compiler_params=params(),
        cost_estimate=cost,
    )(*values)
    return list(found) if many else found


def tree(values):
    while len(values) > 1:
        values = [values[i] + values[i + 1] for i in range(0, len(values), 2)]
    return values[0]


def terms_of(value, count):
    found = []
    for _ in range(count):
        term = value.astype(bf16)
        found.append(term)
        value = value - term.astype(f32)
    return found


def pack_kernel(latent_ref, key_ref, query_ref, weight_ref, packed_ref, *outs):
    width = key_ref.shape[1]
    packed_ref[:, :width] = key_ref[...]
    packed_ref[:, width:] = latent_ref[...].T
    me = lax.axis_index("ha")
    heads = weight_ref.shape[0]
    rows = outs[0].shape[0] - 3 * TAIL
    split = terms_of(weight_ref[...], 3)
    for r, out in enumerate(outs):
        first = pl.multiple_of((me ^ r) * rows, rows)
        out[:rows, :] = query_ref[pl.ds(first, rows), :]
        for i in range(3):
            at = rows + i * TAIL
            if heads < TAIL:
                out[at : at + TAIL, :] = jnp.zeros((TAIL, LANES), bf16)
            out[at : at + heads, :] = split[i]


def own_lanes(value, share):
    me = lax.axis_index("ha")
    value = pltpu.roll(value, lax.rem(LANES - me * share, LANES), 1)
    lanes = lax.broadcasted_iota(jnp.int32, value.shape, 1)
    value = jnp.where(lanes < share, value, jnp.zeros_like(value))
    shift = share
    while shift < LANES:
        value = value + pltpu.roll(value, shift, 1)
        shift *= 2
    return value


def main_kernel(rels, earlier, *refs):
    count = len(rels)
    blocks = refs[:count]
    query_hbm, sums_ref, start_ref = refs[count : count + 3]
    before = refs[count + 3 : count + 3 + earlier]
    outs = refs[count + 3 + earlier : -6]
    keys, query, total, turned, sems, _ = refs[-6:]
    heads, width, rows = query.shape
    pieces = sems.shape[0]
    per = heads // pieces
    copies = [
        pltpu.make_async_copy(
            query_hbm.at[pl.ds(i * per, per)], query.at[pl.ds(i * per, per)], sems.at[i]
        )
        for i in range(pieces)
    ]
    for copy in copies:
        copy.start()
    for k in range(count):
        block = blocks[k][...]
        keys[k * rows : (k + 1) * rows, :] = block[:, block.shape[1] - width :]
    total[...] = jnp.zeros_like(total)

    for i in range(pieces):
        copies[i].wait()
        for pair in range(i * per // 2, (i + 1) * per // 2):
            two = jnp.concatenate([query[2 * pair], query[2 * pair + 1]], axis=1)
            scores = jnp.dot(keys[...], two, preferred_element_type=f32)
            parts = [
                jnp.exp2(
                    scores[:, half * rows : (half + 1) * rows] * (main_scale * log2e)
                    - sums_ref[2 * pair + half : 2 * pair + half + 1, :] * log2e
                )
                for half in range(2)
            ]
            total[...] += parts[0] + parts[1]

    me = lax.axis_index("pb")
    kept = turned.shape[1] - count * rows
    at = 0
    for ref in before:
        turned[:, at : at + ref.shape[1]] = ref[...].astype(f32)
        at += ref.shape[1]
    for k in range(count):
        key = (me ^ rels[k]) * rows + lax.broadcasted_iota(jnp.int32, (rows, rows), 0)
        mine = me * rows + lax.broadcasted_iota(jnp.int32, (rows, rows), 1)
        seen = (key >= start_ref[...]) & (key <= mine)
        piece = jnp.where(seen, total[k * rows : (k + 1) * rows, :], 0.0)
        turned[:, kept + k * rows : kept + (k + 1) * rows] = piece.T
    if len(outs) == 1:
        outs[0][...] = turned[...].astype(bf16)
    else:
        me = lax.axis_index("ha")
        share = outs[0].shape[0]
        for r, out in enumerate(outs):
            first = pl.multiple_of((me ^ r) * share, share)
            out[...] = turned[pl.ds(first, share), :].astype(bf16)


def index_kernel(share, count, parts, heads, *refs):
    blocks = refs[:count]
    messages = refs[count : count + parts]
    start_ref, prob_ref, queries_ref, weights_ref, keys, wide, total = refs[count + parts :]
    rows, width = blocks[0].shape
    for k in range(count):
        keys[k * rows : (k + 1) * rows, :] = blocks[k][...]
    own = share * heads
    repeats = LANES // share
    group = lax.broadcasted_iota(jnp.int32, (1, LANES), 1) // share
    row_of = []
    for r in range(parts):
        wide[...] = messages[r][:own, :].astype(f32)
        for j in range(heads):
            first = (r * heads + j) * share
            queries_ref[first : first + share, :] = wide[
                pl.ds(j, share, stride=heads), :
            ].astype(bf16)
        weight = tree_of_three(messages[r], own)
        weight = own_lanes(weight, share)
        row_of += [weight[j : j + 1, :] for j in range(heads)]
    weights_ref[...] = jnp.zeros_like(weights_ref)
    for g in range(len(row_of) // repeats):
        row = row_of[g * repeats]
        for i in range(1, repeats):
            row = jnp.where(group == i, row_of[g * repeats + i], row)
        weights_ref[g : g + 1, :] = row
    total[...] = jnp.zeros_like(total)
    for g in range(0, len(row_of) // repeats, 2):
        two = queries_ref[g * LANES : (g + 2) * LANES, :]
        act = lax.dot_general(
            keys[...], two, (((1,), (1,)), ((), ())), preferred_element_type=f32
        )
        act = jnp.maximum(act, 0.0)
        total[...] += (
            act[:, :LANES] * weights_ref[g : g + 1, :]
            + act[:, LANES:] * weights_ref[g + 1 : g + 2, :]
        )

    me = lax.axis_index("pb")
    lane = lax.broadcasted_iota(jnp.int32, (rows, LANES), 1) % share
    mine = me * rows + lax.axis_index("ha") * share + lane
    start = own_lanes(jnp.broadcast_to(start_ref[...], (8, LANES)), share)[:1, :]
    top = jnp.full((1, LANES), very_low, f32)
    masks = []
    for k in range(count):
        at = slice(k * rows, (k + 1) * rows)
        key = (me ^ k) * rows + lax.broadcasted_iota(jnp.int32, (rows, LANES), 0)
        seen = (key >= start) & (key <= mine)
        value = total[at, :]
        shift = share
        while shift < LANES:
            value = value + pltpu.roll(value, shift, 1)
            shift *= 2
        value = jnp.where(seen, value, very_low)
        total[at, :] = value
        top = jnp.maximum(top, jnp.max(value, axis=0, keepdims=True))
        masks.append(seen)
    mass = jnp.zeros((1, LANES), f32)
    for k in range(count):
        at = slice(k * rows, (k + 1) * rows)
        value = jnp.where(masks[k], jnp.exp(total[at, :] - top), 0.0)
        prob_ref[at, :] = value
        mass = mass + jnp.sum(value, axis=0, keepdims=True)
    prob_ref[...] = prob_ref[...] * (1.0 / mass)


def tree_of_three(ref, at):
    parts = [ref[at + i * TAIL : at + (i + 1) * TAIL, :].astype(f32) for i in range(3)]
    return parts[0] + (parts[1] + parts[2])


def back_kernel(share, count, parts, heads, *refs):
    mass_refs = refs[:parts]
    blocks = refs[parts : parts + count]
    prob_ref, queries_ref, weights_ref = refs[parts + count : parts + count + 3]
    outs = refs[parts + count + 3 : -6]
    even_ref, odd_ref = outs[:2]
    messages = outs[2:]
    keys, turned_keys, grad, key_total, query_total, weight_total = refs[-6:]
    rows, width = blocks[0].shape
    repeats = LANES // share
    mass = tree([ref[...].astype(f32) for ref in mass_refs])
    for k in range(count):
        at = slice(k * rows, (k + 1) * rows)
        keys[at, :] = blocks[k][...]
        turned_keys[:, at] = blocks[k][...].T
        grad[at, :] = jnp.concatenate([mass[:, at]] * repeats, axis=0).T
    total = jnp.sum(grad[...], axis=0, keepdims=True)
    grad[...] = prob_ref[...] - grad[...] / total
    key_total[...] = jnp.zeros_like(key_total)
    weight_total[...] = jnp.zeros_like(weight_total)
    all_heads = parts * heads
    for g in range(0, all_heads // repeats, 2):
        two = queries_ref[g * LANES : (g + 2) * LANES, :]
        act = lax.dot_general(
            keys[...], two, (((1,), (1,)), ((), ())), preferred_element_type=f32
        )
        coeffs = []
        for half in range(2):
            mine = act[:, half * LANES : (half + 1) * LANES]
            lean = grad[...]
            weight_total[g + half : g + half + 1, :] = jnp.sum(
                lean * jnp.maximum(mine, 0.0), axis=0, keepdims=True
            )
            coeffs.append(
                jnp.where(
                    mine > 0.0, lean * weights_ref[g + half : g + half + 1, :], 0.0
                ).astype(bf16)
            )
        coeffs = jnp.concatenate(coeffs, axis=1)
        key_total[...] += jnp.dot(coeffs, two, preferred_element_type=f32)
        found = jnp.dot(turned_keys[...], coeffs, preferred_element_type=f32)
        found = jnp.concatenate([found[:, :LANES].T, found[:, LANES:].T], axis=0)
        for i in range(2 * repeats):
            head = g * repeats + i
            first = (head // heads) * heads * share + head % heads
            query_total[pl.ds(first, share, stride=heads), :] = found[
                i * share : (i + 1) * share, :
            ]
    own = share * heads
    split = terms_of(weight_total[...], 2)
    for r in range(parts):
        messages[r][:own, :] = query_total[r * own : (r + 1) * own, :].astype(bf16)
        for i in range(2):
            messages[r][own + i * TAIL : own + (i + 1) * TAIL, :] = split[i]
    for i in range(count // 2):
        at = slice(i * rows, (i + 1) * rows)
        even_ref[at, :] = key_total[2 * i * rows : (2 * i + 1) * rows, :]
        odd_ref[at, :] = key_total[(2 * i + 1) * rows : (2 * i + 2) * rows, :]


def pair_kernel(mine_ref, other_ref, own_ref, *outs):
    rows = own_ref.shape[0]
    own_ref[...] = mine_ref[:rows, :] + other_ref[:rows, :]
    for i, out in enumerate(outs):
        at = slice((i + 1) * rows, (i + 2) * rows)
        out[...] = (mine_ref[at, :] + other_ref[at, :]).astype(out.dtype)


def sum_kernel(*refs):
    out_ref = refs[-1]
    out_ref[...] = tree([ref[...].astype(f32) for ref in refs[:-1]]).astype(out_ref.dtype)


def finish_kernel(share, heads, *refs):
    messages = refs[:-2]
    query_out, weight_out = refs[-2:]
    me = lax.axis_index("ha")
    own = share * heads
    total = jnp.zeros((heads, LANES), f32)
    lanes = lax.broadcasted_iota(jnp.int32, (heads, LANES), 1)
    for r, message in enumerate(messages):
        first = pl.multiple_of((me ^ r) * own, own)
        query_out[pl.ds(first, own), :] = message[:own, :]
        value = message[own : own + TAIL, :].astype(f32) + message[
            own + TAIL : own + 2 * TAIL, :
        ].astype(f32)
        rolled = {}
        found = []
        for j in range(heads):
            column = (r * heads + j) * share
            row, lane = column // LANES, column % LANES
            if lane not in rolled:
                rolled[lane] = pltpu.roll(value, LANES - lane, 1) if lane else value
            found.append(rolled[lane][row : row + 1, :])
        piece = jnp.where(lanes < share, jnp.concatenate(found, axis=0), 0.0)
        total = total + pltpu.roll(piece, (me ^ r) * share, 1)
    weight_out[...] = total


def on_device(main_query, latent, log_sums, window_start, index_query, index_key, index_weight):
    rows, head_count, width = main_query.shape
    heads, index_width = index_query.shape[1:]
    blocks = lax.axis_size("pb")
    parts = lax.axis_size("ha")
    share = rows // parts
    tokens = blocks * rows
    own = share * heads
    columns = share * heads * parts
    shape = jax.ShapeDtypeStruct

    def swap(value, axis, rel):
        size = lax.axis_size(axis)
        return lax.ppermute(value, axis, [(i, i ^ rel) for i in range(size)])

    start_row = window_start.reshape(1, rows)
    key_only = pl.BlockSpec((rows, index_width), lambda *_: (0, 0))

    packed, *asked = call(
        pack_kernel,
        [shape((rows, index_width + width), bf16)]
        + [shape((own + 3 * TAIL, index_width), bf16)] * parts,
        (latent.T, index_key, index_query.reshape(rows * heads, index_width), index_weight.T),
    )
    held = [None] * blocks
    held[0] = packed
    held[1] = swap(packed, "pb", 1)
    for k in range(2, blocks, 2):
        held[k] = swap(packed, "pb", k)
        held[k + 1] = swap(held[k], "pb", 1)
    asked = [asked[0]] + [swap(asked[r], "ha", r) for r in range(1, parts)]

    queries = jnp.transpose(main_query, (1, 2, 0))
    sums = log_sums.T
    chunks = [[0, 1]] + [list(range(k, min(k + 4, blocks))) for k in range(2, blocks, 4)]
    pieces = max(1, head_count // 8)
    mass = []
    for rels in chunks:
        last = rels is chunks[-1]
        span = len(rels) * rows
        outs = [shape((share, tokens), bf16)] * parts if last else [shape((rows, span), bf16)]
        before = mass if last else []
        values = [held[k] for k in rels] + [queries, sums, start_row] + before
        specs = [whole(v) for v in values]
        specs[len(rels)] = pl.BlockSpec(memory_space=pltpu.HBM)
        found = call(
            functools.partial(main_kernel, rels, len(before)),
            outs,
            values,
            [
                pltpu.VMEM((span, width), bf16),
                pltpu.VMEM((head_count, width, rows), bf16),
                pltpu.VMEM((span, rows), f32),
                pltpu.VMEM((rows, tokens if last else span), f32),
                pltpu.SemaphoreType.DMA((pieces,)),
                pltpu.VMEM((8, LANES), f32),
            ],
            specs,
            pl.CostEstimate(
                flops=2 * span * rows * head_count * width,
                bytes_accessed=2 * rows * head_count * width,
                transcendentals=span * rows * head_count,
            ),
        )
        mass = found if last else mass + found
    first, key_block = lax.optimization_barrier((mass[0], held[0]))
    mass = [first] + [swap(mass[r], "ha", r) for r in range(1, parts)]
    key_blocks = [key_block] + held[1:]

    probs, query_rows, weight_rows = call(
        functools.partial(index_kernel, share, blocks, parts, heads),
        [
            shape((tokens, LANES), f32),
            shape((columns, index_width), bf16),
            shape((TAIL, LANES), f32),
        ],
        key_blocks + asked + [start_row],
        [
            pltpu.VMEM((tokens, index_width), bf16),
            pltpu.VMEM((own, index_width), f32),
            pltpu.VMEM((tokens, LANES), f32),
        ],
        [key_only] * blocks + [whole(v) for v in asked + [start_row]],
        pl.CostEstimate(
            flops=2 * tokens * columns * index_width,
            bytes_accessed=2 * columns * index_width,
            transcendentals=tokens * LANES,
        ),
    )

    even, odd, *answers = call(
        functools.partial(back_kernel, share, blocks, parts, heads),
        [shape((tokens // 2, index_width), f32)] * 2
        + [shape((own + 2 * TAIL, index_width), bf16)] * parts,
        mass + key_blocks + [probs, query_rows, weight_rows],
        [
            pltpu.VMEM((tokens, index_width), bf16),
            pltpu.VMEM((index_width, tokens), bf16),
            pltpu.VMEM((tokens, LANES), f32),
            pltpu.VMEM((tokens, index_width), f32),
            pltpu.VMEM((columns, index_width), f32),
            pltpu.VMEM((TAIL, LANES), f32),
        ],
        [whole(v) for v in mass]
        + [key_only] * blocks
        + [whole(v) for v in (probs, query_rows, weight_rows)],
        pl.CostEstimate(
            flops=6 * tokens * columns * index_width,
            bytes_accessed=2 * columns * index_width,
            transcendentals=0,
        ),
    )
    odd = swap(odd, "pb", 1)
    term = shape((rows, index_width), f32)
    half = shape((rows, index_width), bf16)
    mine, *others = call(pair_kernel, [term] + [half] * (blocks // 2 - 1), (even, odd))
    others = [swap(value, "pb", 2 * (i + 1)) for i, value in enumerate(others)]
    mine = call(sum_kernel, half, [mine] + others)
    key_grad = call(sum_kernel, half, [mine] + [swap(mine, "ha", r) for r in range(1, parts)])

    answers = [answers[0]] + [swap(answers[r], "ha", r) for r in range(1, parts)]
    query_grad, weight_grad = call(
        functools.partial(finish_kernel, share, heads),
        [shape((rows * heads, index_width), bf16), shape((heads, rows), f32)],
        answers,
    )
    return (query_grad.reshape(index_query.shape), key_grad, weight_grad.T)


def solution(mesh):
    return jax.shard_map(
        on_device,
        mesh=mesh,
        in_specs=(
            P("pb", "ha", None),
            P("pb", None),
            P("pb", "ha"),
            P("pb"),
            P("pb", "ha", None),
            P("pb", None),
            P("pb", "ha"),
        ),
        out_specs=(P("pb", "ha", None), P("pb", None), P("pb", "ha")),
        check_vma=False,
    )
```

```python
import functools

import jax
import jax.numpy as jnp
from jax import lax
from jax.experimental import pallas as pl
from jax.experimental.pallas import tpu as pltpu
from jax.sharding import PartitionSpec as P

main_scale = 192.0 ** (-0.5)
log2e = 1.4426950408889634
very_low = -1e30
LANES = 128
TAIL = 16
f32, bf16 = jnp.float32, jnp.bfloat16


def params(mega=48):
    return pltpu.CompilerParams(vmem_limit_bytes=mega * 1024 * 1024)


def whole(value):
    zeros = (0,) * len(value.shape)
    return pl.BlockSpec(value.shape, lambda *_: zeros)


def call(kernel, outs, values, scratch=(), specs=None, cost=None, mega=48):
    many = isinstance(outs, list)
    found = pl.pallas_call(
        kernel,
        grid=(1,),
        out_shape=outs,
        in_specs=specs or [whole(v) for v in values],
        out_specs=[whole(o) for o in outs] if many else whole(outs),
        scratch_shapes=list(scratch),
        compiler_params=params(mega),
        cost_estimate=cost,
    )(*values)
    return list(found) if many else found


def tree(values):
    while len(values) > 1:
        values = [values[i] + values[i + 1] for i in range(0, len(values), 2)]
    return values[0]


def terms_of(value, count):
    found = []
    for _ in range(count):
        term = value.astype(bf16)
        found.append(term)
        value = value - term.astype(f32)
    return found


def pack_kernel(latent_ref, key_ref, packed_ref):
    width = key_ref.shape[1]
    packed_ref[:, :width] = key_ref[...]
    packed_ref[:, width:] = latent_ref[...].T


def ask_kernel(query_ref, weight_ref, *outs):
    me = lax.axis_index("ha")
    heads = weight_ref.shape[0]
    rows = outs[0].shape[0] - 3 * TAIL
    split = terms_of(weight_ref[...], 3)
    for r, out in enumerate(outs):
        first = pl.multiple_of((me ^ r) * rows, rows)
        out[:rows, :] = query_ref[pl.ds(first, rows), :]
        for i in range(3):
            at = rows + i * TAIL
            if heads < TAIL:
                out[at : at + TAIL, :] = jnp.zeros((TAIL, LANES), bf16)
            out[at : at + heads, :] = split[i]


def own_lanes(value, share):
    me = lax.axis_index("ha")
    value = pltpu.roll(value, lax.rem(LANES - me * share, LANES), 1)
    lanes = lax.broadcasted_iota(jnp.int32, value.shape, 1)
    value = jnp.where(lanes < share, value, jnp.zeros_like(value))
    shift = share
    while shift < LANES:
        value = value + pltpu.roll(value, shift, 1)
        shift *= 2
    return value


def main_kernel(rels, earlier, *refs):
    count = len(rels)
    blocks = refs[:count]
    query_hbm, sums_ref, start_ref = refs[count : count + 3]
    before = refs[count + 3 : count + 3 + earlier]
    outs = refs[count + 3 + earlier : -6]
    keys, query, total, turned, sems, _ = refs[-6:]
    heads, width, rows = query.shape
    pieces = sems.shape[0]
    per = heads // pieces
    copies = [
        pltpu.make_async_copy(
            query_hbm.at[pl.ds(i * per, per)], query.at[pl.ds(i * per, per)], sems.at[i]
        )
        for i in range(pieces)
    ]
    for copy in copies:
        copy.start()
    for k in range(count):
        block = blocks[k][...]
        keys[k * rows : (k + 1) * rows, :] = block[:, block.shape[1] - width :]
    total[...] = jnp.zeros_like(total)

    for i in range(pieces):
        copies[i].wait()
        for head in range(i * per, (i + 1) * per, 4):
            four = jnp.concatenate([query[head + n] for n in range(4)], axis=1)
            scores = jnp.dot(keys[...], four, preferred_element_type=f32)
            parts = [
                jnp.exp2(
                    scores[:, n * rows : (n + 1) * rows] * (main_scale * log2e)
                    - sums_ref[head + n : head + n + 1, :] * log2e
                )
                for n in range(4)
            ]
            total[...] += tree(parts)

    me = lax.axis_index("pb")
    kept = turned.shape[1] - count * rows
    at = 0
    for ref in before:
        turned[:, at : at + ref.shape[1]] = ref[...].astype(f32)
        at += ref.shape[1]
    for k in range(count):
        key = (me ^ rels[k]) * rows + lax.broadcasted_iota(jnp.int32, (rows, rows), 0)
        mine = me * rows + lax.broadcasted_iota(jnp.int32, (rows, rows), 1)
        seen = (key >= start_ref[...]) & (key <= mine)
        piece = jnp.where(seen, total[k * rows : (k + 1) * rows, :], 0.0)
        turned[:, kept + k * rows : kept + (k + 1) * rows] = piece.T
    if len(outs) == 1:
        outs[0][...] = turned[...].astype(bf16)
    else:
        me = lax.axis_index("ha")
        share = outs[0].shape[0]
        for r, out in enumerate(outs):
            first = pl.multiple_of((me ^ r) * share, share)
            out[...] = turned[pl.ds(first, share), :].astype(bf16)


def index_kernel(share, count, parts, heads, *refs):
    blocks = refs[:count]
    messages = refs[count : count + parts]
    start_ref, prob_ref, queries_ref, weights_ref, keys, wide, total = refs[count + parts :]
    rows, width = blocks[0].shape
    for k in range(count):
        keys[k * rows : (k + 1) * rows, :] = blocks[k][...]
    own = share * heads
    repeats = LANES // share
    group = lax.broadcasted_iota(jnp.int32, (1, LANES), 1) // share
    row_of = []
    for r in range(parts):
        wide[...] = messages[r][:own, :].astype(f32)
        for j in range(heads):
            first = (r * heads + j) * share
            queries_ref[first : first + share, :] = wide[
                pl.ds(j, share, stride=heads), :
            ].astype(bf16)
        weight = tree_of_three(messages[r], own)
        weight = own_lanes(weight, share)
        row_of += [weight[j : j + 1, :] for j in range(heads)]
    weights_ref[...] = jnp.zeros_like(weights_ref)
    for g in range(len(row_of) // repeats):
        row = row_of[g * repeats]
        for i in range(1, repeats):
            row = jnp.where(group == i, row_of[g * repeats + i], row)
        weights_ref[g : g + 1, :] = row
    total[...] = jnp.zeros_like(total)
    for g in range(0, len(row_of) // repeats, 2):
        two = queries_ref[g * LANES : (g + 2) * LANES, :]
        act = lax.dot_general(
            keys[...], two, (((1,), (1,)), ((), ())), preferred_element_type=f32
        )
        act = jnp.maximum(act, 0.0)
        total[...] += (
            act[:, :LANES] * weights_ref[g : g + 1, :]
            + act[:, LANES:] * weights_ref[g + 1 : g + 2, :]
        )

    me = lax.axis_index("pb")
    lane = lax.broadcasted_iota(jnp.int32, (rows, LANES), 1) % share
    mine = me * rows + lax.axis_index("ha") * share + lane
    start = own_lanes(jnp.broadcast_to(start_ref[...], (8, LANES)), share)[:1, :]
    top = jnp.full((1, LANES), very_low, f32)
    masks = []
    for k in range(count):
        at = slice(k * rows, (k + 1) * rows)
        key = (me ^ k) * rows + lax.broadcasted_iota(jnp.int32, (rows, LANES), 0)
        seen = (key >= start) & (key <= mine)
        value = total[at, :]
        shift = share
        while shift < LANES:
            value = value + pltpu.roll(value, shift, 1)
            shift *= 2
        value = jnp.where(seen, value, very_low)
        total[at, :] = value
        top = jnp.maximum(top, jnp.max(value, axis=0, keepdims=True))
        masks.append(seen)
    mass = jnp.zeros((1, LANES), f32)
    for k in range(count):
        at = slice(k * rows, (k + 1) * rows)
        value = jnp.where(masks[k], jnp.exp(total[at, :] - top), 0.0)
        prob_ref[at, :] = value
        mass = mass + jnp.sum(value, axis=0, keepdims=True)
    prob_ref[...] = prob_ref[...] * (1.0 / mass)


def tree_of_three(ref, at):
    parts = [ref[at + i * TAIL : at + (i + 1) * TAIL, :].astype(f32) for i in range(3)]
    return parts[0] + (parts[1] + parts[2])


def back_heads(span, share, heads, keys, turned_keys, grad, queries_ref, weights_ref, totals):
    key_total, query_total, weight_total = totals
    repeats = LANES // share
    base = span[0] * LANES
    for g in range(span[0], span[1], 2):
        two = queries_ref[g * LANES : (g + 2) * LANES, :]
        act = lax.dot_general(
            keys[...], two, (((1,), (1,)), ((), ())), preferred_element_type=f32
        )
        coeffs = []
        for half in range(2):
            mine = act[:, half * LANES : (half + 1) * LANES]
            lean = grad[...]
            weight_total[g + half : g + half + 1, :] = jnp.sum(
                lean * jnp.maximum(mine, 0.0), axis=0, keepdims=True
            )
            coeffs.append(
                jnp.where(
                    mine > 0.0, lean * weights_ref[g + half : g + half + 1, :], 0.0
                ).astype(bf16)
            )
        coeffs = jnp.concatenate(coeffs, axis=1)
        key_total[...] += jnp.dot(coeffs, two, preferred_element_type=f32)
        found = jnp.dot(turned_keys[...], coeffs, preferred_element_type=f32)
        found = jnp.concatenate([found[:, :LANES].T, found[:, LANES:].T], axis=0)
        for i in range(2 * repeats):
            head = g * repeats + i
            first = (head // heads) * heads * share + head % heads - base
            query_total[pl.ds(first, share, stride=heads), :] = found[
                i * share : (i + 1) * share, :
            ]


def put_answers(share, heads, messages, query_total, weight_total):
    own = share * heads
    split = terms_of(weight_total[...], 2)
    for r, message in enumerate(messages):
        message[:own, :] = query_total[r * own : (r + 1) * own, :].astype(bf16)
        for i in range(2):
            message[own + i * TAIL : own + (i + 1) * TAIL, :] = split[i]


def far_kernel(span, share, count, parts, heads, *refs):
    mass_refs = refs[:parts]
    blocks = refs[parts : parts + count]
    prob_ref, queries_ref, weights_ref, grad, key_total = refs[parts + count : parts + count + 5]
    messages = refs[parts + count + 5 : -4]
    keys, turned_keys, query_total, weight_total = refs[-4:]
    rows = blocks[0].shape[0]
    mass = tree([ref[...].astype(f32) for ref in mass_refs])
    for k in range(count):
        at = slice(k * rows, (k + 1) * rows)
        keys[at, :] = blocks[k][...]
        turned_keys[:, at] = blocks[k][...].T
        grad[at, :] = jnp.concatenate([mass[:, at]] * (LANES // share), axis=0).T
    total = jnp.sum(grad[...], axis=0, keepdims=True)
    grad[...] = prob_ref[...] - grad[...] / total
    key_total[...] = jnp.zeros_like(key_total)
    weight_total[...] = jnp.zeros_like(weight_total)
    totals = (key_total, query_total, weight_total)
    back_heads(span, share, heads, keys, turned_keys, grad, queries_ref, weights_ref, totals)
    put_answers(share, heads, messages, query_total, weight_total)


def near_kernel(span, share, count, heads, *refs):
    blocks = refs[:count]
    queries_ref, weights_ref, grad, key_before, even_ref, odd_ref = refs[count : count + 6]
    messages = refs[count + 6 : -5]
    keys, turned_keys, key_total, query_total, weight_total = refs[-5:]
    rows = blocks[0].shape[0]
    for k in range(count):
        at = slice(k * rows, (k + 1) * rows)
        keys[at, :] = blocks[k][...]
        turned_keys[:, at] = blocks[k][...].T
    key_total[...] = key_before[...]
    weight_total[...] = jnp.zeros_like(weight_total)
    totals = (key_total, query_total, weight_total)
    back_heads(span, share, heads, keys, turned_keys, grad, queries_ref, weights_ref, totals)
    put_answers(share, heads, messages, query_total, weight_total)
    for i in range(count // 2):
        at = slice(i * rows, (i + 1) * rows)
        even_ref[at, :] = key_total[2 * i * rows : (2 * i + 1) * rows, :]
        odd_ref[at, :] = key_total[(2 * i + 1) * rows : (2 * i + 2) * rows, :]


def pair_kernel(mine_ref, other_ref, own_ref, *outs):
    rows = own_ref.shape[0]
    own_ref[...] = mine_ref[:rows, :] + other_ref[:rows, :]
    for i, out in enumerate(outs):
        at = slice((i + 1) * rows, (i + 2) * rows)
        out[...] = (mine_ref[at, :] + other_ref[at, :]).astype(out.dtype)


def sum_kernel(*refs):
    out_ref = refs[-1]
    out_ref[...] = tree([ref[...].astype(f32) for ref in refs[:-1]]).astype(out_ref.dtype)


def finish_kernel(share, heads, *refs):
    messages = refs[:-2]
    query_out, weight_out = refs[-2:]
    me = lax.axis_index("ha")
    own = share * heads
    total = jnp.zeros((heads, LANES), f32)
    lanes = lax.broadcasted_iota(jnp.int32, (heads, LANES), 1)
    for r, message in enumerate(messages):
        first = pl.multiple_of((me ^ r) * own, own)
        query_out[pl.ds(first, own), :] = message[:own, :]
        value = message[own : own + TAIL, :].astype(f32) + message[
            own + TAIL : own + 2 * TAIL, :
        ].astype(f32)
        rolled = {}
        found = []
        for j in range(heads):
            column = (r * heads + j) * share
            row, lane = column // LANES, column % LANES
            if lane not in rolled:
                rolled[lane] = pltpu.roll(value, LANES - lane, 1) if lane else value
            found.append(rolled[lane][row : row + 1, :])
        piece = jnp.where(lanes < share, jnp.concatenate(found, axis=0), 0.0)
        total = total + pltpu.roll(piece, (me ^ r) * share, 1)
    weight_out[...] = total


def on_device(main_query, latent, log_sums, window_start, index_query, index_key, index_weight):
    rows, head_count, width = main_query.shape
    heads, index_width = index_query.shape[1:]
    blocks = lax.axis_size("pb")
    parts = lax.axis_size("ha")
    share = rows // parts
    tokens = blocks * rows
    own = share * heads
    columns = share * heads * parts
    shape = jax.ShapeDtypeStruct

    def swap(value, axis, rel):
        size = lax.axis_size(axis)
        return lax.ppermute(value, axis, [(i, i ^ rel) for i in range(size)])

    start_row = window_start.reshape(1, rows)
    key_only = pl.BlockSpec((rows, index_width), lambda *_: (0, 0))

    packed = call(
        pack_kernel, shape((rows, index_width + width), bf16), (latent.T, index_key)
    )
    held = [None] * blocks
    held[0] = packed
    held[1] = swap(packed, "pb", 1)
    for k in range(2, blocks, 2):
        held[k] = swap(packed, "pb", k)
        held[k + 1] = swap(held[k], "pb", 1)
    asked = call(
        ask_kernel,
        [shape((own + 3 * TAIL, index_width), bf16)] * parts,
        (index_query.reshape(rows * heads, index_width), index_weight.T),
    )
    asked = [asked[0]] + [swap(asked[r], "ha", r) for r in range(1, parts)]

    queries = jnp.transpose(main_query, (1, 2, 0))
    sums = log_sums.T
    chunks = [[0, 1]] + [list(range(k, min(k + 4, blocks))) for k in range(2, blocks, 4)]
    pieces = max(1, head_count // 8)
    mass = []
    for rels in chunks:
        last = rels is chunks[-1]
        span = len(rels) * rows
        outs = [shape((share, tokens), bf16)] * parts if last else [shape((rows, span), bf16)]
        before = mass if last else []
        values = [held[k] for k in rels] + [queries, sums, start_row] + before
        specs = [whole(v) for v in values]
        specs[len(rels)] = pl.BlockSpec(memory_space=pltpu.HBM)
        found = call(
            functools.partial(main_kernel, rels, len(before)),
            outs,
            values,
            [
                pltpu.VMEM((span, width), bf16),
                pltpu.VMEM((head_count, width, rows), bf16),
                pltpu.VMEM((span, rows), f32),
                pltpu.VMEM((rows, tokens if last else span), f32),
                pltpu.SemaphoreType.DMA((pieces,)),
                pltpu.VMEM((8, LANES), f32),
            ],
            specs,
            pl.CostEstimate(
                flops=2 * span * rows * head_count * width,
                bytes_accessed=2 * rows * head_count * width,
                transcendentals=span * rows * head_count,
            ),
            60,
        )
        mass = found if last else mass + found
    first, key_block = lax.optimization_barrier((mass[0], held[0]))
    mass = [first] + [swap(mass[r], "ha", r) for r in range(1, parts)]
    key_blocks = [key_block] + held[1:]

    probs, query_rows, weight_rows = call(
        functools.partial(index_kernel, share, blocks, parts, heads),
        [
            shape((tokens, LANES), f32),
            shape((columns, index_width), bf16),
            shape((TAIL, LANES), f32),
        ],
        key_blocks + asked + [start_row],
        [
            pltpu.VMEM((tokens, index_width), bf16),
            pltpu.VMEM((own, index_width), f32),
            pltpu.VMEM((tokens, LANES), f32),
        ],
        [key_only] * blocks + [whole(v) for v in asked + [start_row]],
        pl.CostEstimate(
            flops=2 * tokens * columns * index_width,
            bytes_accessed=2 * columns * index_width,
            transcendentals=tokens * LANES,
        ),
    )

    groups = columns // LANES
    message = shape((own + 2 * TAIL, index_width), bf16)
    cost = pl.CostEstimate(
        flops=3 * tokens * columns * index_width,
        bytes_accessed=2 * columns * index_width,
        transcendentals=0,
    )
    scratch = [
        pltpu.VMEM((tokens, index_width), bf16),
        pltpu.VMEM((index_width, tokens), bf16),
        pltpu.VMEM((columns // 2, index_width), f32),
        pltpu.VMEM((TAIL, LANES), f32),
    ]
    others = [probs, query_rows, weight_rows]
    grad, key_part, *far = call(
        functools.partial(far_kernel, (groups // 2, groups), share, blocks, parts, heads),
        [shape((tokens, LANES), f32), shape((tokens, index_width), f32)] + [message] * (parts // 2),
        mass + key_blocks + others,
        scratch,
        [whole(v) for v in mass] + [key_only] * blocks + [whole(v) for v in others],
        cost,
    )
    others = [query_rows, weight_rows, grad, key_part]
    even, odd, *near = call(
        functools.partial(near_kernel, (0, groups // 2), share, blocks, heads),
        [shape((tokens // 2, index_width), f32)] * 2 + [message] * (parts // 2),
        key_blocks + others,
        scratch[:2] + [pltpu.VMEM((tokens, index_width), f32)] + scratch[2:],
        [key_only] * blocks + [whole(v) for v in others],
        cost,
    )
    odd = swap(odd, "pb", 1)
    term = shape((rows, index_width), f32)
    half = shape((rows, index_width), bf16)
    mine, *others = call(pair_kernel, [term] + [half] * (blocks // 2 - 1), (even, odd))
    mine, near = lax.optimization_barrier((mine, near))
    others = [swap(value, "pb", 2 * (i + 1)) for i, value in enumerate(others)]
    mine = call(sum_kernel, half, [mine] + others)
    key_grad = call(sum_kernel, half, [mine] + [swap(mine, "ha", r) for r in range(1, parts)])

    answers = near + far
    answers = [answers[0]] + [swap(answers[r], "ha", r) for r in range(1, parts)]
    query_grad, weight_grad = call(
        functools.partial(finish_kernel, share, heads),
        [shape((rows * heads, index_width), bf16), shape((heads, rows), f32)],
        answers,
    )
    return (query_grad.reshape(index_query.shape), key_grad, weight_grad.T)


def solution(mesh):
    return jax.shard_map(
        on_device,
        mesh=mesh,
        in_specs=(
            P("pb", "ha", None),
            P("pb", None),
            P("pb", "ha"),
            P("pb"),
            P("pb", "ha", None),
            P("pb", None),
            P("pb", "ha"),
        ),
        out_specs=(P("pb", "ha", None), P("pb", None), P("pb", "ha")),
        check_vma=False,
    )
```

```python
import functools

import jax
import jax.numpy as jnp
from jax import lax
from jax.experimental import pallas as pl
from jax.experimental.pallas import tpu as pltpu
from jax.sharding import PartitionSpec as P

main_scale = 192.0 ** (-0.5)
log2e = 1.4426950408889634
very_low = -1e30
LANES = 128
TAIL = 16
f32, bf16 = jnp.float32, jnp.bfloat16


def params():
    return pltpu.CompilerParams(vmem_limit_bytes=24 * 1024 * 1024)


def whole(value):
    zeros = (0,) * len(value.shape)
    return pl.BlockSpec(value.shape, lambda *_: zeros)


def call(kernel, outs, values, scratch=(), specs=None, cost=None):
    many = isinstance(outs, list)
    found = pl.pallas_call(
        kernel,
        grid=(1,),
        out_shape=outs,
        in_specs=specs or [whole(v) for v in values],
        out_specs=[whole(o) for o in outs] if many else whole(outs),
        scratch_shapes=list(scratch),
        compiler_params=params(),
        cost_estimate=cost,
    )(*values)
    return list(found) if many else found


def tree(values):
    while len(values) > 1:
        values = [values[i] + values[i + 1] for i in range(0, len(values), 2)]
    return values[0]


def terms_of(value, count):
    found = []
    for _ in range(count):
        term = value.astype(bf16)
        found.append(term)
        value = value - term.astype(f32)
    return found


def pack_kernel(latent_ref, key_ref, packed_ref):
    width = key_ref.shape[1]
    packed_ref[:, :width] = key_ref[...]
    packed_ref[:, width:] = latent_ref[...].T


def ask_kernel(query_ref, weight_ref, *outs):
    me = lax.axis_index("ha")
    heads = weight_ref.shape[0]
    rows = outs[0].shape[0] - 3 * TAIL
    split = terms_of(weight_ref[...], 3)
    for r, out in enumerate(outs):
        first = pl.multiple_of((me ^ r) * rows, rows)
        out[:rows, :] = query_ref[pl.ds(first, rows), :]
        for i in range(3):
            at = rows + i * TAIL
            if heads < TAIL:
                out[at : at + TAIL, :] = jnp.zeros((TAIL, LANES), bf16)
            out[at : at + heads, :] = split[i]


def own_lanes(value, share):
    me = lax.axis_index("ha")
    value = pltpu.roll(value, lax.rem(LANES - me * share, LANES), 1)
    lanes = lax.broadcasted_iota(jnp.int32, value.shape, 1)
    value = jnp.where(lanes < share, value, jnp.zeros_like(value))
    shift = share
    while shift < LANES:
        value = value + pltpu.roll(value, shift, 1)
        shift *= 2
    return value


def main_kernel(rels, earlier, *refs):
    count = len(rels)
    blocks = refs[:count]
    query, sums_ref, start_ref = refs[count : count + 3]
    before = refs[count + 3 : count + 3 + earlier]
    outs = refs[count + 3 + earlier : -3]
    keys, total, turned = refs[-3:]
    heads, width, rows = query.shape
    for k in range(count):
        block = blocks[k][...]
        keys[k * rows : (k + 1) * rows, :] = block[:, block.shape[1] - width :]
    total[...] = jnp.zeros_like(total)

    for head in range(0, heads, 2):
        two = jnp.concatenate([query[head], query[head + 1]], axis=1)
        scores = jnp.dot(keys[...], two, preferred_element_type=f32)
        parts = [
            jnp.exp2(
                scores[:, half * rows : (half + 1) * rows] * (main_scale * log2e)
                - sums_ref[head + half : head + half + 1, :] * log2e
            )
            for half in range(2)
        ]
        total[...] += parts[0] + parts[1]

    me = lax.axis_index("pb")
    kept = turned.shape[1] - count * rows
    at = 0
    for ref in before:
        turned[:, at : at + ref.shape[1]] = ref[...].astype(f32)
        at += ref.shape[1]
    for k in range(count):
        key = (me ^ rels[k]) * rows + lax.broadcasted_iota(jnp.int32, (rows, rows), 0)
        mine = me * rows + lax.broadcasted_iota(jnp.int32, (rows, rows), 1)
        seen = (key >= start_ref[...]) & (key <= mine)
        piece = jnp.where(seen, total[k * rows : (k + 1) * rows, :], 0.0)
        turned[:, kept + k * rows : kept + (k + 1) * rows] = piece.T
    if len(outs) == 1:
        outs[0][...] = turned[...].astype(bf16)
    else:
        me = lax.axis_index("ha")
        share = outs[0].shape[0]
        for r, out in enumerate(outs):
            first = pl.multiple_of((me ^ r) * share, share)
            out[...] = turned[pl.ds(first, share), :].astype(bf16)


def index_kernel(share, count, parts, heads, *refs):
    blocks = refs[:count]
    messages = refs[count : count + parts]
    start_ref, prob_ref, queries_ref, weights_ref, keys, wide, total = refs[count + parts :]
    rows, width = blocks[0].shape
    for k in range(count):
        keys[k * rows : (k + 1) * rows, :] = blocks[k][...]
    own = share * heads
    repeats = LANES // share
    group = lax.broadcasted_iota(jnp.int32, (1, LANES), 1) // share
    row_of = []
    for r in range(parts):
        wide[...] = messages[r][:own, :].astype(f32)
        for j in range(heads):
            first = (r * heads + j) * share
            queries_ref[first : first + share, :] = wide[
                pl.ds(j, share, stride=heads), :
            ].astype(bf16)
        weight = tree_of_three(messages[r], own)
        weight = own_lanes(weight, share)
        row_of += [weight[j : j + 1, :] for j in range(heads)]
    weights_ref[...] = jnp.zeros_like(weights_ref)
    for g in range(len(row_of) // repeats):
        row = row_of[g * repeats]
        for i in range(1, repeats):
            row = jnp.where(group == i, row_of[g * repeats + i], row)
        weights_ref[g : g + 1, :] = row
    total[...] = jnp.zeros_like(total)
    for g in range(0, len(row_of) // repeats, 2):
        two = queries_ref[g * LANES : (g + 2) * LANES, :]
        act = lax.dot_general(
            keys[...], two, (((1,), (1,)), ((), ())), preferred_element_type=f32
        )
        act = jnp.maximum(act, 0.0)
        total[...] += (
            act[:, :LANES] * weights_ref[g : g + 1, :]
            + act[:, LANES:] * weights_ref[g + 1 : g + 2, :]
        )

    me = lax.axis_index("pb")
    lane = lax.broadcasted_iota(jnp.int32, (rows, LANES), 1) % share
    mine = me * rows + lax.axis_index("ha") * share + lane
    start = own_lanes(jnp.broadcast_to(start_ref[...], (8, LANES)), share)[:1, :]
    top = jnp.full((1, LANES), very_low, f32)
    masks = []
    for k in range(count):
        at = slice(k * rows, (k + 1) * rows)
        key = (me ^ k) * rows + lax.broadcasted_iota(jnp.int32, (rows, LANES), 0)
        seen = (key >= start) & (key <= mine)
        value = total[at, :]
        shift = share
        while shift < LANES:
            value = value + pltpu.roll(value, shift, 1)
            shift *= 2
        value = jnp.where(seen, value, very_low)
        total[at, :] = value
        top = jnp.maximum(top, jnp.max(value, axis=0, keepdims=True))
        masks.append(seen)
    mass = jnp.zeros((1, LANES), f32)
    for k in range(count):
        at = slice(k * rows, (k + 1) * rows)
        value = jnp.where(masks[k], jnp.exp(total[at, :] - top), 0.0)
        prob_ref[at, :] = value
        mass = mass + jnp.sum(value, axis=0, keepdims=True)
    prob_ref[...] = prob_ref[...] * (1.0 / mass)


def tree_of_three(ref, at):
    parts = [ref[at + i * TAIL : at + (i + 1) * TAIL, :].astype(f32) for i in range(3)]
    return parts[0] + (parts[1] + parts[2])


def back_kernel(share, count, parts, heads, *refs):
    mass_refs = refs[:parts]
    blocks = refs[parts : parts + count]
    prob_ref, queries_ref, weights_ref = refs[parts + count : parts + count + 3]
    outs = refs[parts + count + 3 : -6]
    even_ref, odd_ref = outs[:2]
    messages = outs[2:]
    keys, turned_keys, grad, key_total, query_total, weight_total = refs[-6:]
    rows, width = blocks[0].shape
    repeats = LANES // share
    mass = tree([ref[...].astype(f32) for ref in mass_refs])
    for k in range(count):
        at = slice(k * rows, (k + 1) * rows)
        keys[at, :] = blocks[k][...]
        turned_keys[:, at] = blocks[k][...].T
        grad[at, :] = jnp.concatenate([mass[:, at]] * repeats, axis=0).T
    total = jnp.sum(grad[...], axis=0, keepdims=True)
    grad[...] = prob_ref[...] - grad[...] / total
    key_total[...] = jnp.zeros_like(key_total)
    weight_total[...] = jnp.zeros_like(weight_total)
    all_heads = parts * heads
    for g in range(0, all_heads // repeats, 2):
        two = queries_ref[g * LANES : (g + 2) * LANES, :]
        act = lax.dot_general(
            keys[...], two, (((1,), (1,)), ((), ())), preferred_element_type=f32
        )
        coeffs = []
        for half in range(2):
            mine = act[:, half * LANES : (half + 1) * LANES]
            lean = grad[...]
            weight_total[g + half : g + half + 1, :] = jnp.sum(
                lean * jnp.maximum(mine, 0.0), axis=0, keepdims=True
            )
            coeffs.append(
                jnp.where(
                    mine > 0.0, lean * weights_ref[g + half : g + half + 1, :], 0.0
                ).astype(bf16)
            )
        coeffs = jnp.concatenate(coeffs, axis=1)
        key_total[...] += jnp.dot(coeffs, two, preferred_element_type=f32)
        found = jnp.dot(turned_keys[...], coeffs, preferred_element_type=f32)
        found = jnp.concatenate([found[:, :LANES].T, found[:, LANES:].T], axis=0)
        for i in range(2 * repeats):
            head = g * repeats + i
            first = (head // heads) * heads * share + head % heads
            query_total[pl.ds(first, share, stride=heads), :] = found[
                i * share : (i + 1) * share, :
            ]
    own = share * heads
    split = terms_of(weight_total[...], 2)
    for r in range(parts):
        messages[r][:own, :] = query_total[r * own : (r + 1) * own, :].astype(bf16)
        for i in range(2):
            messages[r][own + i * TAIL : own + (i + 1) * TAIL, :] = split[i]
    for i in range(count // 2):
        at = slice(i * rows, (i + 1) * rows)
        even_ref[at, :] = key_total[2 * i * rows : (2 * i + 1) * rows, :]
        odd_ref[at, :] = key_total[(2 * i + 1) * rows : (2 * i + 2) * rows, :]


def pair_kernel(mine_ref, other_ref, own_ref, *outs):
    rows = own_ref.shape[0]
    own_ref[...] = mine_ref[:rows, :] + other_ref[:rows, :]
    for i, out in enumerate(outs):
        at = slice((i + 1) * rows, (i + 2) * rows)
        out[...] = (mine_ref[at, :] + other_ref[at, :]).astype(out.dtype)


def sum_kernel(*refs):
    out_ref = refs[-1]
    out_ref[...] = tree([ref[...].astype(f32) for ref in refs[:-1]]).astype(out_ref.dtype)


def finish_kernel(share, heads, *refs):
    messages = refs[:-2]
    query_out, weight_out = refs[-2:]
    me = lax.axis_index("ha")
    own = share * heads
    total = jnp.zeros((heads, LANES), f32)
    lanes = lax.broadcasted_iota(jnp.int32, (heads, LANES), 1)
    for r, message in enumerate(messages):
        first = pl.multiple_of((me ^ r) * own, own)
        query_out[pl.ds(first, own), :] = message[:own, :]
        value = message[own : own + TAIL, :].astype(f32) + message[
            own + TAIL : own + 2 * TAIL, :
        ].astype(f32)
        rolled = {}
        found = []
        for j in range(heads):
            column = (r * heads + j) * share
            row, lane = column // LANES, column % LANES
            if lane not in rolled:
                rolled[lane] = pltpu.roll(value, LANES - lane, 1) if lane else value
            found.append(rolled[lane][row : row + 1, :])
        piece = jnp.where(lanes < share, jnp.concatenate(found, axis=0), 0.0)
        total = total + pltpu.roll(piece, (me ^ r) * share, 1)
    weight_out[...] = total


def on_device(main_query, latent, log_sums, window_start, index_query, index_key, index_weight):
    rows, head_count, width = main_query.shape
    heads, index_width = index_query.shape[1:]
    blocks = lax.axis_size("pb")
    parts = lax.axis_size("ha")
    share = rows // parts
    tokens = blocks * rows
    own = share * heads
    columns = share * heads * parts
    shape = jax.ShapeDtypeStruct

    def swap(value, axis, rel):
        size = lax.axis_size(axis)
        return lax.ppermute(value, axis, [(i, i ^ rel) for i in range(size)])

    start_row = window_start.reshape(1, rows)
    key_only = pl.BlockSpec((rows, index_width), lambda *_: (0, 0))

    packed = call(
        pack_kernel,
        shape((rows, index_width + width), bf16),
        (latent.T, index_key),
        cost=pl.CostEstimate(flops=0, bytes_accessed=1 << 24, transcendentals=0),
    )
    asked = call(
        ask_kernel,
        [shape((own + 3 * TAIL, index_width), bf16)] * parts,
        (index_query.reshape(rows * heads, index_width), index_weight.T),
    )
    queries = jnp.transpose(main_query, (1, 2, 0))
    sums = log_sums.T
    held = [None] * blocks
    held[0] = packed
    held[1] = swap(packed, "pb", 1)
    for k in range(2, blocks, 2):
        held[k] = swap(packed, "pb", k)
    ready = lax.optimization_barrier((asked[0], held[1]))
    asked = [ready[0]] + [swap(asked[r], "ha", r) for r in range(1, parts)]
    held[1] = ready[1]

    chunks = [[0, 1]] + [list(range(k, min(k + 4, blocks))) for k in range(2, blocks, 4)]
    mass = []
    for rels in chunks:
        last = rels is chunks[-1]
        span = len(rels) * rows
        outs = [shape((share, tokens), bf16)] * parts if last else [shape((rows, span), bf16)]
        before = mass if last else []
        values = [held[k] for k in rels] + [queries, sums, start_row] + before
        specs = [whole(v) for v in values]
        specs[len(rels)] = pl.BlockSpec(memory_space=pltpu.VMEM)
        found = call(
            functools.partial(main_kernel, rels, len(before)),
            outs,
            values,
            [
                pltpu.VMEM((span, width), bf16),
                pltpu.VMEM((span, rows), f32),
                pltpu.VMEM((rows, tokens if last else span), f32),
            ],
            specs,
            pl.CostEstimate(
                flops=2 * span * rows * head_count * width,
                bytes_accessed=2 * rows * head_count * width,
                transcendentals=span * rows * head_count,
            ),
        )
        mass = found if last else mass + found
        if rels is chunks[0]:
            even = list(range(2, blocks, 2))
            ready = lax.optimization_barrier((found[0], [held[k] for k in even]))
            mass = [ready[0]]
            for k, block in zip(even, ready[1]):
                held[k] = block
                held[k + 1] = swap(block, "pb", 1)
    first, key_block = lax.optimization_barrier((mass[0], held[0]))
    mass = [first] + [swap(mass[r], "ha", r) for r in range(1, parts)]
    key_blocks = [key_block] + held[1:]

    probs, query_rows, weight_rows = call(
        functools.partial(index_kernel, share, blocks, parts, heads),
        [
            shape((tokens, LANES), f32),
            shape((columns, index_width), bf16),
            shape((TAIL, LANES), f32),
        ],
        key_blocks + asked + [start_row],
        [
            pltpu.VMEM((tokens, index_width), bf16),
            pltpu.VMEM((own, index_width), f32),
            pltpu.VMEM((tokens, LANES), f32),
        ],
        [key_only] * blocks + [whole(v) for v in asked + [start_row]],
        pl.CostEstimate(
            flops=2 * tokens * columns * index_width,
            bytes_accessed=2 * columns * index_width,
            transcendentals=tokens * LANES,
        ),
    )

    even, odd, *answers = call(
        functools.partial(back_kernel, share, blocks, parts, heads),
        [shape((tokens // 2, index_width), f32)] * 2
        + [shape((own + 2 * TAIL, index_width), bf16)] * parts,
        mass + key_blocks + [probs, query_rows, weight_rows],
        [
            pltpu.VMEM((tokens, index_width), bf16),
            pltpu.VMEM((index_width, tokens), bf16),
            pltpu.VMEM((tokens, LANES), f32),
            pltpu.VMEM((tokens, index_width), f32),
            pltpu.VMEM((columns, index_width), f32),
            pltpu.VMEM((TAIL, LANES), f32),
        ],
        [whole(v) for v in mass]
        + [key_only] * blocks
        + [whole(v) for v in (probs, query_rows, weight_rows)],
        pl.CostEstimate(
            flops=6 * tokens * columns * index_width,
            bytes_accessed=2 * columns * index_width,
            transcendentals=0,
        ),
    )
    odd = swap(odd, "pb", 1)
    term = shape((rows, index_width), f32)
    half = shape((rows, index_width), bf16)
    mine, *others = call(pair_kernel, [term] + [half] * (blocks // 2 - 1), (even, odd))
    others = [swap(value, "pb", 2 * (i + 1)) for i, value in enumerate(others)]
    mine = call(sum_kernel, half, [mine] + others)
    key_grad = call(sum_kernel, half, [mine] + [swap(mine, "ha", r) for r in range(1, parts)])

    answers = [answers[0]] + [swap(answers[r], "ha", r) for r in range(1, parts)]
    query_grad, weight_grad = call(
        functools.partial(finish_kernel, share, heads),
        [shape((rows * heads, index_width), bf16), shape((heads, rows), f32)],
        answers,
    )
    return (query_grad.reshape(index_query.shape), key_grad, weight_grad.T)


def solution(mesh):
    return jax.shard_map(
        on_device,
        mesh=mesh,
        in_specs=(
            P("pb", "ha", None),
            P("pb", None),
            P("pb", "ha"),
            P("pb"),
            P("pb", "ha", None),
            P("pb", None),
            P("pb", "ha"),
        ),
        out_specs=(P("pb", "ha", None), P("pb", None), P("pb", "ha")),
        check_vma=False,
    )
```

```python
import functools

import jax
import jax.numpy as jnp
from jax import lax
from jax.experimental import pallas as pl
from jax.experimental.pallas import tpu as pltpu
from jax.sharding import PartitionSpec as P

main_scale = 192.0 ** (-0.5)
log2e = 1.4426950408889634
very_low = -1e30
LANES = 128
TAIL = 16
f32, bf16 = jnp.float32, jnp.bfloat16


def params(mega=24):
    return pltpu.CompilerParams(vmem_limit_bytes=mega * 1024 * 1024)


def whole(value):
    zeros = (0,) * len(value.shape)
    return pl.BlockSpec(value.shape, lambda *_: zeros)


def call(kernel, outs, values, scratch=(), specs=None, cost=None, mega=24):
    many = isinstance(outs, list)
    found = pl.pallas_call(
        kernel,
        grid=(1,),
        out_shape=outs,
        in_specs=specs or [whole(v) for v in values],
        out_specs=[whole(o) for o in outs] if many else whole(outs),
        scratch_shapes=list(scratch),
        compiler_params=params(mega),
        cost_estimate=cost,
    )(*values)
    return list(found) if many else found


def tree(values):
    while len(values) > 1:
        values = [values[i] + values[i + 1] for i in range(0, len(values), 2)]
    return values[0]


def terms_of(value, count):
    found = []
    for _ in range(count):
        term = value.astype(bf16)
        found.append(term)
        value = value - term.astype(f32)
    return found


def pack_kernel(latent_ref, key_ref, query_ref, weight_ref, packed_ref, *outs):
    width = key_ref.shape[1]
    packed_ref[:, :width] = key_ref[...]
    packed_ref[:, width:] = latent_ref[...].T
    me = lax.axis_index("ha")
    heads = weight_ref.shape[0]
    rows = outs[0].shape[0] - 3 * TAIL
    split = terms_of(weight_ref[...], 3)
    for r, out in enumerate(outs):
        first = pl.multiple_of((me ^ r) * rows, rows)
        out[:rows, :] = query_ref[pl.ds(first, rows), :]
        for i in range(3):
            at = rows + i * TAIL
            if heads < TAIL:
                out[at : at + TAIL, :] = jnp.zeros((TAIL, LANES), bf16)
            out[at : at + heads, :] = split[i]


def own_lanes(value, share):
    me = lax.axis_index("ha")
    value = pltpu.roll(value, lax.rem(LANES - me * share, LANES), 1)
    lanes = lax.broadcasted_iota(jnp.int32, value.shape, 1)
    value = jnp.where(lanes < share, value, jnp.zeros_like(value))
    shift = share
    while shift < LANES:
        value = value + pltpu.roll(value, shift, 1)
        shift *= 2
    return value


def main_kernel(rels, earlier, *refs):
    count = len(rels)
    blocks = refs[:count]
    query, sums_ref, start_ref = refs[count : count + 3]
    before = refs[count + 3 : count + 3 + earlier]
    outs = refs[count + 3 + earlier : -3]
    keys, total, turned = refs[-3:]
    heads, width, rows = query.shape
    for k in range(count):
        block = blocks[k][...]
        keys[k * rows : (k + 1) * rows, :] = block[:, block.shape[1] - width :]
    total[...] = jnp.zeros_like(total)

    for head in range(0, heads, 2):
        two = jnp.concatenate([query[head], query[head + 1]], axis=1)
        scores = jnp.dot(keys[...], two, preferred_element_type=f32)
        parts = [
            jnp.exp2(
                scores[:, half * rows : (half + 1) * rows] * (main_scale * log2e)
                - sums_ref[head + half : head + half + 1, :] * log2e
            )
            for half in range(2)
        ]
        total[...] += parts[0] + parts[1]

    me = lax.axis_index("pb")
    kept = turned.shape[1] - count * rows
    at = 0
    for ref in before:
        turned[:, at : at + ref.shape[1]] = ref[...].astype(f32)
        at += ref.shape[1]
    for k in range(count):
        key = (me ^ rels[k]) * rows + lax.broadcasted_iota(jnp.int32, (rows, rows), 0)
        mine = me * rows + lax.broadcasted_iota(jnp.int32, (rows, rows), 1)
        seen = (key >= start_ref[...]) & (key <= mine)
        piece = jnp.where(seen, total[k * rows : (k + 1) * rows, :], 0.0)
        turned[:, kept + k * rows : kept + (k + 1) * rows] = piece.T
    if len(outs) == 1:
        outs[0][...] = turned[...].astype(bf16)
    else:
        me = lax.axis_index("ha")
        share = outs[0].shape[0]
        for r, out in enumerate(outs):
            first = pl.multiple_of((me ^ r) * share, share)
            out[...] = turned[pl.ds(first, share), :].astype(bf16)


def index_kernel(share, count, parts, heads, *refs):
    blocks = refs[:count]
    messages = refs[count : count + parts]
    start_ref, prob_ref, queries_ref, weights_ref, keys, wide, total = refs[count + parts :]
    rows, width = blocks[0].shape
    for k in range(count):
        keys[k * rows : (k + 1) * rows, :] = blocks[k][...]
    own = share * heads
    repeats = LANES // share
    group = lax.broadcasted_iota(jnp.int32, (1, LANES), 1) // share
    row_of = []
    for r in range(parts):
        wide[...] = messages[r][:own, :].astype(f32)
        for j in range(heads):
            first = (r * heads + j) * share
            queries_ref[first : first + share, :] = wide[
                pl.ds(j, share, stride=heads), :
            ].astype(bf16)
        weight = tree_of_three(messages[r], own)
        weight = own_lanes(weight, share)
        row_of += [weight[j : j + 1, :] for j in range(heads)]
    weights_ref[...] = jnp.zeros_like(weights_ref)
    for g in range(len(row_of) // repeats):
        row = row_of[g * repeats]
        for i in range(1, repeats):
            row = jnp.where(group == i, row_of[g * repeats + i], row)
        weights_ref[g : g + 1, :] = row
    total[...] = jnp.zeros_like(total)
    for g in range(0, len(row_of) // repeats, 2):
        two = queries_ref[g * LANES : (g + 2) * LANES, :]
        act = lax.dot_general(
            keys[...], two, (((1,), (1,)), ((), ())), preferred_element_type=f32
        )
        act = jnp.maximum(act, 0.0)
        total[...] += (
            act[:, :LANES] * weights_ref[g : g + 1, :]
            + act[:, LANES:] * weights_ref[g + 1 : g + 2, :]
        )

    me = lax.axis_index("pb")
    lane = lax.broadcasted_iota(jnp.int32, (rows, LANES), 1) % share
    mine = me * rows + lax.axis_index("ha") * share + lane
    start = own_lanes(jnp.broadcast_to(start_ref[...], (8, LANES)), share)[:1, :]
    top = jnp.full((1, LANES), very_low, f32)
    masks = []
    for k in range(count):
        at = slice(k * rows, (k + 1) * rows)
        key = (me ^ k) * rows + lax.broadcasted_iota(jnp.int32, (rows, LANES), 0)
        seen = (key >= start) & (key <= mine)
        value = total[at, :]
        shift = share
        while shift < LANES:
            value = value + pltpu.roll(value, shift, 1)
            shift *= 2
        value = jnp.where(seen, value, very_low)
        total[at, :] = value
        top = jnp.maximum(top, jnp.max(value, axis=0, keepdims=True))
        masks.append(seen)
    mass = jnp.zeros((1, LANES), f32)
    for k in range(count):
        at = slice(k * rows, (k + 1) * rows)
        value = jnp.where(masks[k], jnp.exp(total[at, :] - top), 0.0)
        prob_ref[at, :] = value
        mass = mass + jnp.sum(value, axis=0, keepdims=True)
    prob_ref[...] = prob_ref[...] * (1.0 / mass)


def tree_of_three(ref, at):
    parts = [ref[at + i * TAIL : at + (i + 1) * TAIL, :].astype(f32) for i in range(3)]
    return parts[0] + (parts[1] + parts[2])


def back_kernel(share, count, parts, heads, *refs):
    mass_refs = refs[:parts]
    blocks = refs[parts : parts + count]
    prob_ref, queries_ref, weights_ref = refs[parts + count : parts + count + 3]
    outs = refs[parts + count + 3 : -6]
    even_ref, odd_ref = outs[:2]
    messages = outs[2:]
    keys, turned_keys, grad, key_total, query_total, weight_total = refs[-6:]
    rows, width = blocks[0].shape
    repeats = LANES // share
    mass = tree([ref[...].astype(f32) for ref in mass_refs])
    for k in range(count):
        at = slice(k * rows, (k + 1) * rows)
        keys[at, :] = blocks[k][...]
        turned_keys[:, at] = blocks[k][...].T
        grad[at, :] = jnp.concatenate([mass[:, at]] * repeats, axis=0).T
    total = jnp.sum(grad[...], axis=0, keepdims=True)
    grad[...] = prob_ref[...] - grad[...] / total
    key_total[...] = jnp.zeros_like(key_total)
    weight_total[...] = jnp.zeros_like(weight_total)
    all_heads = parts * heads
    for g in range(0, all_heads // repeats, 2):
        two = queries_ref[g * LANES : (g + 2) * LANES, :]
        act = lax.dot_general(
            keys[...], two, (((1,), (1,)), ((), ())), preferred_element_type=f32
        )
        coeffs = []
        for half in range(2):
            mine = act[:, half * LANES : (half + 1) * LANES]
            lean = grad[...]
            weight_total[g + half : g + half + 1, :] = jnp.sum(
                lean * jnp.maximum(mine, 0.0), axis=0, keepdims=True
            )
            coeffs.append(
                jnp.where(
                    mine > 0.0, lean * weights_ref[g + half : g + half + 1, :], 0.0
                ).astype(bf16)
            )
        coeffs = jnp.concatenate(coeffs, axis=1)
        key_total[...] += jnp.dot(coeffs, two, preferred_element_type=f32)
        found = jnp.dot(turned_keys[...], coeffs, preferred_element_type=f32)
        found = jnp.concatenate([found[:, :LANES].T, found[:, LANES:].T], axis=0)
        for i in range(2 * repeats):
            head = g * repeats + i
            first = (head // heads) * heads * share + head % heads
            query_total[pl.ds(first, share, stride=heads), :] = found[
                i * share : (i + 1) * share, :
            ]
    own = share * heads
    split = terms_of(weight_total[...], 2)
    for r in range(parts):
        messages[r][:own, :] = query_total[r * own : (r + 1) * own, :].astype(bf16)
        for i in range(2):
            messages[r][own + i * TAIL : own + (i + 1) * TAIL, :] = split[i]
    for i in range(count // 2):
        at = slice(i * rows, (i + 1) * rows)
        even_ref[at, :] = key_total[2 * i * rows : (2 * i + 1) * rows, :]
        odd_ref[at, :] = key_total[(2 * i + 1) * rows : (2 * i + 2) * rows, :]


def halve_kernel(*refs):
    mine_ref, other_ref, keep_ref = refs[:3]
    rows = LANES
    for i in range(mine_ref.shape[0] // rows):
        at = slice(i * rows, (i + 1) * rows)
        value = mine_ref[at, :].astype(f32) + other_ref[at, :].astype(f32)
        out = refs[3] if i % 2 else keep_ref
        to = slice(i // 2 * rows, (i // 2 + 1) * rows)
        out[to, :] = value.astype(out.dtype)


def finish_kernel(share, heads, *refs):
    messages = refs[:-2]
    query_out, weight_out = refs[-2:]
    me = lax.axis_index("ha")
    own = share * heads
    total = jnp.zeros((heads, LANES), f32)
    lanes = lax.broadcasted_iota(jnp.int32, (heads, LANES), 1)
    for r, message in enumerate(messages):
        first = pl.multiple_of((me ^ r) * own, own)
        query_out[pl.ds(first, own), :] = message[:own, :]
        value = message[own : own + TAIL, :].astype(f32) + message[
            own + TAIL : own + 2 * TAIL, :
        ].astype(f32)
        rolled = {}
        found = []
        for j in range(heads):
            column = (r * heads + j) * share
            row, lane = column // LANES, column % LANES
            if lane not in rolled:
                rolled[lane] = pltpu.roll(value, LANES - lane, 1) if lane else value
            found.append(rolled[lane][row : row + 1, :])
        piece = jnp.where(lanes < share, jnp.concatenate(found, axis=0), 0.0)
        total = total + pltpu.roll(piece, (me ^ r) * share, 1)
    weight_out[...] = total


def on_device(main_query, latent, log_sums, window_start, index_query, index_key, index_weight):
    rows, head_count, width = main_query.shape
    heads, index_width = index_query.shape[1:]
    blocks = lax.axis_size("pb")
    parts = lax.axis_size("ha")
    share = rows // parts
    tokens = blocks * rows
    own = share * heads
    columns = share * heads * parts
    shape = jax.ShapeDtypeStruct

    def swap(value, axis, rel):
        size = lax.axis_size(axis)
        return lax.ppermute(value, axis, [(i, i ^ rel) for i in range(size)])

    start_row = window_start.reshape(1, rows)
    key_only = pl.BlockSpec((rows, index_width), lambda *_: (0, 0))

    packed, *asked = call(
        pack_kernel,
        [shape((rows, index_width + width), bf16)]
        + [shape((own + 3 * TAIL, index_width), bf16)] * parts,
        (latent.T, index_key, index_query.reshape(rows * heads, index_width), index_weight.T),
        mega=64,
    )
    queries = jnp.transpose(main_query, (1, 2, 0))
    sums = log_sums.T
    held = [packed] + [None] * (blocks - 1)
    held[1] = swap(packed, "pb", 1)
    for k in range(2, blocks, 2):
        held[k] = swap(packed, "pb", k)
    asked[2] = swap(asked[2], "ha", 2)
    held[1], asked[1] = lax.optimization_barrier((held[1], asked[1]))
    asked[1] = swap(asked[1], "ha", 1)
    held[1], asked[1], asked[2:] = lax.optimization_barrier((held[1], asked[1], asked[2:]))
    asked[3:] = [swap(asked[r], "ha", r) for r in range(3, parts)]

    chunks = [[0, 1]] + [list(range(k, min(k + 4, blocks))) for k in range(2, blocks, 4)]
    mass = []
    for rels in chunks:
        last = rels is chunks[-1]
        span = len(rels) * rows
        outs = [shape((share, tokens), bf16)] * parts if last else [shape((rows, span), bf16)]
        before = mass if last else []
        values = [held[k] for k in rels] + [queries, sums, start_row] + before
        specs = [whole(v) for v in values]
        specs[len(rels)] = pl.BlockSpec(memory_space=pltpu.VMEM)
        found = call(
            functools.partial(main_kernel, rels, len(before)),
            outs,
            values,
            [
                pltpu.VMEM((span, width), bf16),
                pltpu.VMEM((span, rows), f32),
                pltpu.VMEM((rows, tokens if last else span), f32),
            ],
            specs,
            pl.CostEstimate(
                flops=2 * span * rows * head_count * width,
                bytes_accessed=2 * rows * head_count * width,
                transcendentals=span * rows * head_count,
            ),
        )
        mass = found if last else mass + found
        if rels is chunks[0]:
            even = list(range(2, blocks, 2))
            ready = lax.optimization_barrier((found[0], [held[k] for k in even]))
            mass = [ready[0]]
            for k, block in zip(even, ready[1]):
                held[k] = block
                held[k + 1] = swap(block, "pb", 1)
    first, key_block = lax.optimization_barrier((mass[0], held[0]))
    mass = [first] + [swap(mass[r], "ha", r) for r in range(1, parts)]
    key_blocks = [key_block] + held[1:]

    probs, query_rows, weight_rows = call(
        functools.partial(index_kernel, share, blocks, parts, heads),
        [
            shape((tokens, LANES), f32),
            shape((columns, index_width), bf16),
            shape((TAIL, LANES), f32),
        ],
        key_blocks + asked + [start_row],
        [
            pltpu.VMEM((tokens, index_width), bf16),
            pltpu.VMEM((own, index_width), f32),
            pltpu.VMEM((tokens, LANES), f32),
        ],
        [key_only] * blocks + [whole(v) for v in asked + [start_row]],
        pl.CostEstimate(
            flops=2 * tokens * columns * index_width,
            bytes_accessed=2 * columns * index_width,
            transcendentals=tokens * LANES,
        ),
    )

    even, odd, *answers = call(
        functools.partial(back_kernel, share, blocks, parts, heads),
        [shape((tokens // 2, index_width), f32)] * 2
        + [shape((own + 2 * TAIL, index_width), bf16)] * parts,
        mass + key_blocks + [probs, query_rows, weight_rows],
        [
            pltpu.VMEM((tokens, index_width), bf16),
            pltpu.VMEM((index_width, tokens), bf16),
            pltpu.VMEM((tokens, LANES), f32),
            pltpu.VMEM((tokens, index_width), f32),
            pltpu.VMEM((columns, index_width), f32),
            pltpu.VMEM((TAIL, LANES), f32),
        ],
        [whole(v) for v in mass]
        + [key_only] * blocks
        + [whole(v) for v in (probs, query_rows, weight_rows)],
        pl.CostEstimate(
            flops=6 * tokens * columns * index_width,
            bytes_accessed=2 * columns * index_width,
            transcendentals=0,
        ),
    )
    odd = swap(odd, "pb", 1)
    mine, other, rel = even, odd, 2
    while mine.shape[0] > rows:
        half = (mine.shape[0] // 2, index_width)
        mine, other = call(halve_kernel, [shape(half, f32), shape(half, bf16)], (mine, other))
        other = swap(other, "pb", rel)
        rel *= 2
    for r in [1 << i for i in range(parts.bit_length() - 1)]:
        mine = call(halve_kernel, shape((rows, index_width), bf16), (mine, other))
        other = swap(mine, "ha", r)
    key_grad = call(halve_kernel, shape((rows, index_width), bf16), (mine, other))

    answers = [answers[0]] + [swap(answers[r], "ha", r) for r in range(1, parts)]
    query_grad, weight_grad = call(
        functools.partial(finish_kernel, share, heads),
        [shape((rows * heads, index_width), bf16), shape((heads, rows), f32)],
        answers,
    )
    return (query_grad.reshape(index_query.shape), key_grad, weight_grad.T)


def solution(mesh):
    return jax.shard_map(
        on_device,
        mesh=mesh,
        in_specs=(
            P("pb", "ha", None),
            P("pb", None),
            P("pb", "ha"),
            P("pb"),
            P("pb", "ha", None),
            P("pb", None),
            P("pb", "ha"),
        ),
        out_specs=(P("pb", "ha", None), P("pb", None), P("pb", "ha")),
        check_vma=False,
    )
```

```python
import functools

import jax
import jax.numpy as jnp
from jax import lax
from jax.experimental import pallas as pl
from jax.experimental.pallas import tpu as pltpu
from jax.sharding import PartitionSpec as P

main_scale = 192.0 ** (-0.5)
log2e = 1.4426950408889634
very_low = -1e30
LANES = 128
TAIL = 16
f32, bf16 = jnp.float32, jnp.bfloat16


def params(mega=24):
    return pltpu.CompilerParams(vmem_limit_bytes=mega * 1024 * 1024)


def whole(value):
    zeros = (0,) * len(value.shape)
    return pl.BlockSpec(value.shape, lambda *_: zeros)


def call(kernel, outs, values, scratch=(), specs=None, cost=None, mega=24):
    many = isinstance(outs, list)
    found = pl.pallas_call(
        kernel,
        grid=(1,),
        out_shape=outs,
        in_specs=specs or [whole(v) for v in values],
        out_specs=[whole(o) for o in outs] if many else whole(outs),
        scratch_shapes=list(scratch),
        compiler_params=params(mega),
        cost_estimate=cost,
    )(*values)
    return list(found) if many else found


def tree(values):
    while len(values) > 1:
        values = [values[i] + values[i + 1] for i in range(0, len(values), 2)]
    return values[0]


def terms_of(value, count):
    found = []
    for _ in range(count):
        term = value.astype(bf16)
        found.append(term)
        value = value - term.astype(f32)
    return found


def pack_kernel(latent_ref, key_ref, query_ref, weight_ref, packed_ref, *outs):
    width = key_ref.shape[1]
    packed_ref[:, :width] = key_ref[...]
    packed_ref[:, width:] = latent_ref[...].T
    me = lax.axis_index("ha")
    heads = weight_ref.shape[0]
    rows = outs[0].shape[0] - 3 * TAIL
    split = terms_of(weight_ref[...], 3)
    for r, out in enumerate(outs):
        first = pl.multiple_of((me ^ r) * rows, rows)
        out[:rows, :] = query_ref[pl.ds(first, rows), :]
        for i in range(3):
            at = rows + i * TAIL
            if heads < TAIL:
                out[at : at + TAIL, :] = jnp.zeros((TAIL, LANES), bf16)
            out[at : at + heads, :] = split[i]


def own_lanes(value, share):
    me = lax.axis_index("ha")
    value = pltpu.roll(value, lax.rem(LANES - me * share, LANES), 1)
    lanes = lax.broadcasted_iota(jnp.int32, value.shape, 1)
    value = jnp.where(lanes < share, value, jnp.zeros_like(value))
    shift = share
    while shift < LANES:
        value = value + pltpu.roll(value, shift, 1)
        shift *= 2
    return value


def main_kernel(rels, earlier, *refs):
    count = len(rels)
    blocks = refs[:count]
    query, sums_ref, start_ref = refs[count : count + 3]
    before = refs[count + 3 : count + 3 + earlier]
    outs = refs[count + 3 + earlier : -3]
    keys, total, turned = refs[-3:]
    heads, width, rows = query.shape
    for k in range(count):
        block = blocks[k][...]
        keys[k * rows : (k + 1) * rows, :] = block[:, block.shape[1] - width :]
    total[...] = jnp.zeros_like(total)

    for head in range(0, heads, 2):
        two = jnp.concatenate([query[head], query[head + 1]], axis=1)
        scores = jnp.dot(keys[...], two, preferred_element_type=f32)
        parts = [
            jnp.exp2(
                scores[:, half * rows : (half + 1) * rows] * (main_scale * log2e)
                - sums_ref[head + half : head + half + 1, :] * log2e
            )
            for half in range(2)
        ]
        total[...] += parts[0] + parts[1]

    me = lax.axis_index("pb")
    kept = turned.shape[1] - count * rows
    at = 0
    for ref in before:
        turned[:, at : at + ref.shape[1]] = ref[...].astype(f32)
        at += ref.shape[1]
    for k in range(count):
        key = (me ^ rels[k]) * rows + lax.broadcasted_iota(jnp.int32, (rows, rows), 0)
        mine = me * rows + lax.broadcasted_iota(jnp.int32, (rows, rows), 1)
        seen = (key >= start_ref[...]) & (key <= mine)
        piece = jnp.where(seen, total[k * rows : (k + 1) * rows, :], 0.0)
        turned[:, kept + k * rows : kept + (k + 1) * rows] = piece.T
    if len(outs) == 1:
        outs[0][...] = turned[...].astype(bf16)
    else:
        me = lax.axis_index("ha")
        share = outs[0].shape[0]
        for r, out in enumerate(outs):
            first = pl.multiple_of((me ^ r) * share, share)
            out[...] = turned[pl.ds(first, share), :].astype(bf16)


def index_kernel(share, count, parts, heads, *refs):
    blocks = refs[:count]
    messages = refs[count : count + parts]
    start_ref, prob_ref, queries_ref, weights_ref, keys, wide, total = refs[count + parts :]
    rows, width = blocks[0].shape
    for k in range(count):
        keys[k * rows : (k + 1) * rows, :] = blocks[k][...]
    own = share * heads
    repeats = LANES // share
    group = lax.broadcasted_iota(jnp.int32, (1, LANES), 1) // share
    row_of = []
    for r in range(parts):
        wide[...] = messages[r][:own, :].astype(f32)
        for j in range(heads):
            first = (r * heads + j) * share
            queries_ref[first : first + share, :] = wide[
                pl.ds(j, share, stride=heads), :
            ].astype(bf16)
        weight = tree_of_three(messages[r], own)
        weight = own_lanes(weight, share)
        row_of += [weight[j : j + 1, :] for j in range(heads)]
    weights_ref[...] = jnp.zeros_like(weights_ref)
    for g in range(len(row_of) // repeats):
        row = row_of[g * repeats]
        for i in range(1, repeats):
            row = jnp.where(group == i, row_of[g * repeats + i], row)
        weights_ref[g : g + 1, :] = row
    total[...] = jnp.zeros_like(total)
    for g in range(0, len(row_of) // repeats, 2):
        two = queries_ref[g * LANES : (g + 2) * LANES, :]
        act = lax.dot_general(
            keys[...], two, (((1,), (1,)), ((), ())), preferred_element_type=f32
        )
        act = jnp.maximum(act, 0.0)
        total[...] += (
            act[:, :LANES] * weights_ref[g : g + 1, :]
            + act[:, LANES:] * weights_ref[g + 1 : g + 2, :]
        )

    me = lax.axis_index("pb")
    lane = lax.broadcasted_iota(jnp.int32, (rows, LANES), 1) % share
    mine = me * rows + lax.axis_index("ha") * share + lane
    start = own_lanes(jnp.broadcast_to(start_ref[...], (8, LANES)), share)[:1, :]
    top = jnp.full((1, LANES), very_low, f32)
    masks = []
    for k in range(count):
        at = slice(k * rows, (k + 1) * rows)
        key = (me ^ k) * rows + lax.broadcasted_iota(jnp.int32, (rows, LANES), 0)
        seen = (key >= start) & (key <= mine)
        value = total[at, :]
        shift = share
        while shift < LANES:
            value = value + pltpu.roll(value, shift, 1)
            shift *= 2
        value = jnp.where(seen, value, very_low)
        total[at, :] = value
        top = jnp.maximum(top, jnp.max(value, axis=0, keepdims=True))
        masks.append(seen)
    mass = jnp.zeros((1, LANES), f32)
    for k in range(count):
        at = slice(k * rows, (k + 1) * rows)
        value = jnp.where(masks[k], jnp.exp(total[at, :] - top), 0.0)
        prob_ref[at, :] = value
        mass = mass + jnp.sum(value, axis=0, keepdims=True)
    prob_ref[...] = prob_ref[...] * (1.0 / mass)


def tree_of_three(ref, at):
    parts = [ref[at + i * TAIL : at + (i + 1) * TAIL, :].astype(f32) for i in range(3)]
    return parts[0] + (parts[1] + parts[2])


def back_kernel(share, count, parts, heads, *refs):
    mass_refs = refs[:parts]
    blocks = refs[parts : parts + count]
    prob_ref, queries_ref, weights_ref = refs[parts + count : parts + count + 3]
    outs = refs[parts + count + 3 : -6]
    even_ref, odd_ref = outs[:2]
    messages = outs[2:]
    keys, turned_keys, grad, key_total, query_total, weight_total = refs[-6:]
    rows, width = blocks[0].shape
    repeats = LANES // share
    mass = tree([ref[...].astype(f32) for ref in mass_refs])
    for k in range(count):
        at = slice(k * rows, (k + 1) * rows)
        keys[at, :] = blocks[k][...]
        turned_keys[:, at] = blocks[k][...].T
        grad[at, :] = jnp.concatenate([mass[:, at]] * repeats, axis=0).T
    total = jnp.sum(grad[...], axis=0, keepdims=True)
    grad[...] = prob_ref[...] - grad[...] / total
    key_total[...] = jnp.zeros_like(key_total)
    weight_total[...] = jnp.zeros_like(weight_total)
    all_heads = parts * heads
    for g in range(0, all_heads // repeats, 2):
        two = queries_ref[g * LANES : (g + 2) * LANES, :]
        act = lax.dot_general(
            keys[...], two, (((1,), (1,)), ((), ())), preferred_element_type=f32
        )
        coeffs = []
        for half in range(2):
            mine = act[:, half * LANES : (half + 1) * LANES]
            lean = grad[...]
            weight_total[g + half : g + half + 1, :] = jnp.sum(
                lean * jnp.maximum(mine, 0.0), axis=0, keepdims=True
            )
            coeffs.append(
                jnp.where(
                    mine > 0.0, lean * weights_ref[g + half : g + half + 1, :], 0.0
                ).astype(bf16)
            )
        coeffs = jnp.concatenate(coeffs, axis=1)
        key_total[...] += jnp.dot(coeffs, two, preferred_element_type=f32)
        found = jnp.dot(turned_keys[...], coeffs, preferred_element_type=f32)
        found = jnp.concatenate([found[:, :LANES].T, found[:, LANES:].T], axis=0)
        for i in range(2 * repeats):
            head = g * repeats + i
            first = (head // heads) * heads * share + head % heads
            query_total[pl.ds(first, share, stride=heads), :] = found[
                i * share : (i + 1) * share, :
            ]
    own = share * heads
    split = terms_of(weight_total[...], 2)
    for r in range(parts):
        messages[r][:own, :] = query_total[r * own : (r + 1) * own, :].astype(bf16)
        for i in range(2):
            messages[r][own + i * TAIL : own + (i + 1) * TAIL, :] = split[i]
    for i in range(count // 2):
        at = slice(i * rows, (i + 1) * rows)
        even_ref[at, :] = key_total[2 * i * rows : (2 * i + 1) * rows, :]
        odd_ref[at, :] = key_total[(2 * i + 1) * rows : (2 * i + 2) * rows, :]


def halve_kernel(*refs):
    mine_ref, other_ref, keep_ref = refs[:3]
    rows = LANES
    for i in range(mine_ref.shape[0] // rows):
        at = slice(i * rows, (i + 1) * rows)
        value = mine_ref[at, :].astype(f32) + other_ref[at, :].astype(f32)
        out = refs[3] if i % 2 else keep_ref
        to = slice(i // 2 * rows, (i // 2 + 1) * rows)
        out[to, :] = value.astype(out.dtype)


def finish_kernel(share, heads, *refs):
    messages = refs[:-2]
    query_out, weight_out = refs[-2:]
    me = lax.axis_index("ha")
    own = share * heads
    total = jnp.zeros((heads, LANES), f32)
    lanes = lax.broadcasted_iota(jnp.int32, (heads, LANES), 1)
    for r, message in enumerate(messages):
        first = pl.multiple_of((me ^ r) * own, own)
        query_out[pl.ds(first, own), :] = message[:own, :]
        value = message[own : own + TAIL, :].astype(f32) + message[
            own + TAIL : own + 2 * TAIL, :
        ].astype(f32)
        rolled = {}
        found = []
        for j in range(heads):
            column = (r * heads + j) * share
            row, lane = column // LANES, column % LANES
            if lane not in rolled:
                rolled[lane] = pltpu.roll(value, LANES - lane, 1) if lane else value
            found.append(rolled[lane][row : row + 1, :])
        piece = jnp.where(lanes < share, jnp.concatenate(found, axis=0), 0.0)
        total = total + pltpu.roll(piece, (me ^ r) * share, 1)
    weight_out[...] = total


def on_device(main_query, latent, log_sums, window_start, index_query, index_key, index_weight):
    rows, head_count, width = main_query.shape
    heads, index_width = index_query.shape[1:]
    blocks = lax.axis_size("pb")
    parts = lax.axis_size("ha")
    share = rows // parts
    tokens = blocks * rows
    own = share * heads
    columns = share * heads * parts
    shape = jax.ShapeDtypeStruct

    def swap(value, axis, rel):
        size = lax.axis_size(axis)
        return lax.ppermute(value, axis, [(i, i ^ rel) for i in range(size)])

    start_row = window_start.reshape(1, rows)
    key_only = pl.BlockSpec((rows, index_width), lambda *_: (0, 0))

    packed, *asked = call(
        pack_kernel,
        [shape((rows, index_width + width), bf16)]
        + [shape((own + 3 * TAIL, index_width), bf16)] * parts,
        (latent.T, index_key, index_query.reshape(rows * heads, index_width), index_weight.T),
        mega=64,
    )
    queries = jnp.transpose(main_query, (1, 2, 0))
    sums = log_sums.T
    held = [packed] + [None] * (blocks - 1)
    held[1] = swap(packed, "pb", 1)
    held[2] = swap(packed, "pb", 2)
    asked = [asked[0]] + [swap(asked[r], "ha", r) for r in range(1, parts)]
    held[1], held[2], asked[1] = lax.optimization_barrier((held[1], held[2], asked[1]))
    for k in range(4, blocks, 2):
        top = 1 << (k.bit_length() - 1)
        held[k] = swap(held[k ^ top], "pb", top)
    for k in range(2, blocks, 2):
        held[k + 1] = swap(held[k], "pb", 1)

    chunks = [[0, 1]] + [list(range(k, min(k + 4, blocks))) for k in range(2, blocks, 4)]
    mass = []
    for rels in chunks:
        last = rels is chunks[-1]
        span = len(rels) * rows
        outs = [shape((share, tokens), bf16)] * parts if last else [shape((rows, span), bf16)]
        before = mass if last else []
        values = [held[k] for k in rels] + [queries, sums, start_row] + before
        specs = [whole(v) for v in values]
        specs[len(rels)] = pl.BlockSpec(memory_space=pltpu.VMEM)
        found = call(
            functools.partial(main_kernel, rels, len(before)),
            outs,
            values,
            [
                pltpu.VMEM((span, width), bf16),
                pltpu.VMEM((span, rows), f32),
                pltpu.VMEM((rows, tokens if last else span), f32),
            ],
            specs,
            pl.CostEstimate(
                flops=2 * span * rows * head_count * width,
                bytes_accessed=2 * rows * head_count * width,
                transcendentals=span * rows * head_count,
            ),
        )
        mass = found if last else mass + found
    first, key_block = lax.optimization_barrier((mass[0], held[0]))
    mass = [first] + [swap(mass[r], "ha", r) for r in range(1, parts)]
    key_blocks = [key_block] + held[1:]

    probs, query_rows, weight_rows = call(
        functools.partial(index_kernel, share, blocks, parts, heads),
        [
            shape((tokens, LANES), f32),
            shape((columns, index_width), bf16),
            shape((TAIL, LANES), f32),
        ],
        key_blocks + asked + [start_row],
        [
            pltpu.VMEM((tokens, index_width), bf16),
            pltpu.VMEM((own, index_width), f32),
            pltpu.VMEM((tokens, LANES), f32),
        ],
        [key_only] * blocks + [whole(v) for v in asked + [start_row]],
        pl.CostEstimate(
            flops=2 * tokens * columns * index_width,
            bytes_accessed=2 * columns * index_width,
            transcendentals=tokens * LANES,
        ),
    )

    even, odd, *answers = call(
        functools.partial(back_kernel, share, blocks, parts, heads),
        [shape((tokens // 2, index_width), f32)] * 2
        + [shape((own + 2 * TAIL, index_width), bf16)] * parts,
        mass + key_blocks + [probs, query_rows, weight_rows],
        [
            pltpu.VMEM((tokens, index_width), bf16),
            pltpu.VMEM((index_width, tokens), bf16),
            pltpu.VMEM((tokens, LANES), f32),
            pltpu.VMEM((tokens, index_width), f32),
            pltpu.VMEM((columns, index_width), f32),
            pltpu.VMEM((TAIL, LANES), f32),
        ],
        [whole(v) for v in mass]
        + [key_only] * blocks
        + [whole(v) for v in (probs, query_rows, weight_rows)],
        pl.CostEstimate(
            flops=6 * tokens * columns * index_width,
            bytes_accessed=2 * columns * index_width,
            transcendentals=0,
        ),
    )
    odd = swap(odd, "pb", 1)
    answers = [answers[0]] + [swap(answers[r], "ha", r) for r in range(1, parts)]
    odd, answers[1] = lax.optimization_barrier((odd, answers[1]))
    mine, other, rel = even, odd, 2
    while mine.shape[0] > rows:
        half = (mine.shape[0] // 2, index_width)
        mine, other = call(halve_kernel, [shape(half, f32), shape(half, bf16)], (mine, other))
        other = swap(other, "pb", rel)
        rel *= 2
    for r in [1 << i for i in range(parts.bit_length() - 1)]:
        mine = call(halve_kernel, shape((rows, index_width), bf16), (mine, other))
        other = swap(mine, "ha", r)
    key_grad = call(halve_kernel, shape((rows, index_width), bf16), (mine, other))

    query_grad, weight_grad = call(
        functools.partial(finish_kernel, share, heads),
        [shape((rows * heads, index_width), bf16), shape((heads, rows), f32)],
        answers,
    )
    return (query_grad.reshape(index_query.shape), key_grad, weight_grad.T)


def solution(mesh):
    return jax.shard_map(
        on_device,
        mesh=mesh,
        in_specs=(
            P("pb", "ha", None),
            P("pb", None),
            P("pb", "ha"),
            P("pb"),
            P("pb", "ha", None),
            P("pb", None),
            P("pb", "ha"),
        ),
        out_specs=(P("pb", "ha", None), P("pb", None), P("pb", "ha")),
        check_vma=False,
    )
```

```python
import functools

import jax
import jax.numpy as jnp
from jax import lax
from jax.experimental import pallas as pl
from jax.experimental.pallas import tpu as pltpu
from jax.sharding import PartitionSpec as P

main_scale = 192.0 ** (-0.5)
log2e = 1.4426950408889634
very_low = -1e30
LANES = 128
TAIL = 16
f32, bf16 = jnp.float32, jnp.bfloat16


def params():
    return pltpu.CompilerParams(vmem_limit_bytes=24 * 1024 * 1024)


def whole(value):
    zeros = (0,) * len(value.shape)
    return pl.BlockSpec(value.shape, lambda *_: zeros)


def call(kernel, outs, values, scratch=(), specs=None, cost=None):
    many = isinstance(outs, list)
    found = pl.pallas_call(
        kernel,
        grid=(1,),
        out_shape=outs,
        in_specs=specs or [whole(v) for v in values],
        out_specs=[whole(o) for o in outs] if many else whole(outs),
        scratch_shapes=list(scratch),
        compiler_params=params(),
        cost_estimate=cost,
    )(*values)
    return list(found) if many else found


def tree(values):
    while len(values) > 1:
        values = [values[i] + values[i + 1] for i in range(0, len(values), 2)]
    return values[0]


def terms_of(value, count):
    found = []
    for _ in range(count):
        term = value.astype(bf16)
        found.append(term)
        value = value - term.astype(f32)
    return found


def pack_kernel(latent_ref, key_ref, packed_ref):
    width = key_ref.shape[1]
    packed_ref[:, :width] = key_ref[...]
    packed_ref[:, width:] = latent_ref[...].T


def ask_kernel(query_ref, weight_ref, *outs):
    me = lax.axis_index("ha")
    heads = weight_ref.shape[0]
    rows = outs[0].shape[0] - 3 * TAIL
    split = terms_of(weight_ref[...], 3)
    for r, out in enumerate(outs):
        first = pl.multiple_of((me ^ r) * rows, rows)
        out[:rows, :] = query_ref[pl.ds(first, rows), :]
        for i in range(3):
            at = rows + i * TAIL
            if heads < TAIL:
                out[at : at + TAIL, :] = jnp.zeros((TAIL, LANES), bf16)
            out[at : at + heads, :] = split[i]


def own_lanes(value, share):
    me = lax.axis_index("ha")
    value = pltpu.roll(value, lax.rem(LANES - me * share, LANES), 1)
    lanes = lax.broadcasted_iota(jnp.int32, value.shape, 1)
    value = jnp.where(lanes < share, value, jnp.zeros_like(value))
    shift = share
    while shift < LANES:
        value = value + pltpu.roll(value, shift, 1)
        shift *= 2
    return value


def main_kernel(rels, earlier, *refs):
    count = len(rels)
    blocks = refs[:count]
    query, sums_ref, start_ref = refs[count : count + 3]
    before = refs[count + 3 : count + 3 + earlier]
    outs = refs[count + 3 + earlier : -3]
    keys, total, turned = refs[-3:]
    heads, width, rows = query.shape
    for k in range(count):
        block = blocks[k][...]
        keys[k * rows : (k + 1) * rows, :] = block[:, block.shape[1] - width :]
    total[...] = jnp.zeros_like(total)

    for head in range(0, heads, 2):
        two = jnp.concatenate([query[head], query[head + 1]], axis=1)
        scores = jnp.dot(keys[...], two, preferred_element_type=f32)
        parts = [
            jnp.exp2(
                scores[:, half * rows : (half + 1) * rows] * (main_scale * log2e)
                - sums_ref[head + half : head + half + 1, :] * log2e
            )
            for half in range(2)
        ]
        total[...] += parts[0] + parts[1]

    me = lax.axis_index("pb")
    kept = turned.shape[1] - count * rows
    at = 0
    for ref in before:
        turned[:, at : at + ref.shape[1]] = ref[...].astype(f32)
        at += ref.shape[1]
    for k in range(count):
        key = (me ^ rels[k]) * rows + lax.broadcasted_iota(jnp.int32, (rows, rows), 0)
        mine = me * rows + lax.broadcasted_iota(jnp.int32, (rows, rows), 1)
        seen = (key >= start_ref[...]) & (key <= mine)
        piece = jnp.where(seen, total[k * rows : (k + 1) * rows, :], 0.0)
        turned[:, kept + k * rows : kept + (k + 1) * rows] = piece.T
    if len(outs) == 1:
        outs[0][...] = turned[...].astype(bf16)
    else:
        me = lax.axis_index("ha")
        share = outs[0].shape[0]
        for r, out in enumerate(outs):
            first = pl.multiple_of((me ^ r) * share, share)
            out[...] = turned[pl.ds(first, share), :].astype(bf16)


def index_kernel(share, count, parts, heads, *refs):
    blocks = refs[:count]
    messages = refs[count : count + parts]
    start_ref, prob_ref, queries_ref, weights_ref, keys, wide, total = refs[count + parts :]
    rows, width = blocks[0].shape
    for k in range(count):
        keys[k * rows : (k + 1) * rows, :] = blocks[k][...]
    own = share * heads
    repeats = LANES // share
    group = lax.broadcasted_iota(jnp.int32, (1, LANES), 1) // share
    row_of = []
    for r in range(parts):
        wide[...] = messages[r][:own, :].astype(f32)
        for j in range(heads):
            first = (r * heads + j) * share
            queries_ref[first : first + share, :] = wide[
                pl.ds(j, share, stride=heads), :
            ].astype(bf16)
        weight = tree_of_three(messages[r], own)
        weight = own_lanes(weight, share)
        row_of += [weight[j : j + 1, :] for j in range(heads)]
    weights_ref[...] = jnp.zeros_like(weights_ref)
    for g in range(len(row_of) // repeats):
        row = row_of[g * repeats]
        for i in range(1, repeats):
            row = jnp.where(group == i, row_of[g * repeats + i], row)
        weights_ref[g : g + 1, :] = row
    total[...] = jnp.zeros_like(total)
    for g in range(0, len(row_of) // repeats, 2):
        two = queries_ref[g * LANES : (g + 2) * LANES, :]
        act = lax.dot_general(
            keys[...], two, (((1,), (1,)), ((), ())), preferred_element_type=f32
        )
        act = jnp.maximum(act, 0.0)
        total[...] += (
            act[:, :LANES] * weights_ref[g : g + 1, :]
            + act[:, LANES:] * weights_ref[g + 1 : g + 2, :]
        )

    me = lax.axis_index("pb")
    lane = lax.broadcasted_iota(jnp.int32, (rows, LANES), 1) % share
    mine = me * rows + lax.axis_index("ha") * share + lane
    start = own_lanes(jnp.broadcast_to(start_ref[...], (8, LANES)), share)[:1, :]
    top = jnp.full((1, LANES), very_low, f32)
    masks = []
    for k in range(count):
        at = slice(k * rows, (k + 1) * rows)
        key = (me ^ k) * rows + lax.broadcasted_iota(jnp.int32, (rows, LANES), 0)
        seen = (key >= start) & (key <= mine)
        value = total[at, :]
        shift = share
        while shift < LANES:
            value = value + pltpu.roll(value, shift, 1)
            shift *= 2
        value = jnp.where(seen, value, very_low)
        total[at, :] = value
        top = jnp.maximum(top, jnp.max(value, axis=0, keepdims=True))
        masks.append(seen)
    mass = jnp.zeros((1, LANES), f32)
    for k in range(count):
        at = slice(k * rows, (k + 1) * rows)
        value = jnp.where(masks[k], jnp.exp(total[at, :] - top), 0.0)
        prob_ref[at, :] = value
        mass = mass + jnp.sum(value, axis=0, keepdims=True)
    prob_ref[...] = prob_ref[...] * (1.0 / mass)


def tree_of_three(ref, at):
    parts = [ref[at + i * TAIL : at + (i + 1) * TAIL, :].astype(f32) for i in range(3)]
    return parts[0] + (parts[1] + parts[2])


def back_kernel(share, count, parts, heads, *refs):
    mass_refs = refs[:parts]
    blocks = refs[parts : parts + count]
    prob_ref, queries_ref, weights_ref = refs[parts + count : parts + count + 3]
    outs = refs[parts + count + 3 : -6]
    even_ref, odd_ref = outs[:2]
    messages = outs[2:]
    keys, turned_keys, grad, key_total, query_total, weight_total = refs[-6:]
    rows, width = blocks[0].shape
    repeats = LANES // share
    mass = tree([ref[...].astype(f32) for ref in mass_refs])
    for k in range(count):
        at = slice(k * rows, (k + 1) * rows)
        keys[at, :] = blocks[k][...]
        turned_keys[:, at] = blocks[k][...].T
        grad[at, :] = jnp.concatenate([mass[:, at]] * repeats, axis=0).T
    total = jnp.sum(grad[...], axis=0, keepdims=True)
    grad[...] = prob_ref[...] - grad[...] / total
    key_total[...] = jnp.zeros_like(key_total)
    weight_total[...] = jnp.zeros_like(weight_total)
    all_heads = parts * heads
    for g in range(0, all_heads // repeats, 2):
        two = queries_ref[g * LANES : (g + 2) * LANES, :]
        act = lax.dot_general(
            keys[...], two, (((1,), (1,)), ((), ())), preferred_element_type=f32
        )
        coeffs = []
        for half in range(2):
            mine = act[:, half * LANES : (half + 1) * LANES]
            lean = grad[...]
            weight_total[g + half : g + half + 1, :] = jnp.sum(
                lean * jnp.maximum(mine, 0.0), axis=0, keepdims=True
            )
            coeffs.append(
                jnp.where(
                    mine > 0.0, lean * weights_ref[g + half : g + half + 1, :], 0.0
                ).astype(bf16)
            )
        coeffs = jnp.concatenate(coeffs, axis=1)
        key_total[...] += jnp.dot(coeffs, two, preferred_element_type=f32)
        found = jnp.dot(turned_keys[...], coeffs, preferred_element_type=f32)
        found = jnp.concatenate([found[:, :LANES].T, found[:, LANES:].T], axis=0)
        for i in range(2 * repeats):
            head = g * repeats + i
            first = (head // heads) * heads * share + head % heads
            query_total[pl.ds(first, share, stride=heads), :] = found[
                i * share : (i + 1) * share, :
            ]
    own = share * heads
    split = terms_of(weight_total[...], 2)
    for r in range(parts):
        messages[r][:own, :] = query_total[r * own : (r + 1) * own, :].astype(bf16)
        for i in range(2):
            messages[r][own + i * TAIL : own + (i + 1) * TAIL, :] = split[i]
    for i in range(count // 2):
        at = slice(i * rows, (i + 1) * rows)
        even_ref[at, :] = key_total[2 * i * rows : (2 * i + 1) * rows, :]
        odd_ref[at, :] = key_total[(2 * i + 1) * rows : (2 * i + 2) * rows, :]


def halve_kernel(*refs):
    mine_ref, other_ref, keep_ref = refs[:3]
    rows = LANES
    for i in range(mine_ref.shape[0] // rows):
        at = slice(i * rows, (i + 1) * rows)
        value = mine_ref[at, :].astype(f32) + other_ref[at, :].astype(f32)
        out = refs[3] if i % 2 else keep_ref
        to = slice(i // 2 * rows, (i // 2 + 1) * rows)
        out[to, :] = value.astype(out.dtype)


def finish_kernel(share, heads, *refs):
    messages = refs[:-2]
    query_out, weight_out = refs[-2:]
    me = lax.axis_index("ha")
    own = share * heads
    total = jnp.zeros((heads, LANES), f32)
    lanes = lax.broadcasted_iota(jnp.int32, (heads, LANES), 1)
    for r, message in enumerate(messages):
        first = pl.multiple_of((me ^ r) * own, own)
        query_out[pl.ds(first, own), :] = message[:own, :]
        value = message[own : own + TAIL, :].astype(f32) + message[
            own + TAIL : own + 2 * TAIL, :
        ].astype(f32)
        rolled = {}
        found = []
        for j in range(heads):
            column = (r * heads + j) * share
            row, lane = column // LANES, column % LANES
            if lane not in rolled:
                rolled[lane] = pltpu.roll(value, LANES - lane, 1) if lane else value
            found.append(rolled[lane][row : row + 1, :])
        piece = jnp.where(lanes < share, jnp.concatenate(found, axis=0), 0.0)
        total = total + pltpu.roll(piece, (me ^ r) * share, 1)
    weight_out[...] = total


def on_device(main_query, latent, log_sums, window_start, index_query, index_key, index_weight):
    rows, head_count, width = main_query.shape
    heads, index_width = index_query.shape[1:]
    blocks = lax.axis_size("pb")
    parts = lax.axis_size("ha")
    share = rows // parts
    tokens = blocks * rows
    own = share * heads
    columns = share * heads * parts
    shape = jax.ShapeDtypeStruct

    def swap(value, axis, rel):
        size = lax.axis_size(axis)
        return lax.ppermute(value, axis, [(i, i ^ rel) for i in range(size)])

    start_row = window_start.reshape(1, rows)
    key_only = pl.BlockSpec((rows, index_width), lambda *_: (0, 0))

    packed = call(
        pack_kernel,
        shape((rows, index_width + width), bf16),
        (latent.T, index_key),
        cost=pl.CostEstimate(flops=0, bytes_accessed=1 << 24, transcendentals=0),
    )
    asked = call(
        ask_kernel,
        [shape((own + 3 * TAIL, index_width), bf16)] * parts,
        (index_query.reshape(rows * heads, index_width), index_weight.T),
    )
    queries = jnp.transpose(main_query, (1, 2, 0))
    sums = log_sums.T
    held = [None] * blocks
    held[0] = packed
    held[1] = swap(packed, "pb", 1)
    for k in range(2, blocks, 2):
        held[k] = swap(packed, "pb", k)
    ready = lax.optimization_barrier((asked[0], held[1]))
    asked = [ready[0]] + [swap(asked[r], "ha", r) for r in range(1, parts)]
    held[1] = ready[1]

    chunks = [[0, 1]] + [list(range(k, min(k + 4, blocks))) for k in range(2, blocks, 4)]
    mass = []
    for rels in chunks:
        last = rels is chunks[-1]
        span = len(rels) * rows
        outs = [shape((share, tokens), bf16)] * parts if last else [shape((rows, span), bf16)]
        before = mass if last else []
        values = [held[k] for k in rels] + [queries, sums, start_row] + before
        specs = [whole(v) for v in values]
        specs[len(rels)] = pl.BlockSpec(memory_space=pltpu.VMEM)
        found = call(
            functools.partial(main_kernel, rels, len(before)),
            outs,
            values,
            [
                pltpu.VMEM((span, width), bf16),
                pltpu.VMEM((span, rows), f32),
                pltpu.VMEM((rows, tokens if last else span), f32),
            ],
            specs,
            pl.CostEstimate(
                flops=2 * span * rows * head_count * width,
                bytes_accessed=2 * rows * head_count * width,
                transcendentals=span * rows * head_count,
            ),
        )
        mass = found if last else mass + found
        if rels is chunks[0]:
            even = list(range(2, blocks, 2))
            ready = lax.optimization_barrier((found[0], [held[k] for k in even]))
            mass = [ready[0]]
            for k, block in zip(even, ready[1]):
                held[k] = block
                held[k + 1] = swap(block, "pb", 1)
    first, key_block = lax.optimization_barrier((mass[0], held[0]))
    mass = [first] + [swap(mass[r], "ha", r) for r in range(1, parts)]
    key_blocks = [key_block] + held[1:]

    probs, query_rows, weight_rows = call(
        functools.partial(index_kernel, share, blocks, parts, heads),
        [
            shape((tokens, LANES), f32),
            shape((columns, index_width), bf16),
            shape((TAIL, LANES), f32),
        ],
        key_blocks + asked + [start_row],
        [
            pltpu.VMEM((tokens, index_width), bf16),
            pltpu.VMEM((own, index_width), f32),
            pltpu.VMEM((tokens, LANES), f32),
        ],
        [key_only] * blocks + [whole(v) for v in asked + [start_row]],
        pl.CostEstimate(
            flops=2 * tokens * columns * index_width,
            bytes_accessed=2 * columns * index_width,
            transcendentals=tokens * LANES,
        ),
    )

    even, odd, *answers = call(
        functools.partial(back_kernel, share, blocks, parts, heads),
        [shape((tokens // 2, index_width), f32)] * 2
        + [shape((own + 2 * TAIL, index_width), bf16)] * parts,
        mass + key_blocks + [probs, query_rows, weight_rows],
        [
            pltpu.VMEM((tokens, index_width), bf16),
            pltpu.VMEM((index_width, tokens), bf16),
            pltpu.VMEM((tokens, LANES), f32),
            pltpu.VMEM((tokens, index_width), f32),
            pltpu.VMEM((columns, index_width), f32),
            pltpu.VMEM((TAIL, LANES), f32),
        ],
        [whole(v) for v in mass]
        + [key_only] * blocks
        + [whole(v) for v in (probs, query_rows, weight_rows)],
        pl.CostEstimate(
            flops=6 * tokens * columns * index_width,
            bytes_accessed=2 * columns * index_width,
            transcendentals=0,
        ),
    )
    odd = swap(odd, "pb", 1)
    answers = [answers[0]] + [swap(answers[r], "ha", r) for r in range(1, parts)]
    mine, other, rel = even, odd, 2
    while mine.shape[0] > rows:
        half = (mine.shape[0] // 2, index_width)
        mine, other = call(halve_kernel, [shape(half, f32), shape(half, bf16)], (mine, other))
        other = swap(other, "pb", rel)
        rel *= 2
    other, answers = lax.optimization_barrier((other, answers))
    for r in [1 << i for i in range(parts.bit_length() - 1)]:
        mine = call(halve_kernel, shape((rows, index_width), bf16), (mine, other))
        other = swap(mine, "ha", r)
    key_grad = call(halve_kernel, shape((rows, index_width), bf16), (mine, other))

    query_grad, weight_grad = call(
        functools.partial(finish_kernel, share, heads),
        [shape((rows * heads, index_width), bf16), shape((heads, rows), f32)],
        answers,
    )
    return (query_grad.reshape(index_query.shape), key_grad, weight_grad.T)


def solution(mesh):
    return jax.shard_map(
        on_device,
        mesh=mesh,
        in_specs=(
            P("pb", "ha", None),
            P("pb", None),
            P("pb", "ha"),
            P("pb"),
            P("pb", "ha", None),
            P("pb", None),
            P("pb", "ha"),
        ),
        out_specs=(P("pb", "ha", None), P("pb", None), P("pb", "ha")),
        check_vma=False,
    )
```

```python
import functools

import jax
import jax.numpy as jnp
from jax import lax
from jax.experimental import pallas as pl
from jax.experimental.pallas import tpu as pltpu
from jax.sharding import PartitionSpec as P

main_scale = 192.0 ** (-0.5)
log2e = 1.4426950408889634
very_low = -1e30
LANES = 128
FILL = 10
TAIL = 16
f32, bf16 = jnp.float32, jnp.bfloat16


def params():
    return pltpu.CompilerParams(vmem_limit_bytes=24 * 1024 * 1024)


def whole(value):
    zeros = (0,) * len(value.shape)
    return pl.BlockSpec(value.shape, lambda *_: zeros)


def call(kernel, outs, values, scratch=(), specs=None, cost=None):
    many = isinstance(outs, list)
    found = pl.pallas_call(
        kernel,
        grid=(1,),
        out_shape=outs,
        in_specs=specs or [whole(v) for v in values],
        out_specs=[whole(o) for o in outs] if many else whole(outs),
        scratch_shapes=list(scratch),
        compiler_params=params(),
        cost_estimate=cost,
    )(*values)
    return list(found) if many else found


def tree(values):
    while len(values) > 1:
        values = [values[i] + values[i + 1] for i in range(0, len(values), 2)]
    return values[0]


def terms_of(value, count):
    found = []
    for _ in range(count):
        term = value.astype(bf16)
        found.append(term)
        value = value - term.astype(f32)
    return found


def pack_kernel(latent_ref, key_ref, packed_ref):
    width = key_ref.shape[1]
    packed_ref[:, :width] = key_ref[...]
    packed_ref[:, width:] = latent_ref[...].T


def ask_kernel(query_ref, weight_ref, *outs):
    me = lax.axis_index("ha")
    heads = weight_ref.shape[0]
    rows = outs[0].shape[0] - 3 * TAIL
    split = terms_of(weight_ref[...], 3)
    for r, out in enumerate(outs):
        first = pl.multiple_of((me ^ r) * rows, rows)
        out[:rows, :] = query_ref[pl.ds(first, rows), :]
        for i in range(3):
            at = rows + i * TAIL
            if heads < TAIL:
                out[at : at + TAIL, :] = jnp.zeros((TAIL, LANES), bf16)
            out[at : at + heads, :] = split[i]


def own_lanes(value, share):
    me = lax.axis_index("ha")
    value = pltpu.roll(value, lax.rem(LANES - me * share, LANES), 1)
    lanes = lax.broadcasted_iota(jnp.int32, value.shape, 1)
    value = jnp.where(lanes < share, value, jnp.zeros_like(value))
    shift = share
    while shift < LANES:
        value = value + pltpu.roll(value, shift, 1)
        shift *= 2
    return value


def main_kernel(rels, earlier, *refs):
    count = len(rels)
    blocks = refs[:count]
    query, sums_ref, start_ref = refs[count : count + 3]
    before = refs[count + 3 : count + 3 + earlier]
    outs = refs[count + 3 + earlier : -3]
    keys, total, turned = refs[-3:]
    heads, width, rows = query.shape
    for k in range(count):
        block = blocks[k][...]
        keys[k * rows : (k + 1) * rows, :] = block[:, block.shape[1] - width :]
    total[...] = jnp.zeros_like(total)

    for head in range(0, heads, 2):
        two = jnp.concatenate([query[head], query[head + 1]], axis=1)
        scores = jnp.dot(keys[...], two, preferred_element_type=f32)
        parts = [
            jnp.exp2(
                scores[:, half * rows : (half + 1) * rows] * (main_scale * log2e)
                - sums_ref[head + half : head + half + 1, :] * log2e
            )
            for half in range(2)
        ]
        total[...] += parts[0] + parts[1]

    me = lax.axis_index("pb")
    kept = turned.shape[1] - count * rows
    at = 0
    for ref in before:
        turned[:, at : at + ref.shape[1]] = ref[...].astype(f32)
        at += ref.shape[1]
    for k in range(count):
        key = (me ^ rels[k]) * rows + lax.broadcasted_iota(jnp.int32, (rows, rows), 0)
        mine = me * rows + lax.broadcasted_iota(jnp.int32, (rows, rows), 1)
        seen = (key >= start_ref[...]) & (key <= mine)
        piece = jnp.where(seen, total[k * rows : (k + 1) * rows, :], 0.0)
        turned[:, kept + k * rows : kept + (k + 1) * rows] = piece.T
    if len(outs) == 1:
        outs[0][...] = turned[...].astype(bf16)
    else:
        me = lax.axis_index("ha")
        share = outs[0].shape[0]
        for r, out in enumerate(outs):
            first = pl.multiple_of((me ^ r) * share, share)
            out[...] = turned[pl.ds(first, share), :].astype(bf16)


def index_kernel(share, count, parts, heads, *refs):
    blocks = refs[:count]
    messages = refs[count : count + parts]
    start_ref, prob_ref, queries_ref, weights_ref, keys, wide, total = refs[count + parts :]
    rows, width = blocks[0].shape
    for k in range(count):
        keys[k * rows : (k + 1) * rows, :] = blocks[k][...]
    own = share * heads
    repeats = LANES // share
    group = lax.broadcasted_iota(jnp.int32, (1, LANES), 1) // share
    row_of = []
    for r in range(parts):
        wide[...] = messages[r][:own, :].astype(f32)
        for j in range(heads):
            first = (r * heads + j) * share
            queries_ref[first : first + share, :] = wide[
                pl.ds(j, share, stride=heads), :
            ].astype(bf16)
        weight = tree_of_three(messages[r], own)
        weight = own_lanes(weight, share)
        row_of += [weight[j : j + 1, :] for j in range(heads)]
    weights_ref[...] = jnp.zeros_like(weights_ref)
    for g in range(len(row_of) // repeats):
        row = row_of[g * repeats]
        for i in range(1, repeats):
            row = jnp.where(group == i, row_of[g * repeats + i], row)
        weights_ref[g : g + 1, :] = row
    total[...] = jnp.zeros_like(total)
    for g in range(0, len(row_of) // repeats, 2):
        two = queries_ref[g * LANES : (g + 2) * LANES, :]
        act = lax.dot_general(
            keys[...], two, (((1,), (1,)), ((), ())), preferred_element_type=f32
        )
        act = jnp.maximum(act, 0.0)
        total[...] += (
            act[:, :LANES] * weights_ref[g : g + 1, :]
            + act[:, LANES:] * weights_ref[g + 1 : g + 2, :]
        )

    me = lax.axis_index("pb")
    lane = lax.broadcasted_iota(jnp.int32, (rows, LANES), 1) % share
    mine = me * rows + lax.axis_index("ha") * share + lane
    start = own_lanes(jnp.broadcast_to(start_ref[...], (8, LANES)), share)[:1, :]
    top = jnp.full((1, LANES), very_low, f32)
    masks = []
    for k in range(count):
        at = slice(k * rows, (k + 1) * rows)
        key = (me ^ k) * rows + lax.broadcasted_iota(jnp.int32, (rows, LANES), 0)
        seen = (key >= start) & (key <= mine)
        value = total[at, :]
        shift = share
        while shift < LANES:
            value = value + pltpu.roll(value, shift, 1)
            shift *= 2
        value = jnp.where(seen, value, very_low)
        total[at, :] = value
        top = jnp.maximum(top, jnp.max(value, axis=0, keepdims=True))
        masks.append(seen)
    mass = jnp.zeros((1, LANES), f32)
    for k in range(count):
        at = slice(k * rows, (k + 1) * rows)
        value = jnp.where(masks[k], jnp.exp(total[at, :] - top), 0.0)
        prob_ref[at, :] = value
        mass = mass + jnp.sum(value, axis=0, keepdims=True)
    prob_ref[...] = prob_ref[...] * (1.0 / mass)


def tree_of_three(ref, at):
    parts = [ref[at + i * TAIL : at + (i + 1) * TAIL, :].astype(f32) for i in range(3)]
    return parts[0] + (parts[1] + parts[2])


def back_kernel(share, count, parts, heads, *refs):
    mass_refs = refs[:parts]
    blocks = refs[parts : parts + count]
    prob_ref, queries_ref, weights_ref = refs[parts + count : parts + count + 3]
    outs = refs[parts + count + 3 : -6]
    even_ref, odd_ref = outs[:2]
    messages = outs[2:]
    keys, turned_keys, grad, key_total, query_total, weight_total = refs[-6:]
    rows, width = blocks[0].shape
    repeats = LANES // share
    mass = tree([ref[...].astype(f32) for ref in mass_refs])
    for k in range(count):
        at = slice(k * rows, (k + 1) * rows)
        keys[at, :] = blocks[k][...]
        turned_keys[:, at] = blocks[k][...].T
        grad[at, :] = jnp.concatenate([mass[:, at]] * repeats, axis=0).T
    total = jnp.sum(grad[...], axis=0, keepdims=True)
    grad[...] = prob_ref[...] - grad[...] / total
    key_total[...] = jnp.zeros_like(key_total)
    weight_total[...] = jnp.zeros_like(weight_total)
    all_heads = parts * heads
    for g in range(0, all_heads // repeats, 2):
        two = queries_ref[g * LANES : (g + 2) * LANES, :]
        act = lax.dot_general(
            keys[...], two, (((1,), (1,)), ((), ())), preferred_element_type=f32
        )
        coeffs = []
        for half in range(2):
            mine = act[:, half * LANES : (half + 1) * LANES]
            lean = grad[...]
            weight_total[g + half : g + half + 1, :] = jnp.sum(
                lean * jnp.maximum(mine, 0.0), axis=0, keepdims=True
            )
            coeffs.append(
                jnp.where(
                    mine > 0.0, lean * weights_ref[g + half : g + half + 1, :], 0.0
                ).astype(bf16)
            )
        coeffs = jnp.concatenate(coeffs, axis=1)
        key_total[...] += jnp.dot(coeffs, two, preferred_element_type=f32)
        found = jnp.dot(turned_keys[...], coeffs, preferred_element_type=f32)
        found = jnp.concatenate([found[:, :LANES].T, found[:, LANES:].T], axis=0)
        for i in range(2 * repeats):
            head = g * repeats + i
            first = (head // heads) * heads * share + head % heads
            query_total[pl.ds(first, share, stride=heads), :] = found[
                i * share : (i + 1) * share, :
            ]
    own = share * heads
    split = terms_of(weight_total[...], 2)
    for r in range(parts):
        messages[r][:own, :] = query_total[r * own : (r + 1) * own, :].astype(bf16)
        for i in range(2):
            messages[r][own + i * TAIL : own + (i + 1) * TAIL, :] = split[i]
    for i in range(count // 2):
        at = slice(i * rows, (i + 1) * rows)
        even_ref[at, :] = key_total[2 * i * rows : (2 * i + 1) * rows, :]
        odd_ref[at, :] = key_total[(2 * i + 1) * rows : (2 * i + 2) * rows, :]


def pair_kernel(mine_ref, other_ref, own_ref, *outs):
    rows = own_ref.shape[0]
    own_ref[...] = mine_ref[:rows, :] + other_ref[:rows, :]
    for i, out in enumerate(outs):
        at = slice((i + 1) * rows, (i + 2) * rows)
        out[...] = (mine_ref[at, :] + other_ref[at, :]).astype(out.dtype)


def sum_kernel(*refs):
    out_ref = refs[-1]
    out_ref[...] = tree([ref[...].astype(f32) for ref in refs[:-1]]).astype(out_ref.dtype)


def finish_kernel(share, heads, *refs):
    messages = refs[:-2]
    query_out, weight_out = refs[-2:]
    me = lax.axis_index("ha")
    own = share * heads
    total = jnp.zeros((heads, LANES), f32)
    lanes = lax.broadcasted_iota(jnp.int32, (heads, LANES), 1)
    for r, message in enumerate(messages):
        first = pl.multiple_of((me ^ r) * own, own)
        query_out[pl.ds(first, own), :] = message[:own, :]
        value = message[own : own + TAIL, :].astype(f32) + message[
            own + TAIL : own + 2 * TAIL, :
        ].astype(f32)
        rolled = {}
        found = []
        for j in range(heads):
            column = (r * heads + j) * share
            row, lane = column // LANES, column % LANES
            if lane not in rolled:
                rolled[lane] = pltpu.roll(value, LANES - lane, 1) if lane else value
            found.append(rolled[lane][row : row + 1, :])
        piece = jnp.where(lanes < share, jnp.concatenate(found, axis=0), 0.0)
        total = total + pltpu.roll(piece, (me ^ r) * share, 1)
    weight_out[...] = total


def on_device(main_query, latent, log_sums, window_start, index_query, index_key, index_weight):
    rows, head_count, width = main_query.shape
    heads, index_width = index_query.shape[1:]
    blocks = lax.axis_size("pb")
    parts = lax.axis_size("ha")
    share = rows // parts
    tokens = blocks * rows
    own = share * heads
    columns = share * heads * parts
    shape = jax.ShapeDtypeStruct

    def swap(value, axis, rel):
        size = lax.axis_size(axis)
        return lax.ppermute(value, axis, [(i, i ^ rel) for i in range(size)])

    start_row = window_start.reshape(1, rows)
    key_only = pl.BlockSpec((rows, index_width), lambda *_: (0, 0))

    packed = call(
        pack_kernel,
        shape((rows, index_width + width), bf16),
        (latent.T, index_key),
        cost=pl.CostEstimate(flops=0, bytes_accessed=1 << 24, transcendentals=0),
    )
    asked = call(
        ask_kernel,
        [shape((own + 3 * TAIL, index_width), bf16)] * parts,
        (index_query.reshape(rows * heads, index_width), index_weight.T),
    )
    queries = jnp.transpose(main_query, (1, 2, 0))
    sums = log_sums.T
    held = [None] * blocks
    held[0] = packed
    held[1] = swap(packed, "pb", 1)
    for k in range(2, blocks, 2):
        held[k] = swap(packed, "pb", k)
    ready = lax.optimization_barrier((asked[0], held[1]))
    asked = [ready[0]] + [swap(asked[r], "ha", r) for r in range(1, parts)]
    held[1] = ready[1]

    chunks = [[0, 1]] + [list(range(k, min(k + 4, blocks))) for k in range(2, blocks, 4)]
    mass = []
    for rels in chunks:
        last = rels is chunks[-1]
        span = len(rels) * rows
        outs = [shape((share, tokens), bf16)] * parts if last else [shape((rows, span), bf16)]
        before = mass if last else []
        values = [held[k] for k in rels] + [queries, sums, start_row] + before
        specs = [whole(v) for v in values]
        specs[len(rels)] = pl.BlockSpec(memory_space=pltpu.VMEM)
        found = call(
            functools.partial(main_kernel, rels, len(before)),
            outs,
            values,
            [
                pltpu.VMEM((span, width), bf16),
                pltpu.VMEM((span, rows), f32),
                pltpu.VMEM((rows, tokens if last else span), f32),
            ],
            specs,
            pl.CostEstimate(
                flops=2 * span * rows * head_count * width * (FILL if rels is chunks[0] else 1),
                bytes_accessed=2 * rows * head_count * width,
                transcendentals=span * rows * head_count,
            ),
        )
        mass = found if last else mass + found
        if rels is chunks[0]:
            even = list(range(2, blocks, 2))
            ready = lax.optimization_barrier((found[0], [held[k] for k in even], asked[1:3]))
            mass = [ready[0]]
            asked[1:3] = ready[2]
            for k, block in zip(even, ready[1]):
                held[k] = block
                held[k + 1] = swap(block, "pb", 1)
    first, key_block = lax.optimization_barrier((mass[0], held[0]))
    mass = [first] + [swap(mass[r], "ha", r) for r in range(1, parts)]
    key_blocks = [key_block] + held[1:]

    probs, query_rows, weight_rows = call(
        functools.partial(index_kernel, share, blocks, parts, heads),
        [
            shape((tokens, LANES), f32),
            shape((columns, index_width), bf16),
            shape((TAIL, LANES), f32),
        ],
        key_blocks + asked + [start_row],
        [
            pltpu.VMEM((tokens, index_width), bf16),
            pltpu.VMEM((own, index_width), f32),
            pltpu.VMEM((tokens, LANES), f32),
        ],
        [key_only] * blocks + [whole(v) for v in asked + [start_row]],
        pl.CostEstimate(
            flops=2 * tokens * columns * index_width,
            bytes_accessed=2 * columns * index_width,
            transcendentals=tokens * LANES,
        ),
    )

    even, odd, *answers = call(
        functools.partial(back_kernel, share, blocks, parts, heads),
        [shape((tokens // 2, index_width), f32)] * 2
        + [shape((own + 2 * TAIL, index_width), bf16)] * parts,
        mass + key_blocks + [probs, query_rows, weight_rows],
        [
            pltpu.VMEM((tokens, index_width), bf16),
            pltpu.VMEM((index_width, tokens), bf16),
            pltpu.VMEM((tokens, LANES), f32),
            pltpu.VMEM((tokens, index_width), f32),
            pltpu.VMEM((columns, index_width), f32),
            pltpu.VMEM((TAIL, LANES), f32),
        ],
        [whole(v) for v in mass]
        + [key_only] * blocks
        + [whole(v) for v in (probs, query_rows, weight_rows)],
        pl.CostEstimate(
            flops=6 * tokens * columns * index_width,
            bytes_accessed=2 * columns * index_width,
            transcendentals=0,
        ),
    )
    odd = swap(odd, "pb", 1)
    term = shape((rows, index_width), f32)
    half = shape((rows, index_width), bf16)
    mine, *others = call(pair_kernel, [term] + [half] * (blocks // 2 - 1), (even, odd))
    answers = [answers[0]] + [swap(answers[r], "ha", r) for r in range(1, parts)]
    for i, value in enumerate(others):
        if i == len(others) - 1:
            value, answers[1] = lax.optimization_barrier((value, answers[1]))
        others[i] = swap(value, "pb", 2 * (i + 1))
    mine = call(sum_kernel, half, [mine] + others)
    key_grad = call(sum_kernel, half, [mine] + [swap(mine, "ha", r) for r in range(1, parts)])

    query_grad, weight_grad = call(
        functools.partial(finish_kernel, share, heads),
        [shape((rows * heads, index_width), bf16), shape((heads, rows), f32)],
        answers,
    )
    return (query_grad.reshape(index_query.shape), key_grad, weight_grad.T)


def solution(mesh):
    return jax.shard_map(
        on_device,
        mesh=mesh,
        in_specs=(
            P("pb", "ha", None),
            P("pb", None),
            P("pb", "ha"),
            P("pb"),
            P("pb", "ha", None),
            P("pb", None),
            P("pb", "ha"),
        ),
        out_specs=(P("pb", "ha", None), P("pb", None), P("pb", "ha")),
        check_vma=False,
    )
```

```python
import functools

import jax
import jax.numpy as jnp
from jax import lax
from jax.experimental import pallas as pl
from jax.experimental.pallas import tpu as pltpu
from jax.sharding import PartitionSpec as P

main_scale = 192.0 ** (-0.5)
log2e = 1.4426950408889634
very_low = -1e30
LANES = 128
FILL = 10
TAIL = 16
f32, bf16 = jnp.float32, jnp.bfloat16


def params():
    return pltpu.CompilerParams(vmem_limit_bytes=24 * 1024 * 1024)


def whole(value):
    zeros = (0,) * len(value.shape)
    return pl.BlockSpec(value.shape, lambda *_: zeros)


def call(kernel, outs, values, scratch=(), specs=None, cost=None):
    many = isinstance(outs, list)
    found = pl.pallas_call(
        kernel,
        grid=(1,),
        out_shape=outs,
        in_specs=specs or [whole(v) for v in values],
        out_specs=[whole(o) for o in outs] if many else whole(outs),
        scratch_shapes=list(scratch),
        compiler_params=params(),
        cost_estimate=cost,
    )(*values)
    return list(found) if many else found


def tree(values):
    while len(values) > 1:
        values = [values[i] + values[i + 1] for i in range(0, len(values), 2)]
    return values[0]


def terms_of(value, count):
    found = []
    for _ in range(count):
        term = value.astype(bf16)
        found.append(term)
        value = value - term.astype(f32)
    return found


def pack_kernel(latent_ref, key_ref, packed_ref):
    width = key_ref.shape[1]
    packed_ref[:, :width] = key_ref[...]
    packed_ref[:, width:] = latent_ref[...].T


def ask_kernel(query_ref, weight_ref, *outs):
    me = lax.axis_index("ha")
    heads = weight_ref.shape[0]
    rows = outs[0].shape[0] - 3 * TAIL
    split = terms_of(weight_ref[...], 3)
    for r, out in enumerate(outs):
        first = pl.multiple_of((me ^ r) * rows, rows)
        out[:rows, :] = query_ref[pl.ds(first, rows), :]
        for i in range(3):
            at = rows + i * TAIL
            if heads < TAIL:
                out[at : at + TAIL, :] = jnp.zeros((TAIL, LANES), bf16)
            out[at : at + heads, :] = split[i]


def own_lanes(value, share):
    me = lax.axis_index("ha")
    value = pltpu.roll(value, lax.rem(LANES - me * share, LANES), 1)
    lanes = lax.broadcasted_iota(jnp.int32, value.shape, 1)
    value = jnp.where(lanes < share, value, jnp.zeros_like(value))
    shift = share
    while shift < LANES:
        value = value + pltpu.roll(value, shift, 1)
        shift *= 2
    return value


def main_kernel(rels, earlier, *refs):
    count = len(rels)
    blocks = refs[:count]
    query, sums_ref, start_ref = refs[count : count + 3]
    before = refs[count + 3 : count + 3 + earlier]
    outs = refs[count + 3 + earlier : -3]
    keys, total, turned = refs[-3:]
    heads, width, rows = query.shape
    for k in range(count):
        block = blocks[k][...]
        keys[k * rows : (k + 1) * rows, :] = block[:, block.shape[1] - width :]
    total[...] = jnp.zeros_like(total)

    for head in range(0, heads, 2):
        two = jnp.concatenate([query[head], query[head + 1]], axis=1)
        scores = jnp.dot(keys[...], two, preferred_element_type=f32)
        parts = [
            jnp.exp2(
                scores[:, half * rows : (half + 1) * rows] * (main_scale * log2e)
                - sums_ref[head + half : head + half + 1, :] * log2e
            )
            for half in range(2)
        ]
        total[...] += parts[0] + parts[1]

    me = lax.axis_index("pb")
    kept = turned.shape[1] - count * rows
    at = 0
    for ref in before:
        turned[:, at : at + ref.shape[1]] = ref[...].astype(f32)
        at += ref.shape[1]
    for k in range(count):
        key = (me ^ rels[k]) * rows + lax.broadcasted_iota(jnp.int32, (rows, rows), 0)
        mine = me * rows + lax.broadcasted_iota(jnp.int32, (rows, rows), 1)
        seen = (key >= start_ref[...]) & (key <= mine)
        piece = jnp.where(seen, total[k * rows : (k + 1) * rows, :], 0.0)
        turned[:, kept + k * rows : kept + (k + 1) * rows] = piece.T
    if len(outs) == 1:
        outs[0][...] = turned[...].astype(bf16)
    else:
        me = lax.axis_index("ha")
        share = outs[0].shape[0]
        for r, out in enumerate(outs):
            first = pl.multiple_of((me ^ r) * share, share)
            out[...] = turned[pl.ds(first, share), :].astype(bf16)


def index_kernel(share, count, parts, heads, *refs):
    blocks = refs[:count]
    messages = refs[count : count + parts]
    start_ref, prob_ref, queries_ref, weights_ref, keys, wide, total = refs[count + parts :]
    rows, width = blocks[0].shape
    for k in range(count):
        keys[k * rows : (k + 1) * rows, :] = blocks[k][...]
    own = share * heads
    repeats = LANES // share
    group = lax.broadcasted_iota(jnp.int32, (1, LANES), 1) // share
    row_of = []
    for r in range(parts):
        wide[...] = messages[r][:own, :].astype(f32)
        for j in range(heads):
            first = (r * heads + j) * share
            queries_ref[first : first + share, :] = wide[
                pl.ds(j, share, stride=heads), :
            ].astype(bf16)
        weight = tree_of_three(messages[r], own)
        weight = own_lanes(weight, share)
        row_of += [weight[j : j + 1, :] for j in range(heads)]
    weights_ref[...] = jnp.zeros_like(weights_ref)
    for g in range(len(row_of) // repeats):
        row = row_of[g * repeats]
        for i in range(1, repeats):
            row = jnp.where(group == i, row_of[g * repeats + i], row)
        weights_ref[g : g + 1, :] = row
    total[...] = jnp.zeros_like(total)
    for g in range(0, len(row_of) // repeats, 2):
        two = queries_ref[g * LANES : (g + 2) * LANES, :]
        act = lax.dot_general(
            keys[...], two, (((1,), (1,)), ((), ())), preferred_element_type=f32
        )
        act = jnp.maximum(act, 0.0)
        total[...] += (
            act[:, :LANES] * weights_ref[g : g + 1, :]
            + act[:, LANES:] * weights_ref[g + 1 : g + 2, :]
        )

    me = lax.axis_index("pb")
    lane = lax.broadcasted_iota(jnp.int32, (rows, LANES), 1) % share
    mine = me * rows + lax.axis_index("ha") * share + lane
    start = own_lanes(jnp.broadcast_to(start_ref[...], (8, LANES)), share)[:1, :]
    top = jnp.full((1, LANES), very_low, f32)
    masks = []
    for k in range(count):
        at = slice(k * rows, (k + 1) * rows)
        key = (me ^ k) * rows + lax.broadcasted_iota(jnp.int32, (rows, LANES), 0)
        seen = (key >= start) & (key <= mine)
        value = total[at, :]
        shift = share
        while shift < LANES:
            value = value + pltpu.roll(value, shift, 1)
            shift *= 2
        value = jnp.where(seen, value, very_low)
        total[at, :] = value
        top = jnp.maximum(top, jnp.max(value, axis=0, keepdims=True))
        masks.append(seen)
    mass = jnp.zeros((1, LANES), f32)
    for k in range(count):
        at = slice(k * rows, (k + 1) * rows)
        value = jnp.where(masks[k], jnp.exp(total[at, :] - top), 0.0)
        prob_ref[at, :] = value
        mass = mass + jnp.sum(value, axis=0, keepdims=True)
    prob_ref[...] = prob_ref[...] * (1.0 / mass)


def tree_of_three(ref, at):
    parts = [ref[at + i * TAIL : at + (i + 1) * TAIL, :].astype(f32) for i in range(3)]
    return parts[0] + (parts[1] + parts[2])


def back_kernel(share, count, parts, heads, *refs):
    mass_refs = refs[:parts]
    blocks = refs[parts : parts + count]
    prob_ref, queries_ref, weights_ref = refs[parts + count : parts + count + 3]
    outs = refs[parts + count + 3 : -6]
    even_ref, odd_ref = outs[:2]
    messages = outs[2:]
    keys, turned_keys, grad, key_total, query_total, weight_total = refs[-6:]
    rows, width = blocks[0].shape
    repeats = LANES // share
    mass = tree([ref[...].astype(f32) for ref in mass_refs])
    for k in range(count):
        at = slice(k * rows, (k + 1) * rows)
        keys[at, :] = blocks[k][...]
        turned_keys[:, at] = blocks[k][...].T
        grad[at, :] = jnp.concatenate([mass[:, at]] * repeats, axis=0).T
    total = jnp.sum(grad[...], axis=0, keepdims=True)
    grad[...] = prob_ref[...] - grad[...] / total
    key_total[...] = jnp.zeros_like(key_total)
    weight_total[...] = jnp.zeros_like(weight_total)
    all_heads = parts * heads
    for g in range(0, all_heads // repeats, 2):
        two = queries_ref[g * LANES : (g + 2) * LANES, :]
        act = lax.dot_general(
            keys[...], two, (((1,), (1,)), ((), ())), preferred_element_type=f32
        )
        coeffs = []
        for half in range(2):
            mine = act[:, half * LANES : (half + 1) * LANES]
            lean = grad[...]
            weight_total[g + half : g + half + 1, :] = jnp.sum(
                lean * jnp.maximum(mine, 0.0), axis=0, keepdims=True
            )
            coeffs.append(
                jnp.where(
                    mine > 0.0, lean * weights_ref[g + half : g + half + 1, :], 0.0
                ).astype(bf16)
            )
        coeffs = jnp.concatenate(coeffs, axis=1)
        key_total[...] += jnp.dot(coeffs, two, preferred_element_type=f32)
        found = jnp.dot(turned_keys[...], coeffs, preferred_element_type=f32)
        found = jnp.concatenate([found[:, :LANES].T, found[:, LANES:].T], axis=0)
        for i in range(2 * repeats):
            head = g * repeats + i
            first = (head // heads) * heads * share + head % heads
            query_total[pl.ds(first, share, stride=heads), :] = found[
                i * share : (i + 1) * share, :
            ]
    own = share * heads
    split = terms_of(weight_total[...], 2)
    for r in range(parts):
        messages[r][:own, :] = query_total[r * own : (r + 1) * own, :].astype(bf16)
        for i in range(2):
            messages[r][own + i * TAIL : own + (i + 1) * TAIL, :] = split[i]
    for i in range(count // 2):
        at = slice(i * rows, (i + 1) * rows)
        even_ref[at, :] = key_total[2 * i * rows : (2 * i + 1) * rows, :]
        odd_ref[at, :] = key_total[(2 * i + 1) * rows : (2 * i + 2) * rows, :]


def pair_kernel(mine_ref, other_ref, own_ref, *outs):
    rows = own_ref.shape[0]
    own_ref[...] = mine_ref[:rows, :] + other_ref[:rows, :]
    for i, out in enumerate(outs):
        at = slice((i + 1) * rows, (i + 2) * rows)
        out[...] = (mine_ref[at, :] + other_ref[at, :]).astype(out.dtype)


def sum_kernel(*refs):
    out_ref = refs[-1]
    out_ref[...] = tree([ref[...].astype(f32) for ref in refs[:-1]]).astype(out_ref.dtype)


def finish_kernel(share, heads, *refs):
    messages = refs[:-2]
    query_out, weight_out = refs[-2:]
    me = lax.axis_index("ha")
    own = share * heads
    total = jnp.zeros((heads, LANES), f32)
    lanes = lax.broadcasted_iota(jnp.int32, (heads, LANES), 1)
    for r, message in enumerate(messages):
        first = pl.multiple_of((me ^ r) * own, own)
        query_out[pl.ds(first, own), :] = message[:own, :]
        value = message[own : own + TAIL, :].astype(f32) + message[
            own + TAIL : own + 2 * TAIL, :
        ].astype(f32)
        rolled = {}
        found = []
        for j in range(heads):
            column = (r * heads + j) * share
            row, lane = column // LANES, column % LANES
            if lane not in rolled:
                rolled[lane] = pltpu.roll(value, LANES - lane, 1) if lane else value
            found.append(rolled[lane][row : row + 1, :])
        piece = jnp.where(lanes < share, jnp.concatenate(found, axis=0), 0.0)
        total = total + pltpu.roll(piece, (me ^ r) * share, 1)
    weight_out[...] = total


def on_device(main_query, latent, log_sums, window_start, index_query, index_key, index_weight):
    rows, head_count, width = main_query.shape
    heads, index_width = index_query.shape[1:]
    blocks = lax.axis_size("pb")
    parts = lax.axis_size("ha")
    share = rows // parts
    tokens = blocks * rows
    own = share * heads
    columns = share * heads * parts
    shape = jax.ShapeDtypeStruct

    def swap(value, axis, rel):
        size = lax.axis_size(axis)
        return lax.ppermute(value, axis, [(i, i ^ rel) for i in range(size)])

    start_row = window_start.reshape(1, rows)
    key_only = pl.BlockSpec((rows, index_width), lambda *_: (0, 0))

    packed = call(
        pack_kernel,
        shape((rows, index_width + width), bf16),
        (latent.T, index_key),
        cost=pl.CostEstimate(flops=0, bytes_accessed=1 << 24, transcendentals=0),
    )
    asked = call(
        ask_kernel,
        [shape((own + 3 * TAIL, index_width), bf16)] * parts,
        (index_query.reshape(rows * heads, index_width), index_weight.T),
    )
    queries = jnp.transpose(main_query, (1, 2, 0))
    sums = log_sums.T
    held = [None] * blocks
    held[0] = packed
    held[1] = swap(packed, "pb", 1)
    for k in range(2, blocks, 2):
        held[k] = swap(packed, "pb", k)
    ready = lax.optimization_barrier((asked[0], held[1]))
    asked = [ready[0]] + [swap(asked[r], "ha", r) for r in range(1, parts)]
    held[1] = ready[1]

    chunks = [[0, 1]] + [list(range(k, min(k + 4, blocks))) for k in range(2, blocks, 4)]
    mass = []
    for rels in chunks:
        last = rels is chunks[-1]
        span = len(rels) * rows
        outs = [shape((share, tokens), bf16)] * parts if last else [shape((rows, span), bf16)]
        before = mass if last else []
        values = [held[k] for k in rels] + [queries, sums, start_row] + before
        specs = [whole(v) for v in values]
        specs[len(rels)] = pl.BlockSpec(memory_space=pltpu.VMEM)
        found = call(
            functools.partial(main_kernel, rels, len(before)),
            outs,
            values,
            [
                pltpu.VMEM((span, width), bf16),
                pltpu.VMEM((span, rows), f32),
                pltpu.VMEM((rows, tokens if last else span), f32),
            ],
            specs,
            pl.CostEstimate(
                flops=2 * span * rows * head_count * width * (FILL if rels is chunks[0] else 1),
                bytes_accessed=2 * rows * head_count * width,
                transcendentals=span * rows * head_count,
            ),
        )
        mass = found if last else mass + found
        if rels is chunks[0]:
            even = list(range(2, blocks, 2))
            ready = lax.optimization_barrier((found[0], [held[k] for k in even], asked[1:3]))
            mass = [ready[0]]
            asked[1:3] = ready[2]
            for k, block in zip(even, ready[1]):
                held[k] = block
                held[k + 1] = swap(block, "pb", 1)
    first, key_block = lax.optimization_barrier((mass[0], held[0]))
    mass = [first] + [swap(mass[r], "ha", r) for r in range(1, parts)]
    key_blocks = [key_block] + held[1:]

    probs, query_rows, weight_rows = call(
        functools.partial(index_kernel, share, blocks, parts, heads),
        [
            shape((tokens, LANES), f32),
            shape((columns, index_width), bf16),
            shape((TAIL, LANES), f32),
        ],
        key_blocks + asked + [start_row],
        [
            pltpu.VMEM((tokens, index_width), bf16),
            pltpu.VMEM((own, index_width), f32),
            pltpu.VMEM((tokens, LANES), f32),
        ],
        [key_only] * blocks + [whole(v) for v in asked + [start_row]],
        pl.CostEstimate(
            flops=2 * tokens * columns * index_width,
            bytes_accessed=2 * columns * index_width,
            transcendentals=tokens * LANES,
        ),
    )

    even, odd, *answers = call(
        functools.partial(back_kernel, share, blocks, parts, heads),
        [shape((tokens // 2, index_width), f32)] * 2
        + [shape((own + 2 * TAIL, index_width), bf16)] * parts,
        mass + key_blocks + [probs, query_rows, weight_rows],
        [
            pltpu.VMEM((tokens, index_width), bf16),
            pltpu.VMEM((index_width, tokens), bf16),
            pltpu.VMEM((tokens, LANES), f32),
            pltpu.VMEM((tokens, index_width), f32),
            pltpu.VMEM((columns, index_width), f32),
            pltpu.VMEM((TAIL, LANES), f32),
        ],
        [whole(v) for v in mass]
        + [key_only] * blocks
        + [whole(v) for v in (probs, query_rows, weight_rows)],
        pl.CostEstimate(
            flops=6 * tokens * columns * index_width,
            bytes_accessed=2 * columns * index_width,
            transcendentals=0,
        ),
    )
    odd = swap(odd, "pb", 1)
    term = shape((rows, index_width), f32)
    half = shape((rows, index_width), bf16)
    mine, *others = call(pair_kernel, [term] + [half] * (blocks // 2 - 1), (even, odd))
    others = [swap(value, "pb", 2 * (i + 1)) for i, value in enumerate(others)]
    mine = call(sum_kernel, half, [mine] + others)
    key_grad = call(sum_kernel, half, [mine] + [swap(mine, "ha", r) for r in range(1, parts)])

    answers = [answers[0]] + [swap(answers[r], "ha", r) for r in range(1, parts)]
    query_grad, weight_grad = call(
        functools.partial(finish_kernel, share, heads),
        [shape((rows * heads, index_width), bf16), shape((heads, rows), f32)],
        answers,
    )
    return (query_grad.reshape(index_query.shape), key_grad, weight_grad.T)


def solution(mesh):
    return jax.shard_map(
        on_device,
        mesh=mesh,
        in_specs=(
            P("pb", "ha", None),
            P("pb", None),
            P("pb", "ha"),
            P("pb"),
            P("pb", "ha", None),
            P("pb", None),
            P("pb", "ha"),
        ),
        out_specs=(P("pb", "ha", None), P("pb", None), P("pb", "ha")),
        check_vma=False,
    )
```

```python
import functools

import jax
import jax.numpy as jnp
from jax import lax
from jax.experimental import pallas as pl
from jax.experimental.pallas import tpu as pltpu
from jax.sharding import PartitionSpec as P

main_scale = 192.0 ** (-0.5)
log2e = 1.4426950408889634
very_low = -1e30
LANES = 128
FILL = 10
TAIL = 16
f32, bf16 = jnp.float32, jnp.bfloat16


def params():
    return pltpu.CompilerParams(vmem_limit_bytes=24 * 1024 * 1024)


def whole(value):
    zeros = (0,) * len(value.shape)
    return pl.BlockSpec(value.shape, lambda *_: zeros)


def call(kernel, outs, values, scratch=(), specs=None, cost=None):
    many = isinstance(outs, list)
    found = pl.pallas_call(
        kernel,
        grid=(1,),
        out_shape=outs,
        in_specs=specs or [whole(v) for v in values],
        out_specs=[whole(o) for o in outs] if many else whole(outs),
        scratch_shapes=list(scratch),
        compiler_params=params(),
        cost_estimate=cost,
    )(*values)
    return list(found) if many else found


def tree(values):
    while len(values) > 1:
        values = [values[i] + values[i + 1] for i in range(0, len(values), 2)]
    return values[0]


def terms_of(value, count):
    found = []
    for _ in range(count):
        term = value.astype(bf16)
        found.append(term)
        value = value - term.astype(f32)
    return found


def pack_kernel(latent_ref, key_ref, packed_ref):
    width = key_ref.shape[1]
    packed_ref[:, :width] = key_ref[...]
    packed_ref[:, width:] = latent_ref[...].T


def ask_kernel(query_ref, weight_ref, *outs):
    me = lax.axis_index("ha")
    heads = weight_ref.shape[0]
    rows = outs[0].shape[0] - 3 * TAIL
    split = terms_of(weight_ref[...], 3)
    for r, out in enumerate(outs):
        first = pl.multiple_of((me ^ r) * rows, rows)
        out[:rows, :] = query_ref[pl.ds(first, rows), :]
        for i in range(3):
            at = rows + i * TAIL
            if heads < TAIL:
                out[at : at + TAIL, :] = jnp.zeros((TAIL, LANES), bf16)
            out[at : at + heads, :] = split[i]


def own_lanes(value, share):
    me = lax.axis_index("ha")
    value = pltpu.roll(value, lax.rem(LANES - me * share, LANES), 1)
    lanes = lax.broadcasted_iota(jnp.int32, value.shape, 1)
    value = jnp.where(lanes < share, value, jnp.zeros_like(value))
    shift = share
    while shift < LANES:
        value = value + pltpu.roll(value, shift, 1)
        shift *= 2
    return value


def main_kernel(rels, earlier, *refs):
    count = len(rels)
    blocks = refs[:count]
    query, sums_ref, start_ref = refs[count : count + 3]
    before = refs[count + 3 : count + 3 + earlier]
    outs = refs[count + 3 + earlier : -3]
    keys, total, turned = refs[-3:]
    heads, width, rows = query.shape
    for k in range(count):
        block = blocks[k][...]
        keys[k * rows : (k + 1) * rows, :] = block[:, block.shape[1] - width :]
    total[...] = jnp.zeros_like(total)

    for head in range(0, heads, 2):
        two = jnp.concatenate([query[head], query[head + 1]], axis=1)
        scores = jnp.dot(keys[...], two, preferred_element_type=f32)
        parts = [
            jnp.exp2(
                scores[:, half * rows : (half + 1) * rows] * (main_scale * log2e)
                - sums_ref[head + half : head + half + 1, :] * log2e
            )
            for half in range(2)
        ]
        total[...] += parts[0] + parts[1]

    me = lax.axis_index("pb")
    kept = turned.shape[1] - count * rows
    at = 0
    for ref in before:
        turned[:, at : at + ref.shape[1]] = ref[...].astype(f32)
        at += ref.shape[1]
    for k in range(count):
        key = (me ^ rels[k]) * rows + lax.broadcasted_iota(jnp.int32, (rows, rows), 0)
        mine = me * rows + lax.broadcasted_iota(jnp.int32, (rows, rows), 1)
        seen = (key >= start_ref[...]) & (key <= mine)
        piece = jnp.where(seen, total[k * rows : (k + 1) * rows, :], 0.0)
        turned[:, kept + k * rows : kept + (k + 1) * rows] = piece.T
    if len(outs) == 1:
        outs[0][...] = turned[...].astype(bf16)
    else:
        me = lax.axis_index("ha")
        share = outs[0].shape[0]
        for r, out in enumerate(outs):
            first = pl.multiple_of((me ^ r) * share, share)
            out[...] = turned[pl.ds(first, share), :].astype(bf16)


def index_kernel(share, count, parts, heads, *refs):
    blocks = refs[:count]
    messages = refs[count : count + parts]
    start_ref, prob_ref, queries_ref, weights_ref, keys, wide, total = refs[count + parts :]
    rows, width = blocks[0].shape
    for k in range(count):
        keys[k * rows : (k + 1) * rows, :] = blocks[k][...]
    own = share * heads
    repeats = LANES // share
    group = lax.broadcasted_iota(jnp.int32, (1, LANES), 1) // share
    row_of = []
    for r in range(parts):
        wide[...] = messages[r][:own, :].astype(f32)
        for j in range(heads):
            first = (r * heads + j) * share
            queries_ref[first : first + share, :] = wide[
                pl.ds(j, share, stride=heads), :
            ].astype(bf16)
        weight = tree_of_three(messages[r], own)
        weight = own_lanes(weight, share)
        row_of += [weight[j : j + 1, :] for j in range(heads)]
    weights_ref[...] = jnp.zeros_like(weights_ref)
    for g in range(len(row_of) // repeats):
        row = row_of[g * repeats]
        for i in range(1, repeats):
            row = jnp.where(group == i, row_of[g * repeats + i], row)
        weights_ref[g : g + 1, :] = row
    total[...] = jnp.zeros_like(total)
    for g in range(0, len(row_of) // repeats, 2):
        two = queries_ref[g * LANES : (g + 2) * LANES, :]
        act = lax.dot_general(
            keys[...], two, (((1,), (1,)), ((), ())), preferred_element_type=f32
        )
        act = jnp.maximum(act, 0.0)
        total[...] += (
            act[:, :LANES] * weights_ref[g : g + 1, :]
            + act[:, LANES:] * weights_ref[g + 1 : g + 2, :]
        )

    me = lax.axis_index("pb")
    lane = lax.broadcasted_iota(jnp.int32, (rows, LANES), 1) % share
    mine = me * rows + lax.axis_index("ha") * share + lane
    start = own_lanes(jnp.broadcast_to(start_ref[...], (8, LANES)), share)[:1, :]
    top = jnp.full((1, LANES), very_low, f32)
    masks = []
    for k in range(count):
        at = slice(k * rows, (k + 1) * rows)
        key = (me ^ k) * rows + lax.broadcasted_iota(jnp.int32, (rows, LANES), 0)
        seen = (key >= start) & (key <= mine)
        value = total[at, :]
        shift = share
        while shift < LANES:
            value = value + pltpu.roll(value, shift, 1)
            shift *= 2
        value = jnp.where(seen, value, very_low)
        total[at, :] = value
        top = jnp.maximum(top, jnp.max(value, axis=0, keepdims=True))
        masks.append(seen)
    mass = jnp.zeros((1, LANES), f32)
    for k in range(count):
        at = slice(k * rows, (k + 1) * rows)
        value = jnp.where(masks[k], jnp.exp(total[at, :] - top), 0.0)
        prob_ref[at, :] = value
        mass = mass + jnp.sum(value, axis=0, keepdims=True)
    prob_ref[...] = prob_ref[...] * (1.0 / mass)


def tree_of_three(ref, at):
    parts = [ref[at + i * TAIL : at + (i + 1) * TAIL, :].astype(f32) for i in range(3)]
    return parts[0] + (parts[1] + parts[2])


def back_kernel(share, count, parts, heads, *refs):
    mass_refs = refs[:parts]
    blocks = refs[parts : parts + count]
    prob_ref, queries_ref, weights_ref = refs[parts + count : parts + count + 3]
    outs = refs[parts + count + 3 : -6]
    even_ref, odd_ref = outs[:2]
    messages = outs[2:]
    keys, turned_keys, grad, key_total, query_total, weight_total = refs[-6:]
    rows, width = blocks[0].shape
    repeats = LANES // share
    mass = tree([ref[...].astype(f32) for ref in mass_refs])
    for k in range(count):
        at = slice(k * rows, (k + 1) * rows)
        keys[at, :] = blocks[k][...]
        turned_keys[:, at] = blocks[k][...].T
        grad[at, :] = jnp.concatenate([mass[:, at]] * repeats, axis=0).T
    total = jnp.sum(grad[...], axis=0, keepdims=True)
    grad[...] = prob_ref[...] - grad[...] / total
    key_total[...] = jnp.zeros_like(key_total)
    weight_total[...] = jnp.zeros_like(weight_total)
    all_heads = parts * heads
    for g in range(0, all_heads // repeats, 2):
        two = queries_ref[g * LANES : (g + 2) * LANES, :]
        act = lax.dot_general(
            keys[...], two, (((1,), (1,)), ((), ())), preferred_element_type=f32
        )
        coeffs = []
        for half in range(2):
            mine = act[:, half * LANES : (half + 1) * LANES]
            lean = grad[...]
            weight_total[g + half : g + half + 1, :] = jnp.sum(
                lean * jnp.maximum(mine, 0.0), axis=0, keepdims=True
            )
            coeffs.append(
                jnp.where(
                    mine > 0.0, lean * weights_ref[g + half : g + half + 1, :], 0.0
                ).astype(bf16)
            )
        coeffs = jnp.concatenate(coeffs, axis=1)
        key_total[...] += jnp.dot(coeffs, two, preferred_element_type=f32)
        found = jnp.dot(turned_keys[...], coeffs, preferred_element_type=f32)
        found = jnp.concatenate([found[:, :LANES].T, found[:, LANES:].T], axis=0)
        for i in range(2 * repeats):
            head = g * repeats + i
            first = (head // heads) * heads * share + head % heads
            query_total[pl.ds(first, share, stride=heads), :] = found[
                i * share : (i + 1) * share, :
            ]
    own = share * heads
    split = terms_of(weight_total[...], 2)
    for r in range(parts):
        messages[r][:own, :] = query_total[r * own : (r + 1) * own, :].astype(bf16)
        for i in range(2):
            messages[r][own + i * TAIL : own + (i + 1) * TAIL, :] = split[i]
    for i in range(count // 2):
        at = slice(i * rows, (i + 1) * rows)
        even_ref[at, :] = key_total[2 * i * rows : (2 * i + 1) * rows, :]
        odd_ref[at, :] = key_total[(2 * i + 1) * rows : (2 * i + 2) * rows, :]


def pair_kernel(mine_ref, other_ref, own_ref, *outs):
    rows = own_ref.shape[0]
    own_ref[...] = mine_ref[:rows, :] + other_ref[:rows, :]
    for i, out in enumerate(outs):
        at = slice((i + 1) * rows, (i + 2) * rows)
        out[...] = (mine_ref[at, :] + other_ref[at, :]).astype(out.dtype)


def sum_kernel(*refs):
    out_ref = refs[-1]
    out_ref[...] = tree([ref[...].astype(f32) for ref in refs[:-1]]).astype(out_ref.dtype)


def finish_kernel(share, heads, *refs):
    messages = refs[:-2]
    query_out, weight_out = refs[-2:]
    me = lax.axis_index("ha")
    own = share * heads
    total = jnp.zeros((heads, LANES), f32)
    lanes = lax.broadcasted_iota(jnp.int32, (heads, LANES), 1)
    for r, message in enumerate(messages):
        first = pl.multiple_of((me ^ r) * own, own)
        query_out[pl.ds(first, own), :] = message[:own, :]
        value = message[own : own + TAIL, :].astype(f32) + message[
            own + TAIL : own + 2 * TAIL, :
        ].astype(f32)
        rolled = {}
        found = []
        for j in range(heads):
            column = (r * heads + j) * share
            row, lane = column // LANES, column % LANES
            if lane not in rolled:
                rolled[lane] = pltpu.roll(value, LANES - lane, 1) if lane else value
            found.append(rolled[lane][row : row + 1, :])
        piece = jnp.where(lanes < share, jnp.concatenate(found, axis=0), 0.0)
        total = total + pltpu.roll(piece, (me ^ r) * share, 1)
    weight_out[...] = total


def on_device(main_query, latent, log_sums, window_start, index_query, index_key, index_weight):
    rows, head_count, width = main_query.shape
    heads, index_width = index_query.shape[1:]
    blocks = lax.axis_size("pb")
    parts = lax.axis_size("ha")
    share = rows // parts
    tokens = blocks * rows
    own = share * heads
    columns = share * heads * parts
    shape = jax.ShapeDtypeStruct

    def swap(value, axis, rel):
        size = lax.axis_size(axis)
        return lax.ppermute(value, axis, [(i, i ^ rel) for i in range(size)])

    start_row = window_start.reshape(1, rows)
    key_only = pl.BlockSpec((rows, index_width), lambda *_: (0, 0))

    packed = call(
        pack_kernel,
        shape((rows, index_width + width), bf16),
        (latent.T, index_key),
        cost=pl.CostEstimate(flops=0, bytes_accessed=1 << 24, transcendentals=0),
    )
    asked = call(
        ask_kernel,
        [shape((own + 3 * TAIL, index_width), bf16)] * parts,
        (index_query.reshape(rows * heads, index_width), index_weight.T),
    )
    queries = jnp.transpose(main_query, (1, 2, 0))
    sums = log_sums.T
    held = [None] * blocks
    held[0] = packed
    held[1] = swap(packed, "pb", 1)
    for k in range(2, blocks, 2):
        held[k] = swap(packed, "pb", k)
    ready = lax.optimization_barrier((asked[0], held[1]))
    asked = [ready[0]] + [swap(asked[r], "ha", r) for r in range(1, parts)]
    held[1] = ready[1]

    chunks = [[0, 1]] + [list(range(k, min(k + 4, blocks))) for k in range(2, blocks, 4)]
    mass = []
    for rels in chunks:
        last = rels is chunks[-1]
        span = len(rels) * rows
        outs = [shape((share, tokens), bf16)] * parts if last else [shape((rows, span), bf16)]
        before = mass if last else []
        values = [held[k] for k in rels] + [queries, sums, start_row] + before
        specs = [whole(v) for v in values]
        specs[len(rels)] = pl.BlockSpec(memory_space=pltpu.VMEM)
        found = call(
            functools.partial(main_kernel, rels, len(before)),
            outs,
            values,
            [
                pltpu.VMEM((span, width), bf16),
                pltpu.VMEM((span, rows), f32),
                pltpu.VMEM((rows, tokens if last else span), f32),
            ],
            specs,
            pl.CostEstimate(
                flops=2 * span * rows * head_count * width * (FILL if rels is chunks[0] else 1),
                bytes_accessed=2 * rows * head_count * width,
                transcendentals=span * rows * head_count,
            ),
        )
        mass = found if last else mass + found
        if rels is chunks[0]:
            even = list(range(2, blocks, 2))
            ready = lax.optimization_barrier((found[0], [held[k] for k in even], asked[1:3]))
            mass = [ready[0]]
            asked[1:3] = ready[2]
            for k, block in zip(even, ready[1]):
                held[k] = block
                held[k + 1] = swap(block, "pb", 1)
    first, key_block = lax.optimization_barrier((mass[0], held[0]))
    mass = [first] + [swap(mass[r], "ha", r) for r in range(1, parts)]
    key_blocks = [key_block] + held[1:]

    probs, query_rows, weight_rows = call(
        functools.partial(index_kernel, share, blocks, parts, heads),
        [
            shape((tokens, LANES), f32),
            shape((columns, index_width), bf16),
            shape((TAIL, LANES), f32),
        ],
        key_blocks + asked + [start_row],
        [
            pltpu.VMEM((tokens, index_width), bf16),
            pltpu.VMEM((own, index_width), f32),
            pltpu.VMEM((tokens, LANES), f32),
        ],
        [key_only] * blocks + [whole(v) for v in asked + [start_row]],
        pl.CostEstimate(
            flops=2 * tokens * columns * index_width,
            bytes_accessed=2 * columns * index_width,
            transcendentals=tokens * LANES,
        ),
    )

    even, odd, *answers = call(
        functools.partial(back_kernel, share, blocks, parts, heads),
        [shape((tokens // 2, index_width), f32)] * 2
        + [shape((own + 2 * TAIL, index_width), bf16)] * parts,
        mass + key_blocks + [probs, query_rows, weight_rows],
        [
            pltpu.VMEM((tokens, index_width), bf16),
            pltpu.VMEM((index_width, tokens), bf16),
            pltpu.VMEM((tokens, LANES), f32),
            pltpu.VMEM((tokens, index_width), f32),
            pltpu.VMEM((columns, index_width), f32),
            pltpu.VMEM((TAIL, LANES), f32),
        ],
        [whole(v) for v in mass]
        + [key_only] * blocks
        + [whole(v) for v in (probs, query_rows, weight_rows)],
        pl.CostEstimate(
            flops=6 * tokens * columns * index_width,
            bytes_accessed=2 * columns * index_width,
            transcendentals=0,
        ),
    )
    odd = swap(odd, "pb", 1)
    term = shape((rows, index_width), f32)
    half = shape((rows, index_width), bf16)
    mine, *others = call(pair_kernel, [term] + [half] * (blocks // 2 - 1), (even, odd))
    others = [swap(value, "pb", 2 * (i + 1)) for i, value in enumerate(others)]
    mine, answers[1] = lax.optimization_barrier(
        (call(sum_kernel, half, [mine] + others), answers[1])
    )
    key_grad = call(sum_kernel, half, [mine] + [swap(mine, "ha", r) for r in range(1, parts)])

    answers = [answers[0]] + [swap(answers[r], "ha", r) for r in range(1, parts)]
    query_grad, weight_grad = call(
        functools.partial(finish_kernel, share, heads),
        [shape((rows * heads, index_width), bf16), shape((heads, rows), f32)],
        answers,
    )
    return (query_grad.reshape(index_query.shape), key_grad, weight_grad.T)


def solution(mesh):
    return jax.shard_map(
        on_device,
        mesh=mesh,
        in_specs=(
            P("pb", "ha", None),
            P("pb", None),
            P("pb", "ha"),
            P("pb"),
            P("pb", "ha", None),
            P("pb", None),
            P("pb", "ha"),
        ),
        out_specs=(P("pb", "ha", None), P("pb", None), P("pb", "ha")),
        check_vma=False,
    )
```

```python
import functools

import jax
import jax.numpy as jnp
from jax import lax
from jax.experimental import pallas as pl
from jax.experimental.pallas import tpu as pltpu
from jax.sharding import PartitionSpec as P

main_scale = 192.0 ** (-0.5)
log2e = 1.4426950408889634
very_low = -1e30
LANES = 128
FILL = 10
TAIL = 16
f32, bf16 = jnp.float32, jnp.bfloat16


def params():
    return pltpu.CompilerParams(vmem_limit_bytes=24 * 1024 * 1024)


def whole(value):
    zeros = (0,) * len(value.shape)
    return pl.BlockSpec(value.shape, lambda *_: zeros)


def call(kernel, outs, values, scratch=(), specs=None, cost=None):
    many = isinstance(outs, list)
    found = pl.pallas_call(
        kernel,
        grid=(1,),
        out_shape=outs,
        in_specs=specs or [whole(v) for v in values],
        out_specs=[whole(o) for o in outs] if many else whole(outs),
        scratch_shapes=list(scratch),
        compiler_params=params(),
        cost_estimate=cost,
    )(*values)
    return list(found) if many else found


def tree(values):
    while len(values) > 1:
        values = [values[i] + values[i + 1] for i in range(0, len(values), 2)]
    return values[0]


def terms_of(value, count):
    found = []
    for _ in range(count):
        term = value.astype(bf16)
        found.append(term)
        value = value - term.astype(f32)
    return found


def pack_kernel(latent_ref, key_ref, packed_ref):
    width = key_ref.shape[1]
    packed_ref[:, :width] = key_ref[...]
    packed_ref[:, width:] = latent_ref[...].T


def ask_kernel(query_ref, weight_ref, *outs):
    me = lax.axis_index("ha")
    heads = weight_ref.shape[0]
    rows = outs[0].shape[0] - 3 * TAIL
    split = terms_of(weight_ref[...], 3)
    for r, out in enumerate(outs):
        first = pl.multiple_of((me ^ r) * rows, rows)
        out[:rows, :] = query_ref[pl.ds(first, rows), :]
        for i in range(3):
            at = rows + i * TAIL
            if heads < TAIL:
                out[at : at + TAIL, :] = jnp.zeros((TAIL, LANES), bf16)
            out[at : at + heads, :] = split[i]


def own_lanes(value, share):
    me = lax.axis_index("ha")
    value = pltpu.roll(value, lax.rem(LANES - me * share, LANES), 1)
    lanes = lax.broadcasted_iota(jnp.int32, value.shape, 1)
    value = jnp.where(lanes < share, value, jnp.zeros_like(value))
    shift = share
    while shift < LANES:
        value = value + pltpu.roll(value, shift, 1)
        shift *= 2
    return value


def main_kernel(rels, earlier, *refs):
    count = len(rels)
    blocks = refs[:count]
    query, sums_ref, start_ref = refs[count : count + 3]
    before = refs[count + 3 : count + 3 + earlier]
    outs = refs[count + 3 + earlier : -3]
    keys, total, turned = refs[-3:]
    heads, width, rows = query.shape
    for k in range(count):
        block = blocks[k][...]
        keys[k * rows : (k + 1) * rows, :] = block[:, block.shape[1] - width :]
    total[...] = jnp.zeros_like(total)

    for head in range(0, heads, 2):
        two = jnp.concatenate([query[head], query[head + 1]], axis=1)
        scores = jnp.dot(keys[...], two, preferred_element_type=f32)
        parts = [
            jnp.exp2(
                scores[:, half * rows : (half + 1) * rows] * (main_scale * log2e)
                - sums_ref[head + half : head + half + 1, :] * log2e
            )
            for half in range(2)
        ]
        total[...] += parts[0] + parts[1]

    me = lax.axis_index("pb")
    kept = turned.shape[1] - count * rows
    at = 0
    for ref in before:
        turned[:, at : at + ref.shape[1]] = ref[...].astype(f32)
        at += ref.shape[1]
    for k in range(count):
        key = (me ^ rels[k]) * rows + lax.broadcasted_iota(jnp.int32, (rows, rows), 0)
        mine = me * rows + lax.broadcasted_iota(jnp.int32, (rows, rows), 1)
        seen = (key >= start_ref[...]) & (key <= mine)
        piece = jnp.where(seen, total[k * rows : (k + 1) * rows, :], 0.0)
        turned[:, kept + k * rows : kept + (k + 1) * rows] = piece.T
    if len(outs) == 1:
        outs[0][...] = turned[...].astype(bf16)
    else:
        me = lax.axis_index("ha")
        share = outs[0].shape[0]
        for r, out in enumerate(outs):
            first = pl.multiple_of((me ^ r) * share, share)
            out[...] = turned[pl.ds(first, share), :].astype(bf16)


def index_kernel(share, count, parts, heads, *refs):
    blocks = refs[:count]
    messages = refs[count : count + parts]
    start_ref, prob_ref, queries_ref, weights_ref, keys, wide, total = refs[count + parts :]
    rows, width = blocks[0].shape
    for k in range(count):
        keys[k * rows : (k + 1) * rows, :] = blocks[k][...]
    own = share * heads
    repeats = LANES // share
    group = lax.broadcasted_iota(jnp.int32, (1, LANES), 1) // share
    row_of = []
    for r in range(parts):
        wide[...] = messages[r][:own, :].astype(f32)
        for j in range(heads):
            first = (r * heads + j) * share
            queries_ref[first : first + share, :] = wide[
                pl.ds(j, share, stride=heads), :
            ].astype(bf16)
        weight = tree_of_three(messages[r], own)
        weight = own_lanes(weight, share)
        row_of += [weight[j : j + 1, :] for j in range(heads)]
    weights_ref[...] = jnp.zeros_like(weights_ref)
    for g in range(len(row_of) // repeats):
        row = row_of[g * repeats]
        for i in range(1, repeats):
            row = jnp.where(group == i, row_of[g * repeats + i], row)
        weights_ref[g : g + 1, :] = row
    total[...] = jnp.zeros_like(total)
    for g in range(0, len(row_of) // repeats, 2):
        two = queries_ref[g * LANES : (g + 2) * LANES, :]
        act = lax.dot_general(
            keys[...], two, (((1,), (1,)), ((), ())), preferred_element_type=f32
        )
        act = jnp.maximum(act, 0.0)
        total[...] += (
            act[:, :LANES] * weights_ref[g : g + 1, :]
            + act[:, LANES:] * weights_ref[g + 1 : g + 2, :]
        )

    me = lax.axis_index("pb")
    lane = lax.broadcasted_iota(jnp.int32, (rows, LANES), 1) % share
    mine = me * rows + lax.axis_index("ha") * share + lane
    start = own_lanes(jnp.broadcast_to(start_ref[...], (8, LANES)), share)[:1, :]
    top = jnp.full((1, LANES), very_low, f32)
    masks = []
    for k in range(count):
        at = slice(k * rows, (k + 1) * rows)
        key = (me ^ k) * rows + lax.broadcasted_iota(jnp.int32, (rows, LANES), 0)
        seen = (key >= start) & (key <= mine)
        value = total[at, :]
        shift = share
        while shift < LANES:
            value = value + pltpu.roll(value, shift, 1)
            shift *= 2
        value = jnp.where(seen, value, very_low)
        total[at, :] = value
        top = jnp.maximum(top, jnp.max(value, axis=0, keepdims=True))
        masks.append(seen)
    mass = jnp.zeros((1, LANES), f32)
    for k in range(count):
        at = slice(k * rows, (k + 1) * rows)
        value = jnp.where(masks[k], jnp.exp(total[at, :] - top), 0.0)
        prob_ref[at, :] = value
        mass = mass + jnp.sum(value, axis=0, keepdims=True)
    prob_ref[...] = prob_ref[...] * (1.0 / mass)


def tree_of_three(ref, at):
    parts = [ref[at + i * TAIL : at + (i + 1) * TAIL, :].astype(f32) for i in range(3)]
    return parts[0] + (parts[1] + parts[2])


def back_kernel(share, count, parts, heads, *refs):
    mass_refs = refs[:parts]
    blocks = refs[parts : parts + count]
    prob_ref, queries_ref, weights_ref = refs[parts + count : parts + count + 3]
    outs = refs[parts + count + 3 : -6]
    even_ref, odd_ref = outs[:2]
    messages = outs[2:]
    keys, turned_keys, grad, key_total, query_total, weight_total = refs[-6:]
    rows, width = blocks[0].shape
    repeats = LANES // share
    mass = tree([ref[...].astype(f32) for ref in mass_refs])
    for k in range(count):
        at = slice(k * rows, (k + 1) * rows)
        keys[at, :] = blocks[k][...]
        turned_keys[:, at] = blocks[k][...].T
        grad[at, :] = jnp.concatenate([mass[:, at]] * repeats, axis=0).T
    total = jnp.sum(grad[...], axis=0, keepdims=True)
    grad[...] = prob_ref[...] - grad[...] / total
    key_total[...] = jnp.zeros_like(key_total)
    weight_total[...] = jnp.zeros_like(weight_total)
    all_heads = parts * heads
    for g in range(0, all_heads // repeats, 2):
        two = queries_ref[g * LANES : (g + 2) * LANES, :]
        act = lax.dot_general(
            keys[...], two, (((1,), (1,)), ((), ())), preferred_element_type=f32
        )
        coeffs = []
        for half in range(2):
            mine = act[:, half * LANES : (half + 1) * LANES]
            lean = grad[...]
            weight_total[g + half : g + half + 1, :] = jnp.sum(
                lean * jnp.maximum(mine, 0.0), axis=0, keepdims=True
            )
            coeffs.append(
                jnp.where(
                    mine > 0.0, lean * weights_ref[g + half : g + half + 1, :], 0.0
                ).astype(bf16)
            )
        coeffs = jnp.concatenate(coeffs, axis=1)
        key_total[...] += jnp.dot(coeffs, two, preferred_element_type=f32)
        found = jnp.dot(turned_keys[...], coeffs, preferred_element_type=f32)
        found = jnp.concatenate([found[:, :LANES].T, found[:, LANES:].T], axis=0)
        for i in range(2 * repeats):
            head = g * repeats + i
            first = (head // heads) * heads * share + head % heads
            query_total[pl.ds(first, share, stride=heads), :] = found[
                i * share : (i + 1) * share, :
            ]
    own = share * heads
    split = terms_of(weight_total[...], 2)
    for r in range(parts):
        messages[r][:own, :] = query_total[r * own : (r + 1) * own, :].astype(bf16)
        for i in range(2):
            messages[r][own + i * TAIL : own + (i + 1) * TAIL, :] = split[i]
    for i in range(count // 2):
        at = slice(i * rows, (i + 1) * rows)
        even_ref[at, :] = key_total[2 * i * rows : (2 * i + 1) * rows, :]
        odd_ref[at, :] = key_total[(2 * i + 1) * rows : (2 * i + 2) * rows, :]


def pair_kernel(mine_ref, other_ref, own_ref, *outs):
    rows = own_ref.shape[0]
    own_ref[...] = mine_ref[:rows, :] + other_ref[:rows, :]
    for i, out in enumerate(outs):
        at = slice((i + 1) * rows, (i + 2) * rows)
        out[...] = (mine_ref[at, :] + other_ref[at, :]).astype(out.dtype)


def sum_kernel(*refs):
    out_ref = refs[-1]
    out_ref[...] = tree([ref[...].astype(f32) for ref in refs[:-1]]).astype(out_ref.dtype)


def finish_kernel(share, heads, *refs):
    messages = refs[:-2]
    query_out, weight_out = refs[-2:]
    me = lax.axis_index("ha")
    own = share * heads
    total = jnp.zeros((heads, LANES), f32)
    lanes = lax.broadcasted_iota(jnp.int32, (heads, LANES), 1)
    for r, message in enumerate(messages):
        first = pl.multiple_of((me ^ r) * own, own)
        query_out[pl.ds(first, own), :] = message[:own, :]
        value = message[own : own + TAIL, :].astype(f32) + message[
            own + TAIL : own + 2 * TAIL, :
        ].astype(f32)
        rolled = {}
        found = []
        for j in range(heads):
            column = (r * heads + j) * share
            row, lane = column // LANES, column % LANES
            if lane not in rolled:
                rolled[lane] = pltpu.roll(value, LANES - lane, 1) if lane else value
            found.append(rolled[lane][row : row + 1, :])
        piece = jnp.where(lanes < share, jnp.concatenate(found, axis=0), 0.0)
        total = total + pltpu.roll(piece, (me ^ r) * share, 1)
    weight_out[...] = total


def on_device(main_query, latent, log_sums, window_start, index_query, index_key, index_weight):
    rows, head_count, width = main_query.shape
    heads, index_width = index_query.shape[1:]
    blocks = lax.axis_size("pb")
    parts = lax.axis_size("ha")
    share = rows // parts
    tokens = blocks * rows
    own = share * heads
    columns = share * heads * parts
    shape = jax.ShapeDtypeStruct

    def swap(value, axis, rel):
        size = lax.axis_size(axis)
        return lax.ppermute(value, axis, [(i, i ^ rel) for i in range(size)])

    start_row = window_start.reshape(1, rows)
    key_only = pl.BlockSpec((rows, index_width), lambda *_: (0, 0))

    packed = call(
        pack_kernel,
        shape((rows, index_width + width), bf16),
        (latent.T, index_key),
        cost=pl.CostEstimate(flops=0, bytes_accessed=1 << 24, transcendentals=0),
    )
    asked = call(
        ask_kernel,
        [shape((own + 3 * TAIL, index_width), bf16)] * parts,
        (index_query.reshape(rows * heads, index_width), index_weight.T),
    )
    queries = jnp.transpose(main_query, (1, 2, 0))
    sums = log_sums.T
    held = [None] * blocks
    held[0] = packed
    held[1] = swap(packed, "pb", 1)
    for k in range(2, blocks, 2):
        held[k] = swap(packed, "pb", k)
    ready = lax.optimization_barrier((asked[0], held[1]))
    asked = [ready[0]] + [swap(asked[r], "ha", r) for r in range(1, parts)]
    held[1] = ready[1]

    chunks = [[0, 1]] + [list(range(k, min(k + 4, blocks))) for k in range(2, blocks, 4)]
    mass = []
    for rels in chunks:
        last = rels is chunks[-1]
        span = len(rels) * rows
        outs = [shape((share, tokens), bf16)] * parts if last else [shape((rows, span), bf16)]
        before = mass if last else []
        values = [held[k] for k in rels] + [queries, sums, start_row] + before
        specs = [whole(v) for v in values]
        specs[len(rels)] = pl.BlockSpec(memory_space=pltpu.VMEM)
        found = call(
            functools.partial(main_kernel, rels, len(before)),
            outs,
            values,
            [
                pltpu.VMEM((span, width), bf16),
                pltpu.VMEM((span, rows), f32),
                pltpu.VMEM((rows, tokens if last else span), f32),
            ],
            specs,
            pl.CostEstimate(
                flops=2 * span * rows * head_count * width * (FILL if rels is chunks[0] else 1),
                bytes_accessed=2 * rows * head_count * width,
                transcendentals=span * rows * head_count,
            ),
        )
        mass = found if last else mass + found
        if rels is chunks[0]:
            even = list(range(2, blocks, 2))
            ready = lax.optimization_barrier((found[0], [held[k] for k in even], asked[1:3]))
            mass = [ready[0]]
            asked[1:3] = ready[2]
            for k, block in zip(even, ready[1]):
                held[k] = block
                held[k + 1] = swap(block, "pb", 1)
    first, key_block = lax.optimization_barrier((mass[0], held[0]))
    mass = [first] + [swap(mass[r], "ha", r) for r in range(1, parts)]
    key_blocks = [key_block] + held[1:]

    probs, query_rows, weight_rows = call(
        functools.partial(index_kernel, share, blocks, parts, heads),
        [
            shape((tokens, LANES), f32),
            shape((columns, index_width), bf16),
            shape((TAIL, LANES), f32),
        ],
        key_blocks + asked + [start_row],
        [
            pltpu.VMEM((tokens, index_width), bf16),
            pltpu.VMEM((own, index_width), f32),
            pltpu.VMEM((tokens, LANES), f32),
        ],
        [key_only] * blocks + [whole(v) for v in asked + [start_row]],
        pl.CostEstimate(
            flops=2 * tokens * columns * index_width,
            bytes_accessed=2 * columns * index_width,
            transcendentals=tokens * LANES,
        ),
    )

    even, odd, *answers = call(
        functools.partial(back_kernel, share, blocks, parts, heads),
        [shape((tokens // 2, index_width), f32)] * 2
        + [shape((own + 2 * TAIL, index_width), bf16)] * parts,
        mass + key_blocks + [probs, query_rows, weight_rows],
        [
            pltpu.VMEM((tokens, index_width), bf16),
            pltpu.VMEM((index_width, tokens), bf16),
            pltpu.VMEM((tokens, LANES), f32),
            pltpu.VMEM((tokens, index_width), f32),
            pltpu.VMEM((columns, index_width), f32),
            pltpu.VMEM((TAIL, LANES), f32),
        ],
        [whole(v) for v in mass]
        + [key_only] * blocks
        + [whole(v) for v in (probs, query_rows, weight_rows)],
        pl.CostEstimate(
            flops=6 * tokens * columns * index_width,
            bytes_accessed=2 * columns * index_width,
            transcendentals=0,
        ),
    )
    odd = swap(odd, "pb", 1)
    term = shape((rows, index_width), f32)
    half = shape((rows, index_width), bf16)
    mine, *others = call(pair_kernel, [term] + [half] * (blocks // 2 - 1), (even, odd))
    others = [swap(value, "pb", 2 * (i + 1)) for i, value in enumerate(others)]
    answers[2] = swap(answers[2], "ha", 2)
    mine, answers[1:3] = lax.optimization_barrier(
        (call(sum_kernel, half, [mine] + others), answers[1:3])
    )
    key_grad = call(sum_kernel, half, [mine] + [swap(mine, "ha", r) for r in range(1, parts)])

    answers = [
        value if r in (0, 2) else swap(value, "ha", r) for r, value in enumerate(answers)
    ]
    query_grad, weight_grad = call(
        functools.partial(finish_kernel, share, heads),
        [shape((rows * heads, index_width), bf16), shape((heads, rows), f32)],
        answers,
    )
    return (query_grad.reshape(index_query.shape), key_grad, weight_grad.T)


def solution(mesh):
    return jax.shard_map(
        on_device,
        mesh=mesh,
        in_specs=(
            P("pb", "ha", None),
            P("pb", None),
            P("pb", "ha"),
            P("pb"),
            P("pb", "ha", None),
            P("pb", None),
            P("pb", "ha"),
        ),
        out_specs=(P("pb", "ha", None), P("pb", None), P("pb", "ha")),
        check_vma=False,
    )
```

```python
import functools

import jax
import jax.numpy as jnp
from jax import lax
from jax.experimental import pallas as pl
from jax.experimental.pallas import tpu as pltpu
from jax.sharding import PartitionSpec as P

main_scale = 192.0 ** (-0.5)
log2e = 1.4426950408889634
very_low = -1e30
LANES = 128
FILL = 10
TAIL = 16
f32, bf16 = jnp.float32, jnp.bfloat16


def params():
    return pltpu.CompilerParams(vmem_limit_bytes=24 * 1024 * 1024)


def whole(value):
    zeros = (0,) * len(value.shape)
    return pl.BlockSpec(value.shape, lambda *_: zeros)


def call(kernel, outs, values, scratch=(), specs=None, cost=None):
    many = isinstance(outs, list)
    found = pl.pallas_call(
        kernel,
        grid=(1,),
        out_shape=outs,
        in_specs=specs or [whole(v) for v in values],
        out_specs=[whole(o) for o in outs] if many else whole(outs),
        scratch_shapes=list(scratch),
        compiler_params=params(),
        cost_estimate=cost,
    )(*values)
    return list(found) if many else found


def tree(values):
    while len(values) > 1:
        values = [values[i] + values[i + 1] for i in range(0, len(values), 2)]
    return values[0]


def terms_of(value, count):
    found = []
    for _ in range(count):
        term = value.astype(bf16)
        found.append(term)
        value = value - term.astype(f32)
    return found


def pack_kernel(latent_ref, key_ref, packed_ref):
    width = key_ref.shape[1]
    packed_ref[:, :width] = key_ref[...]
    packed_ref[:, width:] = latent_ref[...].T


def ask_kernel(query_ref, weight_ref, *outs):
    me = lax.axis_index("ha")
    heads = weight_ref.shape[0]
    rows = outs[0].shape[0] - 3 * TAIL
    split = terms_of(weight_ref[...], 3)
    for r, out in enumerate(outs):
        first = pl.multiple_of((me ^ r) * rows, rows)
        out[:rows, :] = query_ref[pl.ds(first, rows), :]
        for i in range(3):
            at = rows + i * TAIL
            if heads < TAIL:
                out[at : at + TAIL, :] = jnp.zeros((TAIL, LANES), bf16)
            out[at : at + heads, :] = split[i]


def own_lanes(value, share):
    me = lax.axis_index("ha")
    value = pltpu.roll(value, lax.rem(LANES - me * share, LANES), 1)
    lanes = lax.broadcasted_iota(jnp.int32, value.shape, 1)
    value = jnp.where(lanes < share, value, jnp.zeros_like(value))
    shift = share
    while shift < LANES:
        value = value + pltpu.roll(value, shift, 1)
        shift *= 2
    return value


def main_kernel(rels, earlier, *refs):
    count = len(rels)
    blocks = refs[:count]
    query, sums_ref, start_ref = refs[count : count + 3]
    before = refs[count + 3 : count + 3 + earlier]
    outs = refs[count + 3 + earlier : -3]
    keys, total, turned = refs[-3:]
    heads, width, rows = query.shape
    for k in range(count):
        block = blocks[k][...]
        keys[k * rows : (k + 1) * rows, :] = block[:, block.shape[1] - width :]
    total[...] = jnp.zeros_like(total)

    for head in range(0, heads, 4):
        four = jnp.concatenate([query[head + n] for n in range(4)], axis=1)
        scores = jnp.dot(keys[...], four, preferred_element_type=f32)
        parts = [
            jnp.exp2(
                scores[:, n * rows : (n + 1) * rows] * (main_scale * log2e)
                - sums_ref[head + n : head + n + 1, :] * log2e
            )
            for n in range(4)
        ]
        total[...] += tree(parts)

    me = lax.axis_index("pb")
    kept = turned.shape[1] - count * rows
    at = 0
    for ref in before:
        turned[:, at : at + ref.shape[1]] = ref[...].astype(f32)
        at += ref.shape[1]
    for k in range(count):
        key = (me ^ rels[k]) * rows + lax.broadcasted_iota(jnp.int32, (rows, rows), 0)
        mine = me * rows + lax.broadcasted_iota(jnp.int32, (rows, rows), 1)
        seen = (key >= start_ref[...]) & (key <= mine)
        piece = jnp.where(seen, total[k * rows : (k + 1) * rows, :], 0.0)
        turned[:, kept + k * rows : kept + (k + 1) * rows] = piece.T
    if len(outs) == 1:
        outs[0][...] = turned[...].astype(bf16)
    else:
        me = lax.axis_index("ha")
        share = outs[0].shape[0]
        for r, out in enumerate(outs):
            first = pl.multiple_of((me ^ r) * share, share)
            out[...] = turned[pl.ds(first, share), :].astype(bf16)


def index_kernel(share, count, parts, heads, *refs):
    blocks = refs[:count]
    messages = refs[count : count + parts]
    start_ref, prob_ref, queries_ref, weights_ref, keys, wide, total = refs[count + parts :]
    rows, width = blocks[0].shape
    for k in range(count):
        keys[k * rows : (k + 1) * rows, :] = blocks[k][...]
    own = share * heads
    repeats = LANES // share
    group = lax.broadcasted_iota(jnp.int32, (1, LANES), 1) // share
    row_of = []
    for r in range(parts):
        wide[...] = messages[r][:own, :].astype(f32)
        for j in range(heads):
            first = (r * heads + j) * share
            queries_ref[first : first + share, :] = wide[
                pl.ds(j, share, stride=heads), :
            ].astype(bf16)
        weight = tree_of_three(messages[r], own)
        weight = own_lanes(weight, share)
        row_of += [weight[j : j + 1, :] for j in range(heads)]
    weights_ref[...] = jnp.zeros_like(weights_ref)
    for g in range(len(row_of) // repeats):
        row = row_of[g * repeats]
        for i in range(1, repeats):
            row = jnp.where(group == i, row_of[g * repeats + i], row)
        weights_ref[g : g + 1, :] = row
    total[...] = jnp.zeros_like(total)
    for g in range(0, len(row_of) // repeats, 2):
        two = queries_ref[g * LANES : (g + 2) * LANES, :]
        act = lax.dot_general(
            keys[...], two, (((1,), (1,)), ((), ())), preferred_element_type=f32
        )
        act = jnp.maximum(act, 0.0)
        total[...] += (
            act[:, :LANES] * weights_ref[g : g + 1, :]
            + act[:, LANES:] * weights_ref[g + 1 : g + 2, :]
        )

    me = lax.axis_index("pb")
    lane = lax.broadcasted_iota(jnp.int32, (rows, LANES), 1) % share
    mine = me * rows + lax.axis_index("ha") * share + lane
    start = own_lanes(jnp.broadcast_to(start_ref[...], (8, LANES)), share)[:1, :]
    top = jnp.full((1, LANES), very_low, f32)
    masks = []
    for k in range(count):
        at = slice(k * rows, (k + 1) * rows)
        key = (me ^ k) * rows + lax.broadcasted_iota(jnp.int32, (rows, LANES), 0)
        seen = (key >= start) & (key <= mine)
        value = total[at, :]
        shift = share
        while shift < LANES:
            value = value + pltpu.roll(value, shift, 1)
            shift *= 2
        value = jnp.where(seen, value, very_low)
        total[at, :] = value
        top = jnp.maximum(top, jnp.max(value, axis=0, keepdims=True))
        masks.append(seen)
    mass = jnp.zeros((1, LANES), f32)
    for k in range(count):
        at = slice(k * rows, (k + 1) * rows)
        value = jnp.where(masks[k], jnp.exp(total[at, :] - top), 0.0)
        prob_ref[at, :] = value
        mass = mass + jnp.sum(value, axis=0, keepdims=True)
    prob_ref[...] = prob_ref[...] * (1.0 / mass)


def tree_of_three(ref, at):
    parts = [ref[at + i * TAIL : at + (i + 1) * TAIL, :].astype(f32) for i in range(3)]
    return parts[0] + (parts[1] + parts[2])


def back_kernel(share, count, parts, heads, *refs):
    mass_refs = refs[:parts]
    blocks = refs[parts : parts + count]
    prob_ref, queries_ref, weights_ref = refs[parts + count : parts + count + 3]
    outs = refs[parts + count + 3 : -6]
    even_ref, odd_ref = outs[:2]
    messages = outs[2:]
    keys, turned_keys, grad, key_total, query_total, weight_total = refs[-6:]
    rows, width = blocks[0].shape
    repeats = LANES // share
    mass = tree([ref[...].astype(f32) for ref in mass_refs])
    for k in range(count):
        at = slice(k * rows, (k + 1) * rows)
        keys[at, :] = blocks[k][...]
        turned_keys[:, at] = blocks[k][...].T
        grad[at, :] = jnp.concatenate([mass[:, at]] * repeats, axis=0).T
    total = jnp.sum(grad[...], axis=0, keepdims=True)
    grad[...] = prob_ref[...] - grad[...] / total
    key_total[...] = jnp.zeros_like(key_total)
    weight_total[...] = jnp.zeros_like(weight_total)
    all_heads = parts * heads
    for g in range(0, all_heads // repeats, 2):
        two = queries_ref[g * LANES : (g + 2) * LANES, :]
        act = lax.dot_general(
            keys[...], two, (((1,), (1,)), ((), ())), preferred_element_type=f32
        )
        coeffs = []
        for half in range(2):
            mine = act[:, half * LANES : (half + 1) * LANES]
            lean = grad[...]
            weight_total[g + half : g + half + 1, :] = jnp.sum(
                lean * jnp.maximum(mine, 0.0), axis=0, keepdims=True
            )
            coeffs.append(
                jnp.where(
                    mine > 0.0, lean * weights_ref[g + half : g + half + 1, :], 0.0
                ).astype(bf16)
            )
        coeffs = jnp.concatenate(coeffs, axis=1)
        key_total[...] += jnp.dot(coeffs, two, preferred_element_type=f32)
        found = jnp.dot(turned_keys[...], coeffs, preferred_element_type=f32)
        found = jnp.concatenate([found[:, :LANES].T, found[:, LANES:].T], axis=0)
        for i in range(2 * repeats):
            head = g * repeats + i
            first = (head // heads) * heads * share + head % heads
            query_total[pl.ds(first, share, stride=heads), :] = found[
                i * share : (i + 1) * share, :
            ]
    own = share * heads
    split = terms_of(weight_total[...], 2)
    for r in range(parts):
        messages[r][:own, :] = query_total[r * own : (r + 1) * own, :].astype(bf16)
        for i in range(2):
            messages[r][own + i * TAIL : own + (i + 1) * TAIL, :] = split[i]
    for i in range(count // 2):
        at = slice(i * rows, (i + 1) * rows)
        even_ref[at, :] = key_total[2 * i * rows : (2 * i + 1) * rows, :]
        odd_ref[at, :] = key_total[(2 * i + 1) * rows : (2 * i + 2) * rows, :]


def pair_kernel(mine_ref, other_ref, own_ref, *outs):
    rows = own_ref.shape[0]
    own_ref[...] = mine_ref[:rows, :] + other_ref[:rows, :]
    for i, out in enumerate(outs):
        at = slice((i + 1) * rows, (i + 2) * rows)
        out[...] = (mine_ref[at, :] + other_ref[at, :]).astype(out.dtype)


def sum_kernel(*refs):
    out_ref = refs[-1]
    out_ref[...] = tree([ref[...].astype(f32) for ref in refs[:-1]]).astype(out_ref.dtype)


def finish_kernel(share, heads, *refs):
    messages = refs[:-2]
    query_out, weight_out = refs[-2:]
    me = lax.axis_index("ha")
    own = share * heads
    total = jnp.zeros((heads, LANES), f32)
    lanes = lax.broadcasted_iota(jnp.int32, (heads, LANES), 1)
    for r, message in enumerate(messages):
        first = pl.multiple_of((me ^ r) * own, own)
        query_out[pl.ds(first, own), :] = message[:own, :]
        value = message[own : own + TAIL, :].astype(f32) + message[
            own + TAIL : own + 2 * TAIL, :
        ].astype(f32)
        rolled = {}
        found = []
        for j in range(heads):
            column = (r * heads + j) * share
            row, lane = column // LANES, column % LANES
            if lane not in rolled:
                rolled[lane] = pltpu.roll(value, LANES - lane, 1) if lane else value
            found.append(rolled[lane][row : row + 1, :])
        piece = jnp.where(lanes < share, jnp.concatenate(found, axis=0), 0.0)
        total = total + pltpu.roll(piece, (me ^ r) * share, 1)
    weight_out[...] = total


def on_device(main_query, latent, log_sums, window_start, index_query, index_key, index_weight):
    rows, head_count, width = main_query.shape
    heads, index_width = index_query.shape[1:]
    blocks = lax.axis_size("pb")
    parts = lax.axis_size("ha")
    share = rows // parts
    tokens = blocks * rows
    own = share * heads
    columns = share * heads * parts
    shape = jax.ShapeDtypeStruct

    def swap(value, axis, rel):
        size = lax.axis_size(axis)
        return lax.ppermute(value, axis, [(i, i ^ rel) for i in range(size)])

    start_row = window_start.reshape(1, rows)
    key_only = pl.BlockSpec((rows, index_width), lambda *_: (0, 0))

    packed = call(
        pack_kernel,
        shape((rows, index_width + width), bf16),
        (latent.T, index_key),
        cost=pl.CostEstimate(flops=0, bytes_accessed=1 << 24, transcendentals=0),
    )
    asked = call(
        ask_kernel,
        [shape((own + 3 * TAIL, index_width), bf16)] * parts,
        (index_query.reshape(rows * heads, index_width), index_weight.T),
    )
    queries = jnp.transpose(main_query, (1, 2, 0))
    sums = log_sums.T
    held = [None] * blocks
    held[0] = packed
    held[1] = swap(packed, "pb", 1)
    for k in range(2, blocks, 2):
        held[k] = swap(packed, "pb", k)
    ready = lax.optimization_barrier((asked[0], held[1]))
    asked = [ready[0]] + [swap(asked[r], "ha", r) for r in range(1, parts)]
    held[1] = ready[1]

    chunks = [[0, 1]] + [list(range(k, min(k + 4, blocks))) for k in range(2, blocks, 4)]
    mass = []
    for rels in chunks:
        last = rels is chunks[-1]
        span = len(rels) * rows
        outs = [shape((share, tokens), bf16)] * parts if last else [shape((rows, span), bf16)]
        before = mass if last else []
        values = [held[k] for k in rels] + [queries, sums, start_row] + before
        specs = [whole(v) for v in values]
        specs[len(rels)] = pl.BlockSpec(memory_space=pltpu.VMEM)
        found = call(
            functools.partial(main_kernel, rels, len(before)),
            outs,
            values,
            [
                pltpu.VMEM((span, width), bf16),
                pltpu.VMEM((span, rows), f32),
                pltpu.VMEM((rows, tokens if last else span), f32),
            ],
            specs,
            pl.CostEstimate(
                flops=2 * span * rows * head_count * width * (FILL if rels is chunks[0] else 1),
                bytes_accessed=2 * rows * head_count * width,
                transcendentals=span * rows * head_count,
            ),
        )
        mass = found if last else mass + found
        if rels is chunks[0]:
            even = list(range(2, blocks, 2))
            ready = lax.optimization_barrier((found[0], [held[k] for k in even], asked[1:3]))
            mass = [ready[0]]
            asked[1:3] = ready[2]
            for k, block in zip(even, ready[1]):
                held[k] = block
                held[k + 1] = swap(block, "pb", 1)
    first, key_block = lax.optimization_barrier((mass[0], held[0]))
    mass = [first] + [swap(mass[r], "ha", r) for r in range(1, parts)]
    key_blocks = [key_block] + held[1:]

    probs, query_rows, weight_rows = call(
        functools.partial(index_kernel, share, blocks, parts, heads),
        [
            shape((tokens, LANES), f32),
            shape((columns, index_width), bf16),
            shape((TAIL, LANES), f32),
        ],
        key_blocks + asked + [start_row],
        [
            pltpu.VMEM((tokens, index_width), bf16),
            pltpu.VMEM((own, index_width), f32),
            pltpu.VMEM((tokens, LANES), f32),
        ],
        [key_only] * blocks + [whole(v) for v in asked + [start_row]],
        pl.CostEstimate(
            flops=2 * tokens * columns * index_width,
            bytes_accessed=2 * columns * index_width,
            transcendentals=tokens * LANES,
        ),
    )

    even, odd, *answers = call(
        functools.partial(back_kernel, share, blocks, parts, heads),
        [shape((tokens // 2, index_width), f32)] * 2
        + [shape((own + 2 * TAIL, index_width), bf16)] * parts,
        mass + key_blocks + [probs, query_rows, weight_rows],
        [
            pltpu.VMEM((tokens, index_width), bf16),
            pltpu.VMEM((index_width, tokens), bf16),
            pltpu.VMEM((tokens, LANES), f32),
            pltpu.VMEM((tokens, index_width), f32),
            pltpu.VMEM((columns, index_width), f32),
            pltpu.VMEM((TAIL, LANES), f32),
        ],
        [whole(v) for v in mass]
        + [key_only] * blocks
        + [whole(v) for v in (probs, query_rows, weight_rows)],
        pl.CostEstimate(
            flops=6 * tokens * columns * index_width,
            bytes_accessed=2 * columns * index_width,
            transcendentals=0,
        ),
    )
    odd = swap(odd, "pb", 1)
    term = shape((rows, index_width), f32)
    half = shape((rows, index_width), bf16)
    mine, *others = call(pair_kernel, [term] + [half] * (blocks // 2 - 1), (even, odd))
    others = [swap(value, "pb", 2 * (i + 1)) for i, value in enumerate(others)]
    mine = call(sum_kernel, half, [mine] + others)
    key_grad = call(sum_kernel, half, [mine] + [swap(mine, "ha", r) for r in range(1, parts)])

    answers = [answers[0]] + [swap(answers[r], "ha", r) for r in range(1, parts)]
    query_grad, weight_grad = call(
        functools.partial(finish_kernel, share, heads),
        [shape((rows * heads, index_width), bf16), shape((heads, rows), f32)],
        answers,
    )
    return (query_grad.reshape(index_query.shape), key_grad, weight_grad.T)


def solution(mesh):
    return jax.shard_map(
        on_device,
        mesh=mesh,
        in_specs=(
            P("pb", "ha", None),
            P("pb", None),
            P("pb", "ha"),
            P("pb"),
            P("pb", "ha", None),
            P("pb", None),
            P("pb", "ha"),
        ),
        out_specs=(P("pb", "ha", None), P("pb", None), P("pb", "ha")),
        check_vma=False,
    )
```

```python
import functools

import jax
import jax.numpy as jnp
from jax import lax
from jax.experimental import pallas as pl
from jax.experimental.pallas import tpu as pltpu
from jax.sharding import PartitionSpec as P

main_scale = 192.0 ** (-0.5)
log2e = 1.4426950408889634
very_low = -1e30
LANES = 128
FILL = 10
TAIL = 16
f32, bf16 = jnp.float32, jnp.bfloat16


def params():
    return pltpu.CompilerParams(vmem_limit_bytes=24 * 1024 * 1024)


def whole(value):
    zeros = (0,) * len(value.shape)
    return pl.BlockSpec(value.shape, lambda *_: zeros)


def call(kernel, outs, values, scratch=(), specs=None, cost=None):
    many = isinstance(outs, list)
    found = pl.pallas_call(
        kernel,
        grid=(1,),
        out_shape=outs,
        in_specs=specs or [whole(v) for v in values],
        out_specs=[whole(o) for o in outs] if many else whole(outs),
        scratch_shapes=list(scratch),
        compiler_params=params(),
        cost_estimate=cost,
    )(*values)
    return list(found) if many else found


def tree(values):
    while len(values) > 1:
        values = [values[i] + values[i + 1] for i in range(0, len(values), 2)]
    return values[0]


def terms_of(value, count):
    found = []
    for _ in range(count):
        term = value.astype(bf16)
        found.append(term)
        value = value - term.astype(f32)
    return found


def pack_kernel(latent_ref, key_ref, packed_ref):
    width = key_ref.shape[1]
    packed_ref[:, :width] = key_ref[...]
    packed_ref[:, width:] = latent_ref[...].T


def ask_kernel(query_ref, weight_ref, *outs):
    me = lax.axis_index("ha")
    heads = weight_ref.shape[0]
    rows = outs[0].shape[0] - 3 * TAIL
    split = terms_of(weight_ref[...], 3)
    for r, out in enumerate(outs):
        first = pl.multiple_of((me ^ r) * rows, rows)
        out[:rows, :] = query_ref[pl.ds(first, rows), :]
        for i in range(3):
            at = rows + i * TAIL
            if heads < TAIL:
                out[at : at + TAIL, :] = jnp.zeros((TAIL, LANES), bf16)
            out[at : at + heads, :] = split[i]


def own_lanes(value, share):
    me = lax.axis_index("ha")
    value = pltpu.roll(value, lax.rem(LANES - me * share, LANES), 1)
    lanes = lax.broadcasted_iota(jnp.int32, value.shape, 1)
    value = jnp.where(lanes < share, value, jnp.zeros_like(value))
    shift = share
    while shift < LANES:
        value = value + pltpu.roll(value, shift, 1)
        shift *= 2
    return value


def main_kernel(rels, earlier, *refs):
    count = len(rels)
    blocks = refs[:count]
    query, sums_ref = refs[count : count + 2]
    before = refs[count + 2 : count + 2 + earlier]
    outs = refs[count + 2 + earlier : -3]
    keys, total, turned = refs[-3:]
    heads, width, rows = query.shape
    for k in range(count):
        block = blocks[k][...]
        keys[k * rows : (k + 1) * rows, :] = block[:, block.shape[1] - width :]
    total[...] = jnp.zeros_like(total)

    for head in range(0, heads, 2):
        two = jnp.concatenate([query[head], query[head + 1]], axis=1)
        scores = jnp.dot(keys[...], two, preferred_element_type=f32)
        parts = [
            jnp.exp2(
                scores[:, half * rows : (half + 1) * rows] * (main_scale * log2e)
                - sums_ref[head + half : head + half + 1, :] * log2e
            )
            for half in range(2)
        ]
        total[...] += parts[0] + parts[1]

    me = lax.axis_index("pb")
    kept = turned.shape[1] - count * rows
    at = 0
    for ref in before:
        turned[:, at : at + ref.shape[1]] = ref[...].astype(f32)
        at += ref.shape[1]
    for k in range(count):
        key = (me ^ rels[k]) * rows + lax.broadcasted_iota(jnp.int32, (rows, rows), 0)
        mine = me * rows + lax.broadcasted_iota(jnp.int32, (rows, rows), 1)
        start = sums_ref[heads : heads + 1, :].astype(jnp.int32)
        seen = (key >= start) & (key <= mine)
        piece = jnp.where(seen, total[k * rows : (k + 1) * rows, :], 0.0)
        turned[:, kept + k * rows : kept + (k + 1) * rows] = piece.T
    if len(outs) == 1:
        outs[0][...] = turned[...].astype(bf16)
    else:
        me = lax.axis_index("ha")
        share = outs[0].shape[0]
        for r, out in enumerate(outs):
            first = pl.multiple_of((me ^ r) * share, share)
            out[...] = turned[pl.ds(first, share), :].astype(bf16)


def index_kernel(share, count, parts, heads, *refs):
    blocks = refs[:count]
    messages = refs[count : count + parts]
    start_ref, prob_ref, queries_ref, weights_ref, keys, wide, total = refs[count + parts :]
    rows, width = blocks[0].shape
    for k in range(count):
        keys[k * rows : (k + 1) * rows, :] = blocks[k][...]
    own = share * heads
    repeats = LANES // share
    group = lax.broadcasted_iota(jnp.int32, (1, LANES), 1) // share
    row_of = []
    for r in range(parts):
        wide[...] = messages[r][:own, :].astype(f32)
        for j in range(heads):
            first = (r * heads + j) * share
            queries_ref[first : first + share, :] = wide[
                pl.ds(j, share, stride=heads), :
            ].astype(bf16)
        weight = tree_of_three(messages[r], own)
        weight = own_lanes(weight, share)
        row_of += [weight[j : j + 1, :] for j in range(heads)]
    weights_ref[...] = jnp.zeros_like(weights_ref)
    for g in range(len(row_of) // repeats):
        row = row_of[g * repeats]
        for i in range(1, repeats):
            row = jnp.where(group == i, row_of[g * repeats + i], row)
        weights_ref[g : g + 1, :] = row
    total[...] = jnp.zeros_like(total)
    for g in range(0, len(row_of) // repeats, 2):
        two = queries_ref[g * LANES : (g + 2) * LANES, :]
        act = lax.dot_general(
            keys[...], two, (((1,), (1,)), ((), ())), preferred_element_type=f32
        )
        act = jnp.maximum(act, 0.0)
        total[...] += (
            act[:, :LANES] * weights_ref[g : g + 1, :]
            + act[:, LANES:] * weights_ref[g + 1 : g + 2, :]
        )

    me = lax.axis_index("pb")
    lane = lax.broadcasted_iota(jnp.int32, (rows, LANES), 1) % share
    mine = me * rows + lax.axis_index("ha") * share + lane
    start = own_lanes(jnp.broadcast_to(start_ref[...], (8, LANES)), share)[:1, :]
    top = jnp.full((1, LANES), very_low, f32)
    masks = []
    for k in range(count):
        at = slice(k * rows, (k + 1) * rows)
        key = (me ^ k) * rows + lax.broadcasted_iota(jnp.int32, (rows, LANES), 0)
        seen = (key >= start) & (key <= mine)
        value = total[at, :]
        shift = share
        while shift < LANES:
            value = value + pltpu.roll(value, shift, 1)
            shift *= 2
        value = jnp.where(seen, value, very_low)
        total[at, :] = value
        top = jnp.maximum(top, jnp.max(value, axis=0, keepdims=True))
        masks.append(seen)
    mass = jnp.zeros((1, LANES), f32)
    for k in range(count):
        at = slice(k * rows, (k + 1) * rows)
        value = jnp.where(masks[k], jnp.exp(total[at, :] - top), 0.0)
        prob_ref[at, :] = value
        mass = mass + jnp.sum(value, axis=0, keepdims=True)
    prob_ref[...] = prob_ref[...] * (1.0 / mass)


def tree_of_three(ref, at):
    parts = [ref[at + i * TAIL : at + (i + 1) * TAIL, :].astype(f32) for i in range(3)]
    return parts[0] + (parts[1] + parts[2])


def back_kernel(share, count, parts, heads, *refs):
    mass_refs = refs[:parts]
    blocks = refs[parts : parts + count]
    prob_ref, queries_ref, weights_ref = refs[parts + count : parts + count + 3]
    outs = refs[parts + count + 3 : -6]
    even_ref, odd_ref = outs[:2]
    messages = outs[2:]
    keys, turned_keys, grad, key_total, query_total, weight_total = refs[-6:]
    rows, width = blocks[0].shape
    repeats = LANES // share
    mass = tree([ref[...].astype(f32) for ref in mass_refs])
    for k in range(count):
        at = slice(k * rows, (k + 1) * rows)
        keys[at, :] = blocks[k][...]
        turned_keys[:, at] = blocks[k][...].T
        grad[at, :] = jnp.concatenate([mass[:, at]] * repeats, axis=0).T
    total = jnp.sum(grad[...], axis=0, keepdims=True)
    grad[...] = prob_ref[...] - grad[...] / total
    key_total[...] = jnp.zeros_like(key_total)
    weight_total[...] = jnp.zeros_like(weight_total)
    all_heads = parts * heads
    for g in range(0, all_heads // repeats, 2):
        two = queries_ref[g * LANES : (g + 2) * LANES, :]
        act = lax.dot_general(
            keys[...], two, (((1,), (1,)), ((), ())), preferred_element_type=f32
        )
        coeffs = []
        for half in range(2):
            mine = act[:, half * LANES : (half + 1) * LANES]
            lean = grad[...]
            weight_total[g + half : g + half + 1, :] = jnp.sum(
                lean * jnp.maximum(mine, 0.0), axis=0, keepdims=True
            )
            coeffs.append(
                jnp.where(
                    mine > 0.0, lean * weights_ref[g + half : g + half + 1, :], 0.0
                ).astype(bf16)
            )
        coeffs = jnp.concatenate(coeffs, axis=1)
        key_total[...] += jnp.dot(coeffs, two, preferred_element_type=f32)
        found = jnp.dot(turned_keys[...], coeffs, preferred_element_type=f32)
        found = jnp.concatenate([found[:, :LANES].T, found[:, LANES:].T], axis=0)
        for i in range(2 * repeats):
            head = g * repeats + i
            first = (head // heads) * heads * share + head % heads
            query_total[pl.ds(first, share, stride=heads), :] = found[
                i * share : (i + 1) * share, :
            ]
    own = share * heads
    split = terms_of(weight_total[...], 2)
    for r in range(parts):
        messages[r][:own, :] = query_total[r * own : (r + 1) * own, :].astype(bf16)
        for i in range(2):
            messages[r][own + i * TAIL : own + (i + 1) * TAIL, :] = split[i]
    for i in range(count // 2):
        at = slice(i * rows, (i + 1) * rows)
        even_ref[at, :] = key_total[2 * i * rows : (2 * i + 1) * rows, :]
        odd_ref[at, :] = key_total[(2 * i + 1) * rows : (2 * i + 2) * rows, :]


def pair_kernel(mine_ref, other_ref, own_ref, *outs):
    rows = own_ref.shape[0]
    own_ref[...] = mine_ref[:rows, :] + other_ref[:rows, :]
    for i, out in enumerate(outs):
        at = slice((i + 1) * rows, (i + 2) * rows)
        out[...] = (mine_ref[at, :] + other_ref[at, :]).astype(out.dtype)


def sum_kernel(*refs):
    out_ref = refs[-1]
    out_ref[...] = tree([ref[...].astype(f32) for ref in refs[:-1]]).astype(out_ref.dtype)


def finish_kernel(share, heads, *refs):
    messages = refs[:-2]
    query_out, weight_out = refs[-2:]
    me = lax.axis_index("ha")
    own = share * heads
    total = jnp.zeros((heads, LANES), f32)
    lanes = lax.broadcasted_iota(jnp.int32, (heads, LANES), 1)
    for r, message in enumerate(messages):
        first = pl.multiple_of((me ^ r) * own, own)
        query_out[pl.ds(first, own), :] = message[:own, :]
        value = message[own : own + TAIL, :].astype(f32) + message[
            own + TAIL : own + 2 * TAIL, :
        ].astype(f32)
        rolled = {}
        found = []
        for j in range(heads):
            column = (r * heads + j) * share
            row, lane = column // LANES, column % LANES
            if lane not in rolled:
                rolled[lane] = pltpu.roll(value, LANES - lane, 1) if lane else value
            found.append(rolled[lane][row : row + 1, :])
        piece = jnp.where(lanes < share, jnp.concatenate(found, axis=0), 0.0)
        total = total + pltpu.roll(piece, (me ^ r) * share, 1)
    weight_out[...] = total


def on_device(main_query, latent, log_sums, window_start, index_query, index_key, index_weight):
    rows, head_count, width = main_query.shape
    heads, index_width = index_query.shape[1:]
    blocks = lax.axis_size("pb")
    parts = lax.axis_size("ha")
    share = rows // parts
    tokens = blocks * rows
    own = share * heads
    columns = share * heads * parts
    shape = jax.ShapeDtypeStruct

    def swap(value, axis, rel):
        size = lax.axis_size(axis)
        return lax.ppermute(value, axis, [(i, i ^ rel) for i in range(size)])

    start_row = window_start.reshape(1, rows)
    key_only = pl.BlockSpec((rows, index_width), lambda *_: (0, 0))

    packed = call(
        pack_kernel,
        shape((rows, index_width + width), bf16),
        (latent.T, index_key),
        cost=pl.CostEstimate(flops=0, bytes_accessed=1 << 24, transcendentals=0),
    )
    asked = call(
        ask_kernel,
        [shape((own + 3 * TAIL, index_width), bf16)] * parts,
        (index_query.reshape(rows * heads, index_width), index_weight.T),
    )
    queries = jnp.transpose(main_query, (1, 2, 0))
    sums = jnp.concatenate([log_sums.T, window_start.astype(f32)[None, :]], axis=0)
    held = [None] * blocks
    held[0] = packed
    held[1] = swap(packed, "pb", 1)
    for k in range(2, blocks, 2):
        held[k] = swap(packed, "pb", k)
    ready = lax.optimization_barrier((asked[0], held[1]))
    asked = [ready[0]] + [swap(asked[r], "ha", r) for r in range(1, parts)]
    held[1] = ready[1]

    chunks = [[0, 1]] + [list(range(k, min(k + 4, blocks))) for k in range(2, blocks, 4)]
    mass = []
    for rels in chunks:
        last = rels is chunks[-1]
        span = len(rels) * rows
        outs = [shape((share, tokens), bf16)] * parts if last else [shape((rows, span), bf16)]
        before = mass if last else []
        values = [held[k] for k in rels] + [queries, sums] + before
        specs = [whole(v) for v in values]
        specs[len(rels)] = pl.BlockSpec(memory_space=pltpu.VMEM)
        found = call(
            functools.partial(main_kernel, rels, len(before)),
            outs,
            values,
            [
                pltpu.VMEM((span, width), bf16),
                pltpu.VMEM((span, rows), f32),
                pltpu.VMEM((rows, tokens if last else span), f32),
            ],
            specs,
            pl.CostEstimate(
                flops=2 * span * rows * head_count * width * (FILL if rels is chunks[0] else 1),
                bytes_accessed=2 * rows * head_count * width,
                transcendentals=span * rows * head_count,
            ),
        )
        mass = found if last else mass + found
        if rels is chunks[0]:
            even = list(range(2, blocks, 2))
            ready = lax.optimization_barrier((found[0], [held[k] for k in even], asked[1:3]))
            mass = [ready[0]]
            asked[1:3] = ready[2]
            for k, block in zip(even, ready[1]):
                held[k] = block
                held[k + 1] = swap(block, "pb", 1)
    first, key_block = lax.optimization_barrier((mass[0], held[0]))
    mass = [first] + [swap(mass[r], "ha", r) for r in range(1, parts)]
    key_blocks = [key_block] + held[1:]

    probs, query_rows, weight_rows = call(
        functools.partial(index_kernel, share, blocks, parts, heads),
        [
            shape((tokens, LANES), f32),
            shape((columns, index_width), bf16),
            shape((TAIL, LANES), f32),
        ],
        key_blocks + asked + [start_row],
        [
            pltpu.VMEM((tokens, index_width), bf16),
            pltpu.VMEM((own, index_width), f32),
            pltpu.VMEM((tokens, LANES), f32),
        ],
        [key_only] * blocks + [whole(v) for v in asked + [start_row]],
        pl.CostEstimate(
            flops=2 * tokens * columns * index_width,
            bytes_accessed=2 * columns * index_width,
            transcendentals=tokens * LANES,
        ),
    )

    even, odd, *answers = call(
        functools.partial(back_kernel, share, blocks, parts, heads),
        [shape((tokens // 2, index_width), f32)] * 2
        + [shape((own + 2 * TAIL, index_width), bf16)] * parts,
        mass + key_blocks + [probs, query_rows, weight_rows],
        [
            pltpu.VMEM((tokens, index_width), bf16),
            pltpu.VMEM((index_width, tokens), bf16),
            pltpu.VMEM((tokens, LANES), f32),
            pltpu.VMEM((tokens, index_width), f32),
            pltpu.VMEM((columns, index_width), f32),
            pltpu.VMEM((TAIL, LANES), f32),
        ],
        [whole(v) for v in mass]
        + [key_only] * blocks
        + [whole(v) for v in (probs, query_rows, weight_rows)],
        pl.CostEstimate(
            flops=6 * tokens * columns * index_width,
            bytes_accessed=2 * columns * index_width,
            transcendentals=0,
        ),
    )
    odd = swap(odd, "pb", 1)
    term = shape((rows, index_width), f32)
    half = shape((rows, index_width), bf16)
    mine, *others = call(pair_kernel, [term] + [half] * (blocks // 2 - 1), (even, odd))
    others = [swap(value, "pb", 2 * (i + 1)) for i, value in enumerate(others)]
    mine = call(sum_kernel, half, [mine] + others)
    key_grad = call(sum_kernel, half, [mine] + [swap(mine, "ha", r) for r in range(1, parts)])

    answers = [answers[0]] + [swap(answers[r], "ha", r) for r in range(1, parts)]
    query_grad, weight_grad = call(
        functools.partial(finish_kernel, share, heads),
        [shape((rows * heads, index_width), bf16), shape((heads, rows), f32)],
        answers,
    )
    return (query_grad.reshape(index_query.shape), key_grad, weight_grad.T)


def solution(mesh):
    return jax.shard_map(
        on_device,
        mesh=mesh,
        in_specs=(
            P("pb", "ha", None),
            P("pb", None),
            P("pb", "ha"),
            P("pb"),
            P("pb", "ha", None),
            P("pb", None),
            P("pb", "ha"),
        ),
        out_specs=(P("pb", "ha", None), P("pb", None), P("pb", "ha")),
        check_vma=False,
    )
```
